128 devices in a mesh: section: 4 (over z), dp: 32 (over x, y, core).
Axes of the slice: x: 4, y: 4, z: 4, core: 2. Of those that a mesh axis runs over, the one named last changes fastest.
Arguments:
- block_input: bfloat16 [128, 128, 1024], P('dp'), may hold values from -6 to 6
- cotangent: bfloat16 [128, 128, 1024], P('dp'), may hold values from -6 to 6
- group_ids: int32 [128], P('dp'), may hold values from 0 to 7
- live_count: int32 [32], P('dp'), may hold values from 1 to 4, as said below
- group_scale: float32 [8], replicated, may hold values from 0.25 to 4
- norm_gain: float32 [4, 2, 1024], P('section'), may hold values from 0.1 to 1.9
- norm_bias: float32 [4, 2, 1024], P('section'), may hold values from -2 to 2
- first_weight: bfloat16 [4, 1024, 4096], P('section'), may hold values from -0.1875 to 0.1875
- qv_bias: float32 [2, 2, 1024], replicated, may hold values from -2 to 2
- up_bias: float32 [2, 4096], replicated, may hold values from -2 to 2
- down_weight: bfloat16 [8192, 1024], P('section'), may hold values from -0.09375 to 0.09375
- out_bias: float32 [4, 1024], P('section'), may hold values from -2 to 2
Outputs:
- input_grad: bfloat16 [128, 128, 1024], P('dp', None, 'section')
- first_grad: float32 [4, 1024, 4096], P('section')
- down_grad: float32 [8192, 1024], P('section')
- qv_bias_grad: float32 [2, 2, 1024], replicated
- up_bias_grad: float32 [2, 4096], replicated
- out_bias_grad: float32 [4, 1024], P('section')
- norm_gain_grad: float32 [4, 2, 1024], P('section')
- norm_bias_grad: float32 [4, 2, 1024], P('section')
The draws below stay inside these ranges and needn't reach their ends.
Inputs may be any that keep to these rules, and one draw needn't show every extreme that they name: `live_count`: live slots of each index of dp, counted from its first slot; the slots after them hold sequences of weight zero; some index of dp has all 4 live and some has one.
All inputs are finite; a program needn't handle non-finite values.
Results may differ from the reference program's by a relative error of at most 0.023.
Values may be sent and summed in bfloat16 or wider, within the bound.
A program may use at most 256 MiB of HBM per device.

```python
import math
import jax
import jax.numpy as jnp
from jax import lax

D = 1024
HEADS = 16
FF = 4096
LAYERS = 2
LEN = 128
GROUPS = 8
SLOTS = 4
SEQS = 128
N_DP = 32


def draw_live_count(key, part):
    key = jax.random.fold_in(key, 11)
    first_key, second_key, third_key = jax.random.split(key, 3)
    counts = jax.random.randint(first_key, (N_DP,), 1, SLOTS + 1)
    full_at = jax.random.randint(second_key, (), 0, N_DP)
    single_at = (full_at + 1 + jax.random.randint(third_key, (), 0, N_DP - 1)) % N_DP
    positions = jnp.arange(N_DP)
    counts = jnp.where(positions == full_at, SLOTS, counts)
    counts = jnp.where(positions == single_at, 1, counts)
    return counts.astype(jnp.int32)


def plant(drawn, rng, least, high):
    shape = drawn.shape
    index_at = [jax.random.randint(jax.random.fold_in(rng, axis), (), 0, shape[axis]) for axis in range(len(shape))]
    drawn = drawn.at[tuple(index_at)].set(least)
    longest = shape.index(max(shape))
    index_at[longest] = (index_at[longest] + 1) % shape[longest]
    return drawn.at[tuple(index_at)].set(high)


def block_levels(stream_key, dims, cuts, low, high):
    def one(dim, parts):
        heights = jax.random.uniform(jax.random.fold_in(jax.random.fold_in(stream_key, 6), dim), (parts,), jnp.float32, low / len(cuts), high / len(cuts))
        return jnp.repeat(jnp.exp(heights), dims[dim] // parts).reshape((-1,) + (1,) * (len(dims) - dim - 1))

    loudness = one(*cuts[0])
    for cut in cuts[1:]:
        loudness = loudness * one(*cut)
    return loudness


def scatter_about(own_key, extent, width, reach, cuts=(), kind=jnp.bfloat16):
    level = block_levels(own_key, extent, cuts, -0.22, 0.18) if cuts else 1.0
    drawn = jax.random.normal(own_key, extent, jnp.float32) * width * level
    return jnp.minimum(jnp.maximum(drawn, -reach), reach).astype(kind)


def setup_inputs(seed: int = 0) -> dict:
    arg_keys = jax.random.split(jax.random.key(seed), 13)
    block_input = scatter_about(arg_keys[0], (SEQS, LEN, D), 1.0, 6.0, ((0, 32),))
    cotangent = scatter_about(arg_keys[1], (SEQS, LEN, D), 1.0, 6.0, ((0, 32),))
    group_ids = plant(jax.random.randint(arg_keys[2], (SEQS,), 0, GROUPS), jax.random.fold_in(arg_keys[2], 1), 0, GROUPS - 1).astype(jnp.int32)
    live_count = draw_live_count(jax.random.fold_in(arg_keys[12], 71), 0)
    group_scale = jnp.clip(jnp.exp(jax.random.uniform(arg_keys[4], (GROUPS,), jnp.float32, math.log(0.25), math.log(4.0))), 0.25, 4.0)
    norm_gain = jnp.clip(1.0 + 0.18 * jax.random.normal(arg_keys[5], (2 * LAYERS, 2, D), jnp.float32), 0.1, 1.9)
    norm_bias = scatter_about(arg_keys[6], (2 * LAYERS, 2, D), 0.3, 2.0, ((0, 4),), jnp.float32)
    first_weight = scatter_about(arg_keys[7], (2 * LAYERS, D, FF), D ** -0.5, 0.1875, ((0, 4),))
    qv_bias = scatter_about(arg_keys[8], (LAYERS, 2, D), 0.3, 2.0, (), jnp.float32)
    up_bias = scatter_about(arg_keys[9], (LAYERS, FF), 0.3, 2.0, (), jnp.float32)
    down_weight = scatter_about(arg_keys[10], (LAYERS * FF, D), FF ** -0.5, 0.09375, ((0, 4),))
    out_bias = scatter_about(arg_keys[11], (2 * LAYERS, D), 0.3, 2.0, ((0, 4),), jnp.float32)
    return {"block_input": block_input, "cotangent": cotangent, "group_ids": group_ids, "live_count": live_count, "group_scale": group_scale, "norm_gain": norm_gain, "norm_bias": norm_bias, "first_weight": first_weight, "qv_bias": qv_bias, "up_bias": up_bias, "down_weight": down_weight, "out_bias": out_bias}


relax_alpha = 32.0
norm_eps = 1e-05
far_below = -1000000000.0

@jax.custom_vjp
def low(v):
    return lax.optimization_barrier(v.astype(jnp.bfloat16)).astype(jnp.float32)

@jax.custom_vjp
def low_back(v):
    return v

def low_keep(v):
    return (low(v), None)

def low_pass(kept, grad):
    return (grad,)

def back_keep(v):
    return (v, None)

def back_low(kept, grad):
    return (low(grad),)
low.defvjp(low_keep, low_pass)
low_back.defvjp(back_keep, back_low)

def layer_norm(entries, gain_row, shift_row):
    average = lax.optimization_barrier(jnp.mean(entries, axis=-1, keepdims=True))
    centered = entries - average
    spread = lax.optimization_barrier(jnp.mean(centered * centered, axis=-1, keepdims=True))
    return centered * lax.rsqrt(spread + norm_eps) * gain_row + shift_row

def product(left_side, right_side):
    return jnp.dot(left_side, right_side, precision=lax.Precision.HIGHEST, preferred_element_type=jnp.float32)

def attend_sequence(operands):
    query_heads, key_heads, value_heads = operands
    length = query_heads.shape[0]
    scores = jnp.einsum('qhd,khd->hqk', query_heads, key_heads, precision=lax.Precision.HIGHEST)
    scores = low_back(scores * (1.0 / (relax_alpha * math.sqrt(query_heads.shape[-1]))))
    row_index = lax.broadcasted_iota(jnp.int32, (length, length), 0)
    column_index = lax.broadcasted_iota(jnp.int32, (length, length), 1)
    masked = jnp.where(row_index >= column_index, scores, far_below)
    logits = relax_alpha * (masked - lax.optimization_barrier(jnp.max(masked, axis=-1, keepdims=True)))
    attention_weights = low(jax.nn.softmax(logits, axis=-1))
    return jnp.einsum('hqk,khd->qhd', attention_weights, value_heads, precision=lax.Precision.HIGHEST)

def attention_half(residual, gain_pair, shift_pair, matrix, bias_pair, branch_bias):
    model_width = residual.shape[1]
    normed = low(layer_norm(residual, gain_pair[0], shift_pair[0]))
    bias_row = jnp.concatenate([bias_pair[0], jnp.zeros((model_width,), jnp.float32), bias_pair[1]])
    projected = low_back(low(product(normed, matrix[:, :3 * model_width]) + bias_row))
    shaped = projected.reshape(-1, LEN, 3, HEADS, model_width // HEADS)
    context = lax.map(jax.checkpoint(attend_sequence), (shaped[:, :, 0], shaped[:, :, 1], shaped[:, :, 2]))
    context = low_back(low(context.reshape(-1, model_width)))
    branch = low_back(product(context, matrix[:, 3 * model_width:].T) + branch_bias)
    return residual + layer_norm(branch, gain_pair[1], shift_pair[1])

def feed_forward_half(residual, gain_pair, shift_pair, matrix, hidden_bias, down_matrix, branch_bias):
    normed = low(layer_norm(residual, gain_pair[0], shift_pair[0]))
    hidden = low_back(product(normed, matrix) + hidden_bias)
    active = low(jax.nn.gelu(hidden, approximate=True))
    branch = low_back(product(active, down_matrix) + branch_bias)
    return residual + layer_norm(branch, gain_pair[1], shift_pair[1])

def forward(residual, norm_gain, norm_bias, first_weight, qv_bias, up_bias, down_weight, out_bias):
    hidden_width = first_weight.shape[2]
    for layer_at in range(LAYERS):
        attend_at = 2 * layer_at
        feed_at = attend_at + 1
        residual = attention_half(residual, norm_gain[attend_at], norm_bias[attend_at], first_weight[attend_at], qv_bias[layer_at], out_bias[attend_at])
        residual = low_back(low(residual))
        down_matrix = down_weight[layer_at * hidden_width:(layer_at + 1) * hidden_width]
        residual = feed_forward_half(residual, norm_gain[feed_at], norm_bias[feed_at], first_weight[feed_at], up_bias[layer_at], down_matrix, out_bias[feed_at])
        if layer_at + 1 < LAYERS:
            residual = low_back(low(residual))
    return residual

def reference(block_input, cotangent, group_ids, live_count, group_scale, norm_gain, norm_bias, first_weight, qv_bias, up_bias, down_weight, out_bias):
    positions = jnp.arange(SEQS, dtype=jnp.int32)
    alive_slots = positions % SLOTS < live_count[positions // SLOTS]
    sequence_weight = jnp.where(alive_slots, group_scale[group_ids], 0.0)
    weighted = cotangent.astype(jnp.float32) * sequence_weight[:, None, None]
    block_sequences = math.gcd(SEQS, max(1, 4096 // LEN))
    sources = block_input.astype(jnp.float32).reshape(SEQS // block_sequences, block_sequences * LEN, D)
    targets = weighted.reshape(SEQS // block_sequences, block_sequences * LEN, D)
    parameters = (norm_gain, norm_bias, first_weight.astype(jnp.float32), qv_bias, up_bias, down_weight.astype(jnp.float32), out_bias)

    def one_block(totals, pieces):
        source, target = pieces
        output, pullback = jax.vjp(forward, source, parameters[0], parameters[1], parameters[2], parameters[3], parameters[4], parameters[5], parameters[6])
        gradients = pullback(target)
        return (jax.tree.map(jnp.add, totals, tuple(gradients[1:])), gradients[0])
    zero_totals = jax.tree.map(jnp.zeros_like, parameters)
    totals, input_grads = lax.scan(one_block, zero_totals, (sources, targets))
    input_grad = input_grads.reshape(SEQS, LEN, D).astype(jnp.bfloat16)
    return (input_grad, totals[2], totals[5], totals[3], totals[4], totals[6], totals[0], totals[1])
```

```python
import math

import jax
import jax.numpy as jnp
from jax import lax
from jax.experimental import pallas as pl
from jax.experimental.pallas import tpu as pltpu
from jax.sharding import PartitionSpec as P

MESH = pl.DeviceIdType.MESH
BF16 = jnp.bfloat16
F32 = jnp.float32

WIDTH = 1024
FF = 4096
LEN = 128
SLOTS = 4
ROWS = SLOTS * LEN
PAIRS = 8
SECTIONS = 4
NORM_EPS = 1e-05
GELU_C = math.sqrt(2.0 / math.pi)
CHUNKS = 8
ORDER = (10, 0, 8, 3, 4, 5, 1, 9, 6, 7, 2)
OFFSET = (0, 1, 2, 4, 5, 6, 7, 8, 11, 13, 20)


def device(section, x, y, core):
    return (section, x * 8 + y * 2 + core)


def place():
    at = lax.axis_index("dp")
    return lax.axis_index("section"), at // 8, (at // 2) % 4, at % 2


def neighbours(section, x, y, core):
    found = [device(section, x, y, 1 - core)]
    for d in (1, 2, 3):
        found.append(device(section, (x + d) % 4, y, core))
        found.append(device(section, x, (y + d) % 4, core))
        found.append(device((section + d) % 4, x, y, core))
    return found


def greet(section, x, y, core):
    barrier = pltpu.get_barrier_semaphore()
    others = neighbours(section, x, y, core)
    for other in others:
        pl.semaphore_signal(barrier, inc=1, device_id=other, device_id_type=MESH)
    pl.semaphore_wait(barrier, len(others))


def remote(source, target, send_sem, recv_sem, to):
    return pltpu.make_async_remote_copy(
        src_ref=source,
        dst_ref=target,
        send_sem=send_sem,
        recv_sem=recv_sem,
        device_id=to,
        device_id_type=MESH,
    )


def dot(a, b):
    return jnp.dot(a, b, preferred_element_type=F32)


def dot_nt(a, b):
    return lax.dot_general(a, b, (((1,), (1,)), ((), ())), preferred_element_type=F32)


def dot_tn(a, b):
    return lax.dot_general(a, b, (((0,), (0,)), ((), ())), preferred_element_type=F32)


def normalize(entries):
    average = jnp.mean(entries, axis=-1, keepdims=True)
    centered = entries - average
    inverse = lax.rsqrt(jnp.mean(centered * centered, axis=-1, keepdims=True) + NORM_EPS)
    return centered * inverse, inverse


def norm_backward(grad_out, unit, inverse, gain):
    scaled = grad_out * gain
    middle = jnp.mean(scaled, axis=-1, keepdims=True)
    along = jnp.mean(scaled * unit, axis=-1, keepdims=True)
    return inverse * (scaled - middle - unit * along)


def column_sum(entries):
    return jnp.sum(entries, axis=0, keepdims=True)


def mega_kernel(
    block_hbm, cot_hbm, group_hbm, live_hbm, scale_hbm, gains_hbm, shifts_hbm, qv_hbm, up_hbm, bias_hbm, w1_hbm, down_hbm,
    out_hbm, small_hbm, grad_hbm,
    group_ids, live_count, group_scale, gains, shifts, qv_bias, up_bias, out_bias,
    w1, buffer, w2t, ops, units, inverses, r_in, r_out, g_in, g_out, wide, small, vectors,
    pair, r1, r2, r3, r4, z, sx, sy, ss, sums,
    load_sem, down_send, down_recv, ag_send, ag_recv,
    fwd_send, fwd_recv, bwd_send, bwd_recv, ig_send, ig_recv,
    pair_send, pair_recv, pair_free, ring_send, ring_recv, z_send, z_recv, own_sem, last_send, last_recv,
    tiny_send, tiny_recv,
):
    section, x, y, core = place()
    parity = section % 2
    layer = section // 2
    last = section == SECTIONS - 1
    first = section == 0
    sibling = device(section, x, y, 1 - core)
    w1t, w2 = buffer.at[pl.ds(0, FF)], buffer.at[pl.ds(FF, FF)]

    load_w1 = pltpu.make_async_copy(w1_hbm.at[0], w1, load_sem.at[0])
    load_own = pltpu.make_async_copy(down_hbm, w2.at[pl.ds(2048, 2048)], load_sem.at[1])
    load_block = pltpu.make_async_copy(block_hbm, r_in, load_sem.at[2])
    load_cot = pltpu.make_async_copy(cot_hbm, g_in, load_sem.at[3])

    pieces = [
        (gains_hbm, gains), (shifts_hbm, shifts), (bias_hbm, out_bias), (qv_hbm, qv_bias), (up_hbm, up_bias),
        (group_hbm, group_ids), (live_hbm, live_count), (scale_hbm, group_scale),
    ]
    load_pieces = [pltpu.make_async_copy(*piece, load_sem.at[4 + j]) for j, piece in enumerate(pieces)]

    @pl.when(first)
    def _():
        load_block.start()

    for copy in load_pieces:
        copy.start()
    load_w1.start()

    @pl.when(parity == 1)
    def _():
        load_own.start()

    @pl.when(last)
    def _():
        load_cot.start()

    greet(section, x, y, core)

    row_a = core * 512 + y * 128 + x * 32
    row_b = 1024 + core * 512 + x * 128 + y * 32

    def down_copy(half):
        row = row_a if half == 0 else row_b
        return remote(
            down_hbm.at[pl.ds(row, 32)], w2.at[pl.ds(row, 32)], down_send.at[half], down_recv.at[half],
            device((section + 1) % 4, x, y, core),
        )

    def ag_copy(index):
        d = index % 3 + 1
        along_x = device(section, (x + d) % 4, y, core)
        along_y = device(section, x, (y + d) % 4, core)
        if index < 3:
            rows, to = pl.ds(row_a, 32), along_x
        elif index < 6:
            rows, to = pl.ds(row_b, 32), along_y
        elif index < 9:
            rows, to = pl.ds(core * 512 + y * 128, 128), along_y
        elif index < 12:
            rows, to = pl.ds(1024 + core * 512 + x * 128, 128), along_x
        elif index < 16:
            rows, to = pl.ds(core * 512 + (y + index - 12) % 4 * 128, 128), sibling
        else:
            rows, to = pl.ds(1024 + core * 512 + (x + index - 16) % 4 * 128, 128), sibling
        return remote(w2.at[rows], w2.at[rows], ag_send.at[index], ag_recv.at[index], to)

    @pl.when(parity == 0)
    def _():
        down_copy(0).start()
        down_copy(1).start()

    for copy in load_pieces:
        copy.wait()

    @pl.when(parity == 0)
    def _():
        vectors[5:6, :] = qv_bias[layer, 0:1, :]
        vectors[6:7, :] = jnp.zeros((1, WIDTH), F32)
        vectors[7:8, :] = qv_bias[layer, 1:2, :]

    @pl.when(parity == 1)
    def _():
        for j in range(4):
            vectors[5 + j : 6 + j, :] = up_bias[pl.ds(layer, 1), j * WIDTH : (j + 1) * WIDTH]

    def sequence_weight(micro):
        group = group_ids[micro]
        chosen = jnp.float32(0.0)
        for label in range(8):
            chosen = jnp.where(group == label, group_scale[label], chosen)
        weight = jnp.where(micro < live_count[0], chosen, 0.0)
        return jnp.where(last, weight, 1.0)

    small[...] = jnp.zeros_like(small)

    def gather_start():
        for half in (0, 1):
            down_copy(half).wait_recv()
            for index in range(3 * half, 3 * half + 3):
                ag_copy(index).start()
        for half in (0, 1):
            for index in range(3 * half, 3 * half + 3):
                ag_copy(index).wait()
            for index in range(6 + 3 * half, 9 + 3 * half):
                ag_copy(index).start()
            ag_copy(12 + 4 * half).start()
        load_own.wait()

    def gather_end():
        for d in (1, 3, 2):
            for half in (0, 1):
                ag_copy(5 + 3 * half + 4 - d).wait()
                ag_copy(12 + 4 * half + d).start()
        for index in range(12, 20):
            ag_copy(index).wait()

    pl.when(parity == 1)(gather_start)
    pl.when(last)(gather_end)

    @pl.when(parity == 0)
    def _():
        down_copy(0).wait_send()
        down_copy(1).wait_send()

    load_w1.wait()

    @pl.when(first)
    def _():
        load_block.wait()

    @pl.when(last)
    def _():
        load_cot.wait()

    def fwd_copy(micro):
        return remote(
            r_out.at[micro], r_in.at[micro], fwd_send.at[micro], fwd_recv.at[micro],
            device((section + 1) % 4, x, y, core),
        )

    def bwd_copy(micro):
        return remote(
            g_out.at[micro], g_in.at[micro], bwd_send.at[micro], bwd_recv.at[micro],
            device((section + 3) % 4, x, y, core),
        )

    def ig_copy(micro, d):
        to = (section + d) % 4
        return remote(
            g_out.at[micro, :, pl.ds(d * 256, 256)], grad_hbm.at[micro], ig_send.at[micro, d], ig_recv.at[micro],
            device(to, x, y, core),
        )

    def ig_own(micro):
        return pltpu.make_async_copy(g_out.at[micro, :, pl.ds(0, 256)], grad_hbm.at[micro], ig_send.at[micro, 0])

    lanes = lax.broadcasted_iota(jnp.int32, (LEN, 128), 1)
    low_lanes = lanes < 64

    def two_heads(entries):
        zero = jnp.zeros_like(entries)
        return jnp.concatenate([jnp.where(low_lanes, entries, zero), jnp.where(low_lanes, zero, entries)], axis=0)

    def transposes():
        def one(j, carry):
            cut = pl.ds(pl.multiple_of(j * 256, 256), 256)
            w1t[cut, :] = w1[:, cut].T
            return carry

        lax.fori_loop(0, 16, one, 0)

        @pl.when(parity == 1)
        def _():
            def two(j, carry):
                cut = pl.ds(pl.multiple_of(j * 256, 256), 256)
                w2t[:, cut] = w2[cut, :].T
                return carry

            lax.fori_loop(0, 16, two, 0)

    def attention_forward(micro):
        normed = ops[0, micro]
        for j in range(3):
            part = dot(normed, w1[:, j * WIDTH : (j + 1) * WIDTH]) + vectors[5 + j : 6 + j, :]
            ops[6 + j, micro] = part.astype(BF16)
        rows = lax.broadcasted_iota(jnp.int32, (LEN, 256), 0)
        columns = lax.broadcasted_iota(jnp.int32, (LEN, 256), 1) % 128
        causal = rows >= columns
        for p in range(PAIRS):
            cut = slice(p * 128, (p + 1) * 128)
            query, key, value = (ops[6 + j, micro, :, cut] for j in range(3))
            scores = dot_nt(query, two_heads(key)) * 0.125
            scores = jnp.where(causal, scores, -1e9)
            halves = []
            for half in (scores[:, :128], scores[:, 128:]):
                powers = jnp.exp(half - jnp.max(half, axis=-1, keepdims=True))
                halves.append((powers / jnp.sum(powers, axis=-1, keepdims=True)).astype(BF16))
            weights = jnp.concatenate(halves, axis=1)
            ops[3 + p // 4, micro, :, (p % 4) * 256 : (p % 4 + 1) * 256] = weights
            ops[2, micro, :, cut] = dot(weights, two_heads(value)).astype(BF16)
        wide[...] = dot_nt(ops[2, micro], w1[:, 3 * WIDTH :]) + out_bias[...]

    def feed_forward(micro):
        normed = ops[0, micro]
        branch = out_bias[...]
        for j in (2, 3, 0, 1):
            hidden = dot(normed, w1[:, j * WIDTH : (j + 1) * WIDTH]) + vectors[5 + j : 6 + j, :]
            square = hidden * hidden
            along = jnp.tanh(hidden * (GELU_C + (GELU_C * 0.044715) * square))
            above = 0.5 * (1.0 + along)
            slope = above + 0.5 * hidden * (1.0 - along * along) * (GELU_C + (3.0 * GELU_C * 0.044715) * square)
            active = (hidden * above).astype(BF16)
            ops[6 + j, micro] = slope.astype(BF16)
            ops[2 + j, micro] = active
        for j in (2, 3, 0, 1):
            if j == 0:
                pl.when((micro == 0) & (section == 1))(gather_end)
            branch = branch + dot(ops[2 + j, micro], w2[j * WIDTH : (j + 1) * WIDTH, :])
        wide[...] = branch

    def attention_backward(micro):
        ops[9, micro] = dot(ops[1, micro], w1[:, 3 * WIDTH :]).astype(BF16)
        for p in range(PAIRS):
            cut = slice(p * 128, (p + 1) * 128)
            query, key, value = (ops[6 + j, micro, :, cut] for j in range(3))
            grad = ops[9, micro, :, cut]
            weights = ops[3 + p // 4, micro, :, (p % 4) * 256 : (p % 4 + 1) * 256]
            grad_weights = dot_nt(grad, two_heads(value))
            weights_wide = weights.astype(F32)
            product = weights_wide * grad_weights
            left = product[:, :128] - weights_wide[:, :128] * jnp.sum(product[:, :128], axis=-1, keepdims=True)
            right = product[:, 128:] - weights_wide[:, 128:] * jnp.sum(product[:, 128:], axis=-1, keepdims=True)
            grad_scores = jnp.concatenate([left, right], axis=1).astype(BF16)
            grad_query = dot(grad_scores, two_heads(key)) * 0.125
            both = dot_tn(grad_scores, query) * 0.125
            grad_key = jnp.where(low_lanes, both[:128], both[128:])
            both = dot_tn(weights, grad)
            grad_value = jnp.where(low_lanes, both[:128], both[128:])
            for j, part in enumerate((grad_query, grad_key, grad_value)):
                ops[6 + j, micro, :, cut] = part.astype(BF16)
        total = jnp.zeros((LEN, WIDTH), F32)
        for j in range(3):
            part = ops[6 + j, micro]
            total = total + dot(part, w1t[j * WIDTH : (j + 1) * WIDTH, :])
            if j != 1:
                small[5 + j : 6 + j, :] += column_sum(part.astype(F32))
        wide[...] = total

    def feed_backward(micro):
        grad_branch = ops[1, micro]
        total = jnp.zeros((LEN, WIDTH), F32)
        for j in range(4):
            grad = dot(grad_branch, w2t[:, j * WIDTH : (j + 1) * WIDTH])
            grad = (grad * ops[6 + j, micro].astype(F32)).astype(BF16)
            ops[6 + j, micro] = grad
            small[5 + j : 6 + j, :] += column_sum(grad.astype(F32))
            total = total + dot(grad, w1t[j * WIDTH : (j + 1) * WIDTH, :])
        wide[...] = total

    def forward(micro):
        @pl.when(jnp.logical_not(first))
        def _():
            fwd_copy(micro).wait_recv()

        residual = r_in[micro].astype(F32)
        unit, _ = normalize(residual)
        ops[0, micro] = (unit * gains[0, 0:1, :] + shifts[0, 0:1, :]).astype(BF16)

        @pl.when(parity == 0)
        def _():
            attention_forward(micro)

        @pl.when(parity == 1)
        def _():
            feed_forward(micro)

        unit, inverse = normalize(wide[...])
        units[micro] = unit.astype(BF16)
        inverses[micro] = inverse

        @pl.when(jnp.logical_not(last))
        def _():
            r_out[micro] = (r_in[micro].astype(F32) + unit * gains[0, 1:2, :] + shifts[0, 1:2, :]).astype(BF16)
            fwd_copy(micro).start()

    def backward(micro):
        @pl.when(jnp.logical_not(last))
        def _():
            bwd_copy(micro).wait_recv()

        incoming = g_in[micro].astype(F32) * sequence_weight(micro)
        unit = units[micro].astype(F32)
        small[1:2, :] += column_sum(incoming * unit)
        small[3:4, :] += column_sum(incoming)
        grad_branch = norm_backward(incoming, unit, inverses[micro], gains[0, 1:2, :]).astype(BF16)
        ops[1, micro] = grad_branch
        small[4:5, :] += column_sum(grad_branch.astype(F32))

        @pl.when(parity == 0)
        def _():
            attention_backward(micro)

        @pl.when(parity == 1)
        def _():
            feed_backward(micro)

        grad_normed = wide[...]
        unit, inverse = normalize(r_in[micro].astype(F32))
        small[0:1, :] += column_sum(grad_normed * unit)
        small[2:3, :] += column_sum(grad_normed)
        incoming = g_in[micro].astype(F32) * sequence_weight(micro)
        grad = incoming + norm_backward(grad_normed, unit, inverse, gains[0, 0:1, :])
        g_out[micro] = grad.astype(BF16)

        @pl.when(jnp.logical_not(first))
        def _():
            bwd_copy(micro).start()

        @pl.when(first)
        def _():
            ig_own(micro).start()
            for d in (1, 2, 3):
                ig_copy(micro, d).start()

    turn_at = jnp.where(section >= 2, 0, SLOTS)

    def step(t, carry):
        is_forward = jnp.where(last, (t + 1) % 2, jnp.where(t < SLOTS, 1, 0))
        micro = jnp.where(last, t // 2, t % SLOTS)

        @pl.when(t == turn_at)
        def _():
            transposes()

        @pl.when(is_forward == 1)
        def _():
            forward(micro)

        @pl.when(is_forward == 0)
        def _():
            backward(micro)

        return carry

    lax.fori_loop(0, 2 * SLOTS, step, 0)

    def spot(h):
        return (x, y) if h == 0 else (y, x)

    def peer(axis, d):
        if axis == 0:
            return device(section, (x + d) % 4, y, core)
        return device(section, x, (y + d) % 4, core)

    def at(k, h, b1, b2, n, c=None):
        c = core if c is None else c
        row = k * 1024 + c * 512 + h * 256 + b1 * 64 + b2 * 16
        return pl.ds(pl.multiple_of(row, 16), n)

    def out_chunk(k):
        return jnp.where(parity == 1, k - 2, jnp.where(k < 2, k, k - 2))

    left, right = pl.ds(0, 512), pl.ds(512, 512)

    def ring(stage, k, h, d, source, target, to):
        return remote(source, target, ring_send.at[stage, k, h, d], ring_recv.at[stage, k, h, d], to)

    def pair_copy(k):
        rows = at(k, 0, 0, 0, 512, 1 - core)
        return remote(buffer.at[rows], pair.at[k % 2], pair_send.at[k], pair_recv.at[k], sibling)

    def rs_one(k, h, d):
        p1, _ = spot(h)
        rows = at(k, h, (p1 + 2) % 4, 0, 64)
        return ring(0, k, h, d, buffer.at[rows, left if d == 0 else right], r1.at[k, h, d], peer(h, 1 - 2 * d))

    def rs_two(k, h, d):
        p1, _ = spot(h)
        step = 1 - 2 * d
        return ring(1, k, h, d, buffer.at[at(k, h, (p1 + step) % 4, 0, 64)], r2.at[k, h, d], peer(h, step))

    def rs_three(k, h, d):
        p1, p2 = spot(h)
        rows = at(k, h, p1, (p2 + 2) % 4, 16)
        return ring(2, k, h, d, buffer.at[rows, left if d == 0 else right], r3.at[k, h, d], peer(1 - h, 1 - 2 * d))

    def rs_four(k, h, d):
        p1, p2 = spot(h)
        step = 1 - 2 * d
        return ring(3, k, h, d, buffer.at[at(k, h, p1, (p2 + step) % 4, 16)], r4.at[k, h, d], peer(1 - h, step))

    def z_copy(k, h):
        p1, p2 = spot(h)
        return remote(
            buffer.at[at(k, h, p1, p2, 16)], z.at[k, h], z_send.at[k, h], z_recv.at[k, h],
            device((section + 3) % 4, x, y, core),
        )

    def own_copy(k, h):
        p1, p2 = spot(h)
        return pltpu.make_async_copy(
            buffer.at[at(k, h, p1, p2, 16)], out_hbm.at[at(out_chunk(k), h, p1, p2, 16)], own_sem.at[k, h]
        )

    def ag_one(k, h, d):
        p1, p2 = spot(h)
        return ring(
            4, k, h, d, buffer.at[at(k, h, p1, p2, 16)], out_hbm.at[at(out_chunk(k), h, p1, p2, 16)], peer(1 - h, 1 - 2 * d)
        )

    def ag_two(k, h, d):
        p1, p2 = spot(h)
        step = 1 - 2 * d
        piece = out_hbm.at[at(out_chunk(k), h, p1, (p2 - step) % 4, 16), left if d == 0 else right]
        return ring(5, k, h, d, piece, piece, peer(1 - h, step))

    def ag_three(k, h, d):
        p1, _ = spot(h)
        piece = out_hbm.at[at(out_chunk(k), h, p1, 0, 64)]
        return ring(6, k, h, d, piece, piece, peer(h, 1 - 2 * d))

    def ag_four(k, h, d):
        p1, _ = spot(h)
        step = 1 - 2 * d
        piece = out_hbm.at[at(out_chunk(k), h, (p1 - step) % 4, 0, 64), left if d == 0 else right]
        return ring(7, k, h, d, piece, piece, peer(h, step))

    def last_copy(k):
        piece = out_hbm.at[at(out_chunk(k), 0, 0, 0, 512)]
        return remote(piece, piece, last_send.at[k], last_recv.at[k], sibling)

    both = [(h, d) for h in (0, 1) for d in (0, 1)]

    def stage_0(k):
        feed_down = (parity == 1) & (k < 4)
        from_context = (parity == 0) & (k == 7)
        a = jnp.where(feed_down, 2 + k, jnp.where(from_context, 1, 0))
        b = jnp.where(feed_down, 1, jnp.where(from_context, 2, 2 + k))
        right_side = ops[b].reshape(ROWS, WIDTH)
        for cut in range(4):
            left_side = ops[a, :, :, cut * 256 : (cut + 1) * 256].reshape(ROWS, 256)
            product = dot_tn(left_side, right_side)
            buffer[pl.ds(pl.multiple_of(k * 1024 + cut * 256, 256), 256), :] = product.astype(BF16)
        pl.when(k >= 6 - 4 * parity)(lambda: pl.semaphore_wait(pair_free, 1))
        pair_copy(k).start()

    def stage_1(k):
        pair_copy(k).wait()
        rows = at(k, 0, 0, 0, 512)
        buffer[rows, :] = buffer[rows, :] + pair[k % 2]

        @pl.when(k < CHUNKS - 2)
        def _():
            pl.semaphore_signal(pair_free, inc=1, device_id=sibling, device_id_type=MESH)

        for h, d in both:
            rs_one(k, h, d).start()

    def stage_2(k):
        for h, d in both:
            rs_one(k, h, d).wait()
            p1, _ = spot(h)
            rows = at(k, h, (p1 + 1 - 2 * d) % 4, 0, 64)
            cut = left if d == 0 else right
            buffer[rows, cut] = buffer[rows, cut] + r1[k, h, d]
            rs_two(k, h, d).start()

    def stage_3(k):
        for h in (0, 1):
            p1, _ = spot(h)
            for d in (0, 1):
                rs_two(k, h, d).wait()
            rows = at(k, h, p1, 0, 64)
            total = buffer[rows, :].astype(F32) + r2[k, h, 0].astype(F32) + r2[k, h, 1].astype(F32)
            buffer[rows, :] = total.astype(BF16)
            for d in (0, 1):
                rs_three(k, h, d).start()

    def stage_4(k):
        for h, d in both:
            rs_three(k, h, d).wait()
            p1, p2 = spot(h)
            rows = at(k, h, p1, (p2 + 1 - 2 * d) % 4, 16)
            cut = left if d == 0 else right
            buffer[rows, cut] = buffer[rows, cut] + r3[k, h, d]
            rs_four(k, h, d).start()

    def spread(k):
        for h in (0, 1):
            own_copy(k, h).start()
            for d in (0, 1):
                ag_one(k, h, d).start()

    def stage_5(k):
        @pl.when((parity == 1) | (k >= 4))
        def _():
            for h in (0, 1):
                p1, p2 = spot(h)
                for d in (0, 1):
                    rs_four(k, h, d).wait()
                rows = at(k, h, p1, p2, 16)
                total = buffer[rows, :].astype(F32) + r4[k, h, 0].astype(F32) + r4[k, h, 1].astype(F32)
                buffer[rows, :] = total.astype(BF16)

        @pl.when((parity == 1) & (k < 2))
        def _():
            for h in (0, 1):
                z_copy(k, h).start()

        @pl.when((parity == 0) & (k < 2))
        def _():
            for h in (0, 1):
                p1, p2 = spot(h)
                z_copy(k, h).wait_recv()
                buffer[at(k, h, p1, p2, 16), :] = z[k, h]

        @pl.when(((parity == 1) & (k >= 2)) | (parity == 0))
        def _():
            spread(k)

    def stage_6(k):
        for h in (0, 1):
            for d in (0, 1):
                ag_one(k, h, d).wait()
            for d in (0, 1):
                ag_two(k, h, d).start()
            own_copy(k, h).wait()

    def stage_7(k):
        for h in (0, 1):
            for d in (0, 1):
                ag_two(k, h, d).wait()
            for d in (0, 1):
                ag_three(k, h, d).start()

    def stage_8(k):
        for h in (0, 1):
            for d in (0, 1):
                ag_three(k, h, d).wait()
            for d in (0, 1):
                ag_four(k, h, d).start()

    def stage_9(k):
        for h, d in both:
            ag_four(k, h, d).wait()
        last_copy(k).start()

    def stage_10(k):
        last_copy(k).wait()

    stages = [stage_0, stage_1, stage_2, stage_3, stage_4, stage_5, stage_6, stage_7, stage_8, stage_9, stage_10]

    def tiny(phase, d):
        if phase == 0:
            return remote(small, sx.at[d - 1], tiny_send.at[d - 1], tiny_recv.at[d - 1], peer(0, d))
        if phase == 1:
            return remote(sums.at[0], sy.at[d - 1], tiny_send.at[d + 2], tiny_recv.at[d + 2], peer(1, d))
        if phase == 2:
            return remote(sums.at[1], ss, tiny_send.at[6], tiny_recv.at[6], sibling)
        return remote(
            sums.at[2], small_hbm.at[section], tiny_send.at[6 + d], tiny_recv.at[6 + d],
            device((section + d) % 4, x, y, core),
        )

    keep_own = [
        pltpu.make_async_copy(sums.at[2], small_hbm.at[section], tiny_send.at[10]),
        pltpu.make_async_copy(sums.at[2], small_hbm.at[SECTIONS], tiny_send.at[11]),
    ]

    def tiny_0():
        for d in (1, 2, 3):
            tiny(0, d).start()

    def tiny_1():
        for d in (1, 2, 3):
            tiny(0, d).wait()
        sums[0] = (small[...] + sx[0]) + (sx[1] + sx[2])
        for d in (1, 2, 3):
            tiny(1, d).start()

    def tiny_2():
        for d in (1, 2, 3):
            tiny(1, d).wait()
        sums[1] = (sums[0] + sy[0]) + (sy[1] + sy[2])
        tiny(2, 1).start()

    def tiny_3():
        tiny(2, 1).wait()
        sums[2] = sums[1] + ss[...]
        for copy in keep_own:
            copy.start()
        for d in (1, 2, 3):
            tiny(3, d).start()

    def slot(t, carry):
        for number, turn in enumerate((tiny_0, tiny_1, tiny_2, tiny_3)):
            pl.when(t == number)(turn)
        for s in ORDER:
            k = t - OFFSET[s]
            live = (k >= 0) & (k < CHUNKS)
            if s < 5:
                live = live & ((parity == 1) | (k >= 4))
            elif s == 5:
                live = live & ((parity == 1) | (k < 2) | (k >= 4))
            else:
                live = live & (((parity == 1) & (k >= 2)) | ((parity == 0) & ((k < 2) | (k >= 4))))
            pl.when(live)(lambda turn=stages[s], k=k: turn(k))
        return carry

    lax.fori_loop(0, CHUNKS + max(OFFSET), slot, 0)

    for d in (1, 2, 3):
        tiny(3, d).wait()
    for copy in keep_own:
        copy.wait()

    @pl.when(parity == 1)
    def _():
        for k in range(2):
            for h in (0, 1):
                z_copy(k, h).wait_send()

    @pl.when(jnp.logical_not(last))
    def _():
        for micro in range(SLOTS):
            fwd_copy(micro).wait_send()

    @pl.when(jnp.logical_not(first))
    def _():
        for micro in range(SLOTS):
            bwd_copy(micro).wait_send()
            ig_copy(micro, 1).wait_recv()

    @pl.when(first)
    def _():
        for micro in range(SLOTS):
            ig_own(micro).wait()
            for d in (1, 2, 3):
                ig_copy(micro, d).wait_send()


def mega(block, cot, group_ids, live_count, group_scale, gains, shifts, qv_bias, up_bias, out_bias, w1, down):
    any_space = pl.BlockSpec(memory_space=pl.ANY)
    dma = pltpu.SemaphoreType.DMA
    return pl.pallas_call(
        mega_kernel,
        name="mega",
        out_shape=[
            jax.ShapeDtypeStruct((6 * 1024, WIDTH), BF16),
            jax.ShapeDtypeStruct((SECTIONS + 1, 16, WIDTH), F32),
            jax.ShapeDtypeStruct((SLOTS, LEN, 256), BF16),
        ],
        in_specs=[any_space] * 12,
        out_specs=[any_space, any_space, any_space],
        scratch_shapes=[
            pltpu.SMEM((SLOTS,), jnp.int32),
            pltpu.SMEM((1,), jnp.int32),
            pltpu.SMEM((8,), F32),
            pltpu.VMEM((1, 2, WIDTH), F32),
            pltpu.VMEM((1, 2, WIDTH), F32),
            pltpu.VMEM((2, 2, WIDTH), F32),
            pltpu.VMEM((2, FF), F32),
            pltpu.VMEM((1, WIDTH), F32),
            pltpu.VMEM((WIDTH, FF), BF16),
            pltpu.VMEM((2 * FF, WIDTH), BF16),
            pltpu.VMEM((WIDTH, FF), BF16),
            pltpu.VMEM((10, SLOTS, LEN, WIDTH), BF16),
            pltpu.VMEM((SLOTS, LEN, WIDTH), BF16),
            pltpu.VMEM((SLOTS, LEN, 1), F32),
            pltpu.VMEM((SLOTS, LEN, WIDTH), BF16),
            pltpu.VMEM((SLOTS, LEN, WIDTH), BF16),
            pltpu.VMEM((SLOTS, LEN, WIDTH), BF16),
            pltpu.VMEM((SLOTS, LEN, WIDTH), BF16),
            pltpu.VMEM((LEN, WIDTH), F32),
            pltpu.VMEM((16, WIDTH), F32),
            pltpu.VMEM((16, WIDTH), F32),
            pltpu.VMEM((2, 512, WIDTH), BF16),
            pltpu.VMEM((CHUNKS, 2, 2, 64, 512), BF16),
            pltpu.VMEM((CHUNKS, 2, 2, 64, WIDTH), BF16),
            pltpu.VMEM((CHUNKS, 2, 2, 16, 512), BF16),
            pltpu.VMEM((CHUNKS, 2, 2, 16, WIDTH), BF16),
            pltpu.VMEM((2, 2, 16, WIDTH), BF16),
            pltpu.VMEM((3, 16, WIDTH), F32),
            pltpu.VMEM((3, 16, WIDTH), F32),
            pltpu.VMEM((16, WIDTH), F32),
            pltpu.VMEM((3, 16, WIDTH), F32),
            dma((12,)), dma((2,)), dma((2,)), dma((20,)), dma((20,)),
            dma((SLOTS,)), dma((SLOTS,)), dma((SLOTS,)), dma((SLOTS,)),
            dma((SLOTS, 4)), dma((SLOTS,)),
            dma((CHUNKS,)), dma((CHUNKS,)), pltpu.SemaphoreType.REGULAR,
            dma((8, CHUNKS, 2, 2)), dma((8, CHUNKS, 2, 2)),
            dma((2, 2)), dma((2, 2)), dma((CHUNKS, 2)), dma((CHUNKS,)), dma((CHUNKS,)),
            dma((12,)), dma((12,)),
        ],
        compiler_params=pltpu.CompilerParams(
            collective_id=0, has_side_effects=True, vmem_limit_bytes=63 * 2**20
        ),
    )(block, cot, group_ids, live_count, group_scale, gains, shifts, qv_bias, up_bias, out_bias, w1, down)


def widen_kernel(
    reduced, sums_hbm, grad_in,
    first_out, down_out, qv_out, up_out, bias_out, gain_out, shift_out, grad_out,
    narrow, wide, sums, qv, up, bias, gain, shift, in_sem, out_sem, small_sem,
):
    rows, depth = wide.shape[1], wide.shape[0]
    count = 6 * 1024 // rows

    def load(i):
        return pltpu.make_async_copy(reduced.at[pl.ds(i * rows, rows)], narrow.at[i % depth], in_sem.at[i % depth])

    def store(i):
        chunk, cut = i * rows // 1024, pl.ds(i * rows % 1024, rows)
        if chunk < 2:
            target = down_out.at[pl.ds(i * rows, rows)]
        else:
            target = first_out.at[0, cut, pl.ds((chunk - 2) * 1024, 1024)]
        return pltpu.make_async_copy(wide.at[i % depth], target, out_sem.at[i % depth])

    for i in range(depth):
        load(i).start()
    load_sums = pltpu.make_async_copy(sums_hbm, sums, small_sem.at[0])
    load_sums.start()
    move_grad = pltpu.make_async_copy(grad_in, grad_out, small_sem.at[1])
    move_grad.start()
    small = [(qv, qv_out), (up, up_out), (bias, bias_out), (gain, gain_out), (shift, shift_out)]
    small = [pltpu.make_async_copy(*piece, small_sem.at[2 + j]) for j, piece in enumerate(small)]
    for i in range(count):
        load(i).wait()
        if i >= depth:
            store(i - depth).wait()
        wide[i % depth] = narrow[i % depth].astype(F32)
        store(i).start()
        if i + depth < count:
            load(i + depth).start()
        if i == 2:
            load_sums.wait()
            for layer in (0, 1):
                qv[layer, 0:1, :] = sums[2 * layer, 5:6, :]
                qv[layer, 1:2, :] = sums[2 * layer, 7:8, :]
                for j in range(4):
                    up[layer : layer + 1, j * WIDTH : (j + 1) * WIDTH] = sums[2 * layer + 1, 5 + j : 6 + j, :]
            bias[...] = sums[SECTIONS, 4:5, :]
            gain[0] = sums[SECTIONS, 0:2, :]
            shift[0] = sums[SECTIONS, 2:4, :]
            for copy in small:
                copy.start()
    for i in range(count - depth, count):
        store(i).wait()
    for copy in small:
        copy.wait()
    move_grad.wait()


def widen(reduced, sums, grad):
    any_space = pl.BlockSpec(memory_space=pl.ANY)
    rows, depth = 512, 4
    dma = pltpu.SemaphoreType.DMA
    shapes = [(2, 2, WIDTH), (2, FF), (1, WIDTH), (1, 2, WIDTH), (1, 2, WIDTH)]
    return pl.pallas_call(
        widen_kernel,
        name="widen",
        out_shape=[
            jax.ShapeDtypeStruct((1, WIDTH, FF), F32),
            jax.ShapeDtypeStruct((2 * WIDTH, WIDTH), F32),
            *[jax.ShapeDtypeStruct(shape, F32) for shape in shapes],
            jax.ShapeDtypeStruct((SLOTS, LEN, 256), BF16),
        ],
        in_specs=[any_space] * 3,
        out_specs=[any_space] * 8,
        scratch_shapes=[
            pltpu.VMEM((depth, rows, WIDTH), BF16),
            pltpu.VMEM((depth, rows, WIDTH), F32),
            pltpu.VMEM((SECTIONS + 1, 16, WIDTH), F32),
            *[pltpu.VMEM(shape, F32) for shape in shapes],
            dma((depth,)), dma((depth,)), dma((7,)),
        ],
        compiler_params=pltpu.CompilerParams(vmem_limit_bytes=48 * 2**20),
    )(reduced, sums, grad)


def on_device(
    block_input, cotangent, group_ids, live_count, group_scale, norm_gain, norm_bias, first_weight,
    qv_bias, up_bias, down_weight, out_bias,
):
    reduced, sums, grad = mega(
        block_input, cotangent, group_ids, live_count, group_scale, norm_gain, norm_bias,
        qv_bias, up_bias, out_bias, first_weight, down_weight,
    )
    first_grad, down_grad, qv_grad, up_grad, bias_grad, gain_grad, shift_grad, input_grad = widen(reduced, sums, grad)
    return input_grad, first_grad, down_grad, qv_grad, up_grad, bias_grad, gain_grad, shift_grad


def solution(mesh):
    in_specs = (
        P("dp", None, None),
        P("dp", None, None),
        P("dp"),
        P("dp"),
        P(),
        P("section", None, None),
        P("section", None, None),
        P("section", None, None),
        P(),
        P(),
        P("section", None),
        P("section", None),
    )
    out_specs = (
        P("dp", None, "section"),
        P("section", None, None),
        P("section", None),
        P(),
        P(),
        P("section", None),
        P("section", None, None),
        P("section", None, None),
    )
    return jax.shard_map(on_device, mesh=mesh, in_specs=in_specs, out_specs=out_specs, check_vma=False)
```

```python
import math

import jax
import jax.numpy as jnp
from jax import lax
from jax.experimental import pallas as pl
from jax.experimental.pallas import tpu as pltpu
from jax.sharding import PartitionSpec as P

MESH = pl.DeviceIdType.MESH
BF16 = jnp.bfloat16
F32 = jnp.float32

WIDTH = 1024
FF = 4096
LEN = 128
SLOTS = 4
ROWS = SLOTS * LEN
PAIRS = 8
SECTIONS = 4
NORM_EPS = 1e-05
GELU_C = math.sqrt(2.0 / math.pi)
CHUNKS = 8
ORDER = (0, 3, 4, 5, 8, 9, 1, 6, 7, 2)
OFFSET_FEED = (0, 1, 2, 4, 5, 6, 7, 8, 11, 13)
OFFSET_ATTEND = (0, 1, 5, 7, 8, 9, 10, 11, 14, 16)


def device(section, x, y, core):
    return (section, x * 8 + y * 2 + core)


def place():
    at = lax.axis_index("dp")
    return lax.axis_index("section"), at // 8, (at // 2) % 4, at % 2


def neighbours(section, x, y, core):
    found = [device(section, x, y, 1 - core)]
    for d in (1, 2, 3):
        found.append(device(section, (x + d) % 4, y, core))
        found.append(device(section, x, (y + d) % 4, core))
        found.append(device((section + d) % 4, x, y, core))
    return found


def greet(section, x, y, core):
    barrier = pltpu.get_barrier_semaphore()
    others = neighbours(section, x, y, core)
    for other in others:
        pl.semaphore_signal(barrier, inc=1, device_id=other, device_id_type=MESH)
    pl.semaphore_wait(barrier, len(others))


def remote(source, target, send_sem, recv_sem, to):
    return pltpu.make_async_remote_copy(
        src_ref=source,
        dst_ref=target,
        send_sem=send_sem,
        recv_sem=recv_sem,
        device_id=to,
        device_id_type=MESH,
    )


def dot(a, b):
    return jnp.dot(a, b, preferred_element_type=F32)


def dot_nt(a, b):
    return lax.dot_general(a, b, (((1,), (1,)), ((), ())), preferred_element_type=F32)


def dot_tn(a, b):
    return lax.dot_general(a, b, (((0,), (0,)), ((), ())), preferred_element_type=F32)


def normalize(entries):
    average = jnp.mean(entries, axis=-1, keepdims=True)
    centered = entries - average
    inverse = lax.rsqrt(jnp.mean(centered * centered, axis=-1, keepdims=True) + NORM_EPS)
    return centered * inverse, inverse


def norm_backward(grad_out, unit, inverse, gain):
    scaled = grad_out * gain
    middle = jnp.mean(scaled, axis=-1, keepdims=True)
    along = jnp.mean(scaled * unit, axis=-1, keepdims=True)
    return inverse * (scaled - middle - unit * along)


def column_sum(entries):
    return jnp.sum(entries, axis=0, keepdims=True)


def mega_kernel(
    block_hbm, cot_hbm, group_hbm, live_hbm, scale_hbm, gains_hbm, shifts_hbm, qv_hbm, up_hbm, bias_hbm, w1_hbm, down_hbm,
    out_hbm, small_hbm, grad_hbm,
    group_ids, live_count, group_scale, gains, shifts, qv_bias, up_bias, out_bias,
    w1, buffer, w2t, ops, units, inverses, r_in, r_out, g_in, g_out, wide, small, vectors,
    pair, r1, r2, r3, r4, z, sx, sy, ss, sums,
    load_sem, down_send, down_recv, ag_send, ag_recv,
    fwd_send, fwd_recv, bwd_send, bwd_recv, ig_send, ig_recv,
    pair_send, pair_recv, pair_free, ring_send, ring_recv, z_send, z_recv, own_sem, last_send, last_recv,
    tiny_send, tiny_recv,
):
    section, x, y, core = place()
    parity = section % 2
    layer = section // 2
    last = section == SECTIONS - 1
    first = section == 0
    sibling = device(section, x, y, 1 - core)
    w1t, w2 = buffer.at[pl.ds(0, FF)], buffer.at[pl.ds(FF, FF)]

    load_w1 = pltpu.make_async_copy(w1_hbm.at[0], w1, load_sem.at[0])
    load_own = pltpu.make_async_copy(down_hbm, w2.at[pl.ds(2048, 2048)], load_sem.at[1])
    load_block = pltpu.make_async_copy(block_hbm, r_in, load_sem.at[2])
    load_cot = pltpu.make_async_copy(cot_hbm, g_in, load_sem.at[3])

    pieces = [
        (gains_hbm, gains), (shifts_hbm, shifts), (bias_hbm, out_bias), (qv_hbm, qv_bias), (up_hbm, up_bias),
        (group_hbm, group_ids), (live_hbm, live_count), (scale_hbm, group_scale),
    ]
    load_pieces = [pltpu.make_async_copy(*piece, load_sem.at[4 + j]) for j, piece in enumerate(pieces)]

    @pl.when(first)
    def _():
        load_block.start()

    for copy in load_pieces:
        copy.start()
    load_w1.start()

    @pl.when(parity == 1)
    def _():
        load_own.start()

    @pl.when(last)
    def _():
        load_cot.start()

    greet(section, x, y, core)

    row_a = core * 512 + y * 128 + x * 32
    row_b = 1024 + core * 512 + x * 128 + y * 32

    def down_copy(half):
        row = row_a if half == 0 else row_b
        return remote(
            down_hbm.at[pl.ds(row, 32)], w2.at[pl.ds(row, 32)], down_send.at[half], down_recv.at[half],
            device((section + 1) % 4, x, y, core),
        )

    def ag_copy(index):
        d = index % 3 + 1
        along_x = device(section, (x + d) % 4, y, core)
        along_y = device(section, x, (y + d) % 4, core)
        if index < 3:
            rows, to = pl.ds(row_a, 32), along_x
        elif index < 6:
            rows, to = pl.ds(row_b, 32), along_y
        elif index < 9:
            rows, to = pl.ds(core * 512 + y * 128, 128), along_y
        elif index < 12:
            rows, to = pl.ds(1024 + core * 512 + x * 128, 128), along_x
        elif index < 16:
            rows, to = pl.ds(core * 512 + (y + index - 12) % 4 * 128, 128), sibling
        else:
            rows, to = pl.ds(1024 + core * 512 + (x + index - 16) % 4 * 128, 128), sibling
        return remote(w2.at[rows], w2.at[rows], ag_send.at[index], ag_recv.at[index], to)

    @pl.when(parity == 0)
    def _():
        down_copy(0).start()
        down_copy(1).start()

    for copy in load_pieces:
        copy.wait()

    @pl.when(parity == 0)
    def _():
        vectors[5:6, :] = qv_bias[layer, 0:1, :]
        vectors[6:7, :] = jnp.zeros((1, WIDTH), F32)
        vectors[7:8, :] = qv_bias[layer, 1:2, :]

    @pl.when(parity == 1)
    def _():
        for j in range(4):
            vectors[5 + j : 6 + j, :] = up_bias[pl.ds(layer, 1), j * WIDTH : (j + 1) * WIDTH]

    def sequence_weight(micro):
        group = group_ids[micro]
        chosen = jnp.float32(0.0)
        for label in range(8):
            chosen = jnp.where(group == label, group_scale[label], chosen)
        weight = jnp.where(micro < live_count[0], chosen, 0.0)
        return jnp.where(last, weight, 1.0)

    small[...] = jnp.zeros_like(small)

    def gather_start():
        for half in (0, 1):
            down_copy(half).wait_recv()
            for index in range(3 * half, 3 * half + 3):
                ag_copy(index).start()
        for half in (0, 1):
            for index in range(3 * half, 3 * half + 3):
                ag_copy(index).wait()
            for index in range(6 + 3 * half, 9 + 3 * half):
                ag_copy(index).start()
            ag_copy(12 + 4 * half).start()
        load_own.wait()

    def gather_end():
        for d in (1, 3, 2):
            for half in (0, 1):
                ag_copy(5 + 3 * half + 4 - d).wait()
                ag_copy(12 + 4 * half + d).start()
        for index in range(12, 20):
            ag_copy(index).wait()

    pl.when(parity == 1)(gather_start)
    pl.when(last)(gather_end)

    @pl.when(parity == 0)
    def _():
        down_copy(0).wait_send()
        down_copy(1).wait_send()

    load_w1.wait()

    @pl.when(first)
    def _():
        load_block.wait()

    @pl.when(last)
    def _():
        load_cot.wait()

    halves = (pl.ds(0, LEN // 2), pl.ds(LEN // 2, LEN // 2))

    def fwd_copy(micro, half):
        rows = halves[half]
        return remote(
            r_out.at[micro, rows], r_in.at[micro, rows], fwd_send.at[micro, half], fwd_recv.at[micro, half],
            device((section + 1) % 4, x, y, core),
        )

    def bwd_copy(micro, half):
        rows = halves[half]
        return remote(
            g_out.at[micro, rows], g_in.at[micro, rows], bwd_send.at[micro, half], bwd_recv.at[micro, half],
            device((section + 3) % 4, x, y, core),
        )

    def ig_copy(micro, d):
        to = (section + d) % 4
        return remote(
            g_out.at[micro, :, pl.ds(d * 256, 256)], grad_hbm.at[micro], ig_send.at[micro, d], ig_recv.at[micro],
            device(to, x, y, core),
        )

    def ig_own(micro):
        return pltpu.make_async_copy(g_out.at[micro, :, pl.ds(0, 256)], grad_hbm.at[micro], ig_send.at[micro, 0])

    lanes = lax.broadcasted_iota(jnp.int32, (LEN, 128), 1)
    low_lanes = lanes < 64

    def two_heads(entries):
        zero = jnp.zeros_like(entries)
        return jnp.concatenate([jnp.where(low_lanes, entries, zero), jnp.where(low_lanes, zero, entries)], axis=0)

    def transposes():
        def one(j, carry):
            cut = pl.ds(pl.multiple_of(j * 256, 256), 256)
            w1t[cut, :] = w1[:, cut].T
            return carry

        lax.fori_loop(0, 16, one, 0)

        @pl.when(parity == 1)
        def _():
            def two(j, carry):
                cut = pl.ds(pl.multiple_of(j * 256, 256), 256)
                w2t[:, cut] = w2[cut, :].T
                return carry

            lax.fori_loop(0, 16, two, 0)

    def attention_forward(micro):
        normed = ops[0, micro]
        for j in range(3):
            part = dot(normed, w1[:, j * WIDTH : (j + 1) * WIDTH]) + vectors[5 + j : 6 + j, :]
            ops[6 + j, micro] = part.astype(BF16)
        rows = lax.broadcasted_iota(jnp.int32, (LEN, 256), 0)
        columns = lax.broadcasted_iota(jnp.int32, (LEN, 256), 1) % 128
        causal = rows >= columns
        for p in range(PAIRS):
            cut = slice(p * 128, (p + 1) * 128)
            query, key, value = (ops[6 + j, micro, :, cut] for j in range(3))
            scores = dot_nt(query, two_heads(key)) * 0.125
            scores = jnp.where(causal, scores, -1e9)
            halves = []
            for half in (scores[:, :128], scores[:, 128:]):
                powers = jnp.exp(half - jnp.max(half, axis=-1, keepdims=True))
                halves.append((powers / jnp.sum(powers, axis=-1, keepdims=True)).astype(BF16))
            weights = jnp.concatenate(halves, axis=1)
            ops[3 + p // 4, micro, :, (p % 4) * 256 : (p % 4 + 1) * 256] = weights
            ops[2, micro, :, cut] = dot(weights, two_heads(value)).astype(BF16)
        wide[...] = dot_nt(ops[2, micro], w1[:, 3 * WIDTH :]) + out_bias[...]

    def feed_forward(micro):
        normed = ops[0, micro]
        branch = out_bias[...]
        for j in (2, 3, 0, 1):
            hidden = dot(normed, w1[:, j * WIDTH : (j + 1) * WIDTH]) + vectors[5 + j : 6 + j, :]
            square = hidden * hidden
            along = jnp.tanh(hidden * (GELU_C + (GELU_C * 0.044715) * square))
            above = 0.5 * (1.0 + along)
            slope = above + 0.5 * hidden * (1.0 - along * along) * (GELU_C + (3.0 * GELU_C * 0.044715) * square)
            active = (hidden * above).astype(BF16)
            ops[6 + j, micro] = slope.astype(BF16)
            ops[2 + j, micro] = active
        for j in (2, 3, 0, 1):
            if j == 0:
                pl.when((micro == 0) & (section == 1))(gather_end)
            branch = branch + dot(ops[2 + j, micro], w2[j * WIDTH : (j + 1) * WIDTH, :])
        wide[...] = branch

    def attention_backward(micro):
        ops[9, micro] = dot(ops[1, micro], w1[:, 3 * WIDTH :]).astype(BF16)
        for p in range(PAIRS):
            cut = slice(p * 128, (p + 1) * 128)
            query, key, value = (ops[6 + j, micro, :, cut] for j in range(3))
            grad = ops[9, micro, :, cut]
            weights = ops[3 + p // 4, micro, :, (p % 4) * 256 : (p % 4 + 1) * 256]
            grad_weights = dot_nt(grad, two_heads(value))
            weights_wide = weights.astype(F32)
            product = weights_wide * grad_weights
            left = product[:, :128] - weights_wide[:, :128] * jnp.sum(product[:, :128], axis=-1, keepdims=True)
            right = product[:, 128:] - weights_wide[:, 128:] * jnp.sum(product[:, 128:], axis=-1, keepdims=True)
            grad_scores = jnp.concatenate([left, right], axis=1).astype(BF16)
            grad_query = dot(grad_scores, two_heads(key)) * 0.125
            both = dot_tn(grad_scores, query) * 0.125
            grad_key = jnp.where(low_lanes, both[:128], both[128:])
            both = dot_tn(weights, grad)
            grad_value = jnp.where(low_lanes, both[:128], both[128:])
            for j, part in enumerate((grad_query, grad_key, grad_value)):
                ops[6 + j, micro, :, cut] = part.astype(BF16)
        total = jnp.zeros((LEN, WIDTH), F32)
        for j in range(3):
            part = ops[6 + j, micro]
            total = total + dot(part, w1t[j * WIDTH : (j + 1) * WIDTH, :])
            if j != 1:
                small[5 + j : 6 + j, :] += column_sum(part.astype(F32))
        wide[...] = total

    def feed_backward(micro):
        grad_branch = ops[1, micro]
        total = jnp.zeros((LEN, WIDTH), F32)
        for j in range(4):
            grad = dot(grad_branch, w2t[:, j * WIDTH : (j + 1) * WIDTH])
            grad = (grad * ops[6 + j, micro].astype(F32)).astype(BF16)
            ops[6 + j, micro] = grad
            small[5 + j : 6 + j, :] += column_sum(grad.astype(F32))
            total = total + dot(grad, w1t[j * WIDTH : (j + 1) * WIDTH, :])
        wide[...] = total

    def forward(micro):
        for half in (0, 1):
            rows = halves[half]

            @pl.when(jnp.logical_not(first))
            def _():
                fwd_copy(micro, half).wait_recv()

            unit, _ = normalize(r_in[micro, rows].astype(F32))
            ops[0, micro, rows] = (unit * gains[0, 0:1, :] + shifts[0, 0:1, :]).astype(BF16)

        @pl.when(parity == 0)
        def _():
            attention_forward(micro)

        @pl.when(parity == 1)
        def _():
            feed_forward(micro)

        for half in (0, 1):
            rows = halves[half]
            unit, inverse = normalize(wide[rows])
            units[micro, rows] = unit.astype(BF16)
            inverses[micro, rows] = inverse

            @pl.when(jnp.logical_not(last))
            def _():
                after = r_in[micro, rows].astype(F32) + unit * gains[0, 1:2, :] + shifts[0, 1:2, :]
                r_out[micro, rows] = after.astype(BF16)
                fwd_copy(micro, half).start()

    def backward(micro):
        weight = sequence_weight(micro)
        for half in (0, 1):
            rows = halves[half]

            @pl.when(jnp.logical_not(last))
            def _():
                bwd_copy(micro, half).wait_recv()

            incoming = g_in[micro, rows].astype(F32) * weight
            unit = units[micro, rows].astype(F32)
            ops[1, micro, rows] = norm_backward(incoming, unit, inverses[micro, rows], gains[0, 1:2, :]).astype(BF16)

        @pl.when(parity == 0)
        def _():
            attention_backward(micro)

        @pl.when(parity == 1)
        def _():
            feed_backward(micro)

        units_pre = []
        for half in (0, 1):
            rows = halves[half]
            unit, inverse = normalize(r_in[micro, rows].astype(F32))
            units_pre.append(unit)
            incoming = g_in[micro, rows].astype(F32) * weight
            grad = incoming + norm_backward(wide[rows], unit, inverse, gains[0, 0:1, :])
            g_out[micro, rows] = grad.astype(BF16)

            @pl.when(jnp.logical_not(first))
            def _():
                bwd_copy(micro, half).start()

        @pl.when(first)
        def _():
            ig_own(micro).start()
            for d in (1, 2, 3):
                ig_copy(micro, d).start()

        for half in (0, 1):
            rows = halves[half]
            incoming = g_in[micro, rows].astype(F32) * weight
            small[0:1, :] += column_sum(wide[rows] * units_pre[half])
            small[1:2, :] += column_sum(incoming * units[micro, rows].astype(F32))
            small[2:3, :] += column_sum(wide[rows])
            small[3:4, :] += column_sum(incoming)
            small[4:5, :] += column_sum(ops[1, micro, rows].astype(F32))

    turn_at = jnp.where(section >= 2, 0, SLOTS)

    def step(t, carry):
        is_forward = jnp.where(last, (t + 1) % 2, jnp.where(t < SLOTS, 1, 0))
        micro = jnp.where(last, t // 2, t % SLOTS)

        @pl.when(t == turn_at)
        def _():
            transposes()

        @pl.when(is_forward == 1)
        def _():
            forward(micro)

        @pl.when(is_forward == 0)
        def _():
            backward(micro)

        return carry

    lax.fori_loop(0, 2 * SLOTS, step, 0)

    def spot(h):
        return (x, y) if h == 0 else (y, x)

    def peer(axis, d):
        if axis == 0:
            return device(section, (x + d) % 4, y, core)
        return device(section, x, (y + d) % 4, core)

    def chunk(q):
        return jnp.where(parity == 1, q, jnp.where(q < 4, q + 4, q - 4))

    def at(q, h, b1, b2, n, c=None):
        c = core if c is None else c
        row = chunk(q) * 1024 + c * 512 + h * 256 + b1 * 64 + b2 * 16
        return pl.ds(pl.multiple_of(row, 16), n)

    def out_at(q, h, b1, b2, n):
        k = chunk(q)
        k = jnp.where((parity == 1) | (k >= 4), k - 2, k)
        row = k * 1024 + core * 512 + h * 256 + b1 * 64 + b2 * 16
        return pl.ds(pl.multiple_of(row, 16), n)

    left, right = pl.ds(0, 512), pl.ds(512, 512)
    both = [(h, d) for h in (0, 1) for d in (0, 1)]

    def ring(stage, q, source, target, to):
        return remote(source, target, ring_send.at[stage // 4], ring_recv.at[stage, q], to)

    def arrived(like, sem):
        pltpu.make_async_copy(like, like, sem).wait()

    def pair_copy(q):
        rows = at(q, 0, 0, 0, 512, 1 - core)
        return remote(buffer.at[rows], pair.at[q % 2], pair_send, pair_recv.at[q % 2], sibling)

    def rs_one(q, h, d):
        p1, _ = spot(h)
        rows = at(q, h, (p1 + 2) % 4, 0, 64)
        return ring(0, q, buffer.at[rows, left if d == 0 else right], r1.at[q, h, d], peer(h, 1 - 2 * d))

    def rs_two(q, h, d):
        p1, _ = spot(h)
        step = 1 - 2 * d
        return ring(1, q, buffer.at[at(q, h, (p1 + step) % 4, 0, 64)], r2.at[q, h, d], peer(h, step))

    def rs_three(q, h, d):
        p1, p2 = spot(h)
        rows = at(q, h, p1, (p2 + 2) % 4, 16)
        return ring(2, q, buffer.at[rows, left if d == 0 else right], r3.at[q, h, d], peer(1 - h, 1 - 2 * d))

    def rs_four(q, h, d):
        p1, p2 = spot(h)
        step = 1 - 2 * d
        return ring(3, q, buffer.at[at(q, h, p1, (p2 + step) % 4, 16)], r4.at[q, h, d], peer(1 - h, step))

    def z_copy(k, h):
        p1, p2 = spot(h)
        row = k * 1024 + core * 512 + h * 256 + p1 * 64 + p2 * 16
        return remote(
            buffer.at[pl.ds(pl.multiple_of(row, 16), 16)], z.at[k, h], z_send, z_recv.at[k, h],
            device((section + 3) % 4, x, y, core),
        )

    def own_copy(q, h):
        p1, p2 = spot(h)
        return pltpu.make_async_copy(
            buffer.at[at(q, h, p1, p2, 16)], out_hbm.at[out_at(q, h, p1, p2, 16)], own_sem.at[q]
        )

    def ag_one(q, h, d):
        p1, p2 = spot(h)
        target = out_hbm.at[out_at(q, h, p1, p2, 16)]
        return ring(4, q, buffer.at[at(q, h, p1, p2, 16)], target, peer(1 - h, 1 - 2 * d))

    def ag_two(q, h, d):
        p1, p2 = spot(h)
        step = 1 - 2 * d
        piece = out_hbm.at[out_at(q, h, p1, (p2 - step) % 4, 16), left if d == 0 else right]
        return ring(5, q, piece, piece, peer(1 - h, step))

    def ag_three(q, h, d):
        p1, _ = spot(h)
        piece = out_hbm.at[out_at(q, h, p1, 0, 64)]
        return ring(6, q, piece, piece, peer(h, 1 - 2 * d))

    def ag_four(q, h, d):
        p1, _ = spot(h)
        step = 1 - 2 * d
        piece = out_hbm.at[out_at(q, h, (p1 - step) % 4, 0, 64), left if d == 0 else right]
        return ring(7, q, piece, piece, peer(h, step))

    def last_copy(q, h, d):
        p1, _ = spot(h)
        piece = out_hbm.at[out_at(q, h, (p1 + d) % 4, 0, 64)]
        return remote(piece, piece, last_send, last_recv, sibling)

    def stage_0(q):
        k = chunk(q)
        feed_down = (parity == 1) & (k < 4)
        from_context = (parity == 0) & (k == 7)
        a = jnp.where(feed_down, 2 + k, jnp.where(from_context, 1, 0))
        b = jnp.where(feed_down, 1, jnp.where(from_context, 2, 2 + k))
        right_side = ops[b].reshape(ROWS, WIDTH)
        for cut in range(4):
            left_side = ops[a, :, :, cut * 256 : (cut + 1) * 256].reshape(ROWS, 256)
            product = dot_tn(left_side, right_side)
            buffer[pl.ds(pl.multiple_of(k * 1024 + cut * 256, 256), 256), :] = product.astype(BF16)
        pl.when(q >= 2)(lambda: pl.semaphore_wait(pair_free, 1))
        pair_copy(q).start()

    def stage_1(q):
        pair_copy(q).wait_recv()
        rows = at(q, 0, 0, 0, 512)
        buffer[rows, :] = buffer[rows, :] + pair[q % 2]

        @pl.when(q < 2 + 4 * parity)
        def _():
            pl.semaphore_signal(pair_free, inc=1, device_id=sibling, device_id_type=MESH)

        for h, d in both:
            rs_one(q, h, d).start()

    def stage_2(q):
        arrived(r1.at[q], ring_recv.at[0, q])
        for h, d in both:
            p1, _ = spot(h)
            rows = at(q, h, (p1 + 1 - 2 * d) % 4, 0, 64)
            cut = left if d == 0 else right
            buffer[rows, cut] = buffer[rows, cut] + r1[q, h, d]
            rs_two(q, h, d).start()

    def stage_3(q):
        arrived(r2.at[q], ring_recv.at[1, q])
        for h in (0, 1):
            p1, _ = spot(h)
            rows = at(q, h, p1, 0, 64)
            total = buffer[rows, :].astype(F32) + r2[q, h, 0].astype(F32) + r2[q, h, 1].astype(F32)
            buffer[rows, :] = total.astype(BF16)
            for d in (0, 1):
                rs_three(q, h, d).start()

    def stage_4(q):
        arrived(r3.at[q], ring_recv.at[2, q])
        for h, d in both:
            p1, p2 = spot(h)
            rows = at(q, h, p1, (p2 + 1 - 2 * d) % 4, 16)
            cut = left if d == 0 else right
            buffer[rows, cut] = buffer[rows, cut] + r3[q, h, d]
            rs_four(q, h, d).start()

    def stage_5(q):
        @pl.when((parity == 1) | (q < 4))
        def _():
            arrived(r4.at[q], ring_recv.at[3, q])
            for h in (0, 1):
                p1, p2 = spot(h)
                rows = at(q, h, p1, p2, 16)
                total = buffer[rows, :].astype(F32) + r4[q, h, 0].astype(F32) + r4[q, h, 1].astype(F32)
                buffer[rows, :] = total.astype(BF16)

        @pl.when((parity == 1) & (q < 2))
        def _():
            for h in (0, 1):
                z_copy(q, h).start()

        @pl.when((parity == 0) & (q >= 4))
        def _():
            for h in (0, 1):
                p1, p2 = spot(h)
                z_copy(q - 4, h).wait_recv()
                buffer[at(q, h, p1, p2, 16), :] = z[q - 4, h]

        @pl.when((parity == 0) | (q >= 2))
        def _():
            for h in (0, 1):
                own_copy(q, h).start()
                for d in (0, 1):
                    ag_one(q, h, d).start()

    def stage_6(q):
        arrived(r4.at[q], ring_recv.at[4, q])
        for h, d in both:
            ag_two(q, h, d).start()
        arrived(r3.at[q], own_sem.at[q])

    def stage_7(q):
        arrived(r3.at[q], ring_recv.at[5, q])
        for h, d in both:
            ag_three(q, h, d).start()
        for h in (0, 1):
            last_copy(q, h, 0).start()

    def stage_8(q):
        arrived(r2.at[q], ring_recv.at[6, q])
        for h, d in both:
            ag_four(q, h, d).start()
        for h in (0, 1):
            last_copy(q, h, 1).start()
            last_copy(q, h, 3).start()

    def stage_9(q):
        arrived(r1.at[q], ring_recv.at[7, q])
        for h in (0, 1):
            last_copy(q, h, 2).start()

    stages = [stage_0, stage_1, stage_2, stage_3, stage_4, stage_5, stage_6, stage_7, stage_8, stage_9]

    def tiny(phase, d):
        if phase == 0:
            return remote(small, sx.at[d - 1], tiny_send.at[d - 1], tiny_recv.at[d - 1], peer(0, d))
        if phase == 1:
            return remote(sums.at[0], sy.at[d - 1], tiny_send.at[d + 2], tiny_recv.at[d + 2], peer(1, d))
        if phase == 2:
            return remote(sums.at[1], ss, tiny_send.at[6], tiny_recv.at[6], sibling)
        return remote(
            sums.at[2], small_hbm.at[section], tiny_send.at[6 + d], tiny_recv.at[6 + d],
            device((section + d) % 4, x, y, core),
        )

    keep_own = [
        pltpu.make_async_copy(sums.at[2], small_hbm.at[section], tiny_send.at[10]),
        pltpu.make_async_copy(sums.at[2], small_hbm.at[SECTIONS], tiny_send.at[11]),
    ]

    def tiny_0():
        for d in (1, 2, 3):
            tiny(0, d).start()

    def tiny_1():
        for d in (1, 2, 3):
            tiny(0, d).wait()
        sums[0] = (small[...] + sx[0]) + (sx[1] + sx[2])
        for d in (1, 2, 3):
            tiny(1, d).start()

    def tiny_2():
        for d in (1, 2, 3):
            tiny(1, d).wait()
        sums[1] = (sums[0] + sy[0]) + (sy[1] + sy[2])
        tiny(2, 1).start()

    def tiny_3():
        tiny(2, 1).wait()
        sums[2] = sums[1] + ss[...]
        for copy in keep_own:
            copy.start()
        for d in (1, 2, 3):
            tiny(3, d).start()

    def slot(t, carry):
        for number, turn in enumerate((tiny_0, tiny_1, tiny_2, tiny_3)):
            pl.when(t == number)(turn)
        for s in ORDER:
            k = t - jnp.where(parity == 1, OFFSET_FEED[s], OFFSET_ATTEND[s])
            live = (k >= 0) & (k < CHUNKS)
            if s < 5:
                live = live & ((parity == 1) | (k < 4))
            elif s == 5:
                live = live & ((parity == 1) | (k < 6))
            else:
                live = live & jnp.where(parity == 1, k >= 2, k < 6)
            pl.when(live)(lambda turn=stages[s], k=k: turn(k))
        return carry

    lax.fori_loop(0, CHUNKS + max(OFFSET_FEED + OFFSET_ATTEND), slot, 0)

    for d in (1, 2, 3):
        tiny(3, d).wait()
    for copy in keep_own:
        copy.wait()

    def sent(rows, sem):
        arrived(buffer.at[pl.ds(0, rows)], sem)

    @pl.when(parity == 1)
    def _():
        sent(8 * 512, pair_send)
        sent(8 * 480, ring_send.at[0])
        sent(2 * 32, z_send)

    @pl.when(parity == 0)
    def _():
        sent(4 * 512, pair_send)
        sent(4 * 480, ring_send.at[0])

    sent(6 * 480, ring_send.at[1])
    sent(6 * 512, last_send)
    sent(6 * 512, last_recv)

    @pl.when(jnp.logical_not(last))
    def _():
        for micro in range(SLOTS):
            for half in (0, 1):
                fwd_copy(micro, half).wait_send()

    @pl.when(jnp.logical_not(first))
    def _():
        for micro in range(SLOTS):
            for half in (0, 1):
                bwd_copy(micro, half).wait_send()
            ig_copy(micro, 1).wait_recv()

    @pl.when(first)
    def _():
        for micro in range(SLOTS):
            ig_own(micro).wait()
            for d in (1, 2, 3):
                ig_copy(micro, d).wait_send()


def mega(block, cot, group_ids, live_count, group_scale, gains, shifts, qv_bias, up_bias, out_bias, w1, down):
    any_space = pl.BlockSpec(memory_space=pl.ANY)
    dma = pltpu.SemaphoreType.DMA
    return pl.pallas_call(
        mega_kernel,
        name="mega",
        out_shape=[
            jax.ShapeDtypeStruct((6 * 1024, WIDTH), BF16),
            jax.ShapeDtypeStruct((SECTIONS + 1, 16, WIDTH), F32),
            jax.ShapeDtypeStruct((SLOTS, LEN, 256), BF16),
        ],
        in_specs=[any_space] * 12,
        out_specs=[any_space, any_space, any_space],
        scratch_shapes=[
            pltpu.SMEM((SLOTS,), jnp.int32),
            pltpu.SMEM((1,), jnp.int32),
            pltpu.SMEM((8,), F32),
            pltpu.VMEM((1, 2, WIDTH), F32),
            pltpu.VMEM((1, 2, WIDTH), F32),
            pltpu.VMEM((2, 2, WIDTH), F32),
            pltpu.VMEM((2, FF), F32),
            pltpu.VMEM((1, WIDTH), F32),
            pltpu.VMEM((WIDTH, FF), BF16),
            pltpu.VMEM((2 * FF, WIDTH), BF16),
            pltpu.VMEM((WIDTH, FF), BF16),
            pltpu.VMEM((10, SLOTS, LEN, WIDTH), BF16),
            pltpu.VMEM((SLOTS, LEN, WIDTH), BF16),
            pltpu.VMEM((SLOTS, LEN, 1), F32),
            pltpu.VMEM((SLOTS, LEN, WIDTH), BF16),
            pltpu.VMEM((SLOTS, LEN, WIDTH), BF16),
            pltpu.VMEM((SLOTS, LEN, WIDTH), BF16),
            pltpu.VMEM((SLOTS, LEN, WIDTH), BF16),
            pltpu.VMEM((LEN, WIDTH), F32),
            pltpu.VMEM((16, WIDTH), F32),
            pltpu.VMEM((16, WIDTH), F32),
            pltpu.VMEM((2, 512, WIDTH), BF16),
            pltpu.VMEM((CHUNKS, 2, 2, 64, 512), BF16),
            pltpu.VMEM((CHUNKS, 2, 2, 64, WIDTH), BF16),
            pltpu.VMEM((CHUNKS, 2, 2, 16, 512), BF16),
            pltpu.VMEM((CHUNKS, 2, 2, 16, WIDTH), BF16),
            pltpu.VMEM((2, 2, 16, WIDTH), BF16),
            pltpu.VMEM((3, 16, WIDTH), F32),
            pltpu.VMEM((3, 16, WIDTH), F32),
            pltpu.VMEM((16, WIDTH), F32),
            pltpu.VMEM((3, 16, WIDTH), F32),
            dma((12,)), dma((2,)), dma((2,)), dma((20,)), dma((20,)),
            dma((SLOTS, 2)), dma((SLOTS, 2)), dma((SLOTS, 2)), dma((SLOTS, 2)),
            dma((SLOTS, 4)), dma((SLOTS,)),
            dma, dma((2,)), pltpu.SemaphoreType.REGULAR,
            dma((2,)), dma((8, CHUNKS)), dma, dma((2, 2)), dma((CHUNKS,)), dma, dma,
            dma((12,)), dma((12,)),
        ],
        compiler_params=pltpu.CompilerParams(
            collective_id=0, has_side_effects=True, vmem_limit_bytes=63 * 2**20
        ),
    )(block, cot, group_ids, live_count, group_scale, gains, shifts, qv_bias, up_bias, out_bias, w1, down)


def widen_kernel(
    reduced, sums_hbm, grad_in,
    first_out, down_out, qv_out, up_out, bias_out, gain_out, shift_out, grad_out,
    narrow, wide, sums, qv, up, bias, gain, shift, in_sem, out_sem, small_sem,
):
    rows, depth = wide.shape[1], wide.shape[0]
    count = 6 * 1024 // rows

    def load(i):
        return pltpu.make_async_copy(reduced.at[pl.ds(i * rows, rows)], narrow.at[i % depth], in_sem.at[i % depth])

    def store(i):
        chunk, cut = i * rows // 1024, pl.ds(i * rows % 1024, rows)
        if chunk < 2:
            target = down_out.at[pl.ds(i * rows, rows)]
        else:
            target = first_out.at[0, cut, pl.ds((chunk - 2) * 1024, 1024)]
        return pltpu.make_async_copy(wide.at[i % depth], target, out_sem.at[i % depth])

    for i in range(depth):
        load(i).start()
    load_sums = pltpu.make_async_copy(sums_hbm, sums, small_sem.at[0])
    load_sums.start()
    move_grad = pltpu.make_async_copy(grad_in, grad_out, small_sem.at[1])
    move_grad.start()
    small = [(qv, qv_out), (up, up_out), (bias, bias_out), (gain, gain_out), (shift, shift_out)]
    small = [pltpu.make_async_copy(*piece, small_sem.at[2 + j]) for j, piece in enumerate(small)]
    for i in range(count):
        load(i).wait()
        if i >= depth:
            store(i - depth).wait()
        wide[i % depth] = narrow[i % depth].astype(F32)
        store(i).start()
        if i + depth < count:
            load(i + depth).start()
        if i == 2:
            load_sums.wait()
            for layer in (0, 1):
                qv[layer, 0:1, :] = sums[2 * layer, 5:6, :]
                qv[layer, 1:2, :] = sums[2 * layer, 7:8, :]
                for j in range(4):
                    up[layer : layer + 1, j * WIDTH : (j + 1) * WIDTH] = sums[2 * layer + 1, 5 + j : 6 + j, :]
            bias[...] = sums[SECTIONS, 4:5, :]
            gain[0] = sums[SECTIONS, 0:2, :]
            shift[0] = sums[SECTIONS, 2:4, :]
            for copy in small:
                copy.start()
    for i in range(count - depth, count):
        store(i).wait()
    for copy in small:
        copy.wait()
    move_grad.wait()


def widen(reduced, sums, grad):
    any_space = pl.BlockSpec(memory_space=pl.ANY)
    rows, depth = 512, 4
    dma = pltpu.SemaphoreType.DMA
    shapes = [(2, 2, WIDTH), (2, FF), (1, WIDTH), (1, 2, WIDTH), (1, 2, WIDTH)]
    return pl.pallas_call(
        widen_kernel,
        name="widen",
        out_shape=[
            jax.ShapeDtypeStruct((1, WIDTH, FF), F32),
            jax.ShapeDtypeStruct((2 * WIDTH, WIDTH), F32),
            *[jax.ShapeDtypeStruct(shape, F32) for shape in shapes],
            jax.ShapeDtypeStruct((SLOTS, LEN, 256), BF16),
        ],
        in_specs=[any_space] * 3,
        out_specs=[any_space] * 8,
        scratch_shapes=[
            pltpu.VMEM((depth, rows, WIDTH), BF16),
            pltpu.VMEM((depth, rows, WIDTH), F32),
            pltpu.VMEM((SECTIONS + 1, 16, WIDTH), F32),
            *[pltpu.VMEM(shape, F32) for shape in shapes],
            dma((depth,)), dma((depth,)), dma((7,)),
        ],
        compiler_params=pltpu.CompilerParams(vmem_limit_bytes=63 * 2**20),
    )(reduced, sums, grad)


def on_device(
    block_input, cotangent, group_ids, live_count, group_scale, norm_gain, norm_bias, first_weight,
    qv_bias, up_bias, down_weight, out_bias,
):
    reduced, sums, grad = mega(
        block_input, cotangent, group_ids, live_count, group_scale, norm_gain, norm_bias,
        qv_bias, up_bias, out_bias, first_weight, down_weight,
    )
    first_grad, down_grad, qv_grad, up_grad, bias_grad, gain_grad, shift_grad, input_grad = widen(reduced, sums, grad)
    return input_grad, first_grad, down_grad, qv_grad, up_grad, bias_grad, gain_grad, shift_grad


def solution(mesh):
    in_specs = (
        P("dp", None, None),
        P("dp", None, None),
        P("dp"),
        P("dp"),
        P(),
        P("section", None, None),
        P("section", None, None),
        P("section", None, None),
        P(),
        P(),
        P("section", None),
        P("section", None),
    )
    out_specs = (
        P("dp", None, "section"),
        P("section", None, None),
        P("section", None),
        P(),
        P(),
        P("section", None),
        P("section", None, None),
        P("section", None, None),
    )
    return jax.shard_map(on_device, mesh=mesh, in_specs=in_specs, out_specs=out_specs, check_vma=False)
```

```python
import math

import jax
import jax.numpy as jnp
from jax import lax
from jax.experimental import pallas as pl
from jax.experimental.pallas import tpu as pltpu
from jax.sharding import PartitionSpec as P

MESH = pl.DeviceIdType.MESH
BF16 = jnp.bfloat16
F32 = jnp.float32

WIDTH = 1024
FF = 4096
LEN = 128
SLOTS = 4
ROWS = SLOTS * LEN
PAIRS = 8
SECTIONS = 4
NORM_EPS = 1e-05
GELU_C = math.sqrt(2.0 / math.pi)
CHUNKS = 8
ORDER = (0, 3, 4, 5, 8, 9, 6, 7, 2)
OFFSET_FEED = (0, 0, 1, 3, 4, 5, 6, 7, 10, 12)
OFFSET_ATTEND = (0, 0, 4, 6, 7, 8, 9, 10, 13, 15)


def device(section, x, y, core):
    return (section, x * 8 + y * 2 + core)


def place():
    at = lax.axis_index("dp")
    return lax.axis_index("section"), at // 8, (at // 2) % 4, at % 2


def neighbours(section, x, y, core):
    found = [device(section, x, y, 1 - core)]
    for d in (1, 2, 3):
        found.append(device(section, (x + d) % 4, y, core))
        found.append(device(section, x, (y + d) % 4, core))
        found.append(device((section + d) % 4, x, y, core))
    return found


def greet(section, x, y, core):
    barrier = pltpu.get_barrier_semaphore()
    others = neighbours(section, x, y, core)
    for other in others:
        pl.semaphore_signal(barrier, inc=1, device_id=other, device_id_type=MESH)
    pl.semaphore_wait(barrier, len(others))


def remote(source, target, send_sem, recv_sem, to):
    return pltpu.make_async_remote_copy(
        src_ref=source,
        dst_ref=target,
        send_sem=send_sem,
        recv_sem=recv_sem,
        device_id=to,
        device_id_type=MESH,
    )


def dot(a, b):
    return jnp.dot(a, b, preferred_element_type=F32)


def dot_nt(a, b):
    return lax.dot_general(a, b, (((1,), (1,)), ((), ())), preferred_element_type=F32)


def dot_tn(a, b):
    return lax.dot_general(a, b, (((0,), (0,)), ((), ())), preferred_element_type=F32)


def normalize(entries):
    average = jnp.mean(entries, axis=-1, keepdims=True)
    centered = entries - average
    inverse = lax.rsqrt(jnp.mean(centered * centered, axis=-1, keepdims=True) + NORM_EPS)
    return centered * inverse, inverse


def norm_backward(grad_out, unit, inverse, gain):
    scaled = grad_out * gain
    middle = jnp.mean(scaled, axis=-1, keepdims=True)
    along = jnp.mean(scaled * unit, axis=-1, keepdims=True)
    return inverse * (scaled - middle - unit * along)


def column_sum(entries):
    return jnp.sum(entries, axis=0, keepdims=True)


def mega_kernel(
    block_hbm, cot_hbm, group_hbm, live_hbm, scale_hbm, gains_hbm, shifts_hbm, qv_hbm, up_hbm, bias_hbm, w1_hbm, down_hbm,
    out_hbm, small_hbm, grad_hbm,
    group_ids, live_count, group_scale, gains, shifts, qv_bias, up_bias, out_bias,
    w1, buffer, w2t, ops, other, units, stats, r_in, r_out, g_in, g_out, wide, small, vectors,
    z, sx, sy, ss, sums,
    load_sem, down_send, down_recv, ag_send, ag_recv,
    fwd_send, fwd_recv, bwd_send, bwd_recv, ig_send, ig_recv,
    swap_send, swap_recv, ready, ring_send, ring_recv, z_send, z_recv, own_sem, last_send, last_recv,
    tiny_send, tiny_recv,
):
    section, x, y, core = place()
    parity = section % 2
    layer = section // 2
    last = section == SECTIONS - 1
    first = section == 0
    sibling = device(section, x, y, 1 - core)
    w1t, w2 = buffer.at[pl.ds(0, FF)], buffer.at[pl.ds(FF, FF)]

    load_w1 = pltpu.make_async_copy(w1_hbm.at[0], w1, load_sem.at[0])
    load_own = pltpu.make_async_copy(down_hbm, w2.at[pl.ds(2048, 2048)], load_sem.at[1])
    load_block = pltpu.make_async_copy(block_hbm, r_in, load_sem.at[2])
    load_cot = pltpu.make_async_copy(cot_hbm, g_in, load_sem.at[3])

    pieces = [
        (gains_hbm, gains), (shifts_hbm, shifts), (bias_hbm, out_bias), (qv_hbm, qv_bias), (up_hbm, up_bias),
        (group_hbm, group_ids), (live_hbm, live_count), (scale_hbm, group_scale),
    ]
    load_pieces = [pltpu.make_async_copy(*piece, load_sem.at[4 + j]) for j, piece in enumerate(pieces)]

    @pl.when(first)
    def _():
        load_block.start()

    for copy in load_pieces:
        copy.start()
    load_w1.start()

    @pl.when(parity == 1)
    def _():
        load_own.start()

    @pl.when(last)
    def _():
        load_cot.start()

    greet(section, x, y, core)

    row_a = core * 512 + y * 128 + x * 32
    row_b = 1024 + core * 512 + x * 128 + y * 32

    def down_copy(half):
        row = row_a if half == 0 else row_b
        return remote(
            down_hbm.at[pl.ds(row, 32)], w2.at[pl.ds(row, 32)], down_send.at[half], down_recv.at[half],
            device((section + 1) % 4, x, y, core),
        )

    def ag_copy(index):
        d = index % 3 + 1
        along_x = device(section, (x + d) % 4, y, core)
        along_y = device(section, x, (y + d) % 4, core)
        if index < 3:
            rows, to = pl.ds(row_a, 32), along_x
        elif index < 6:
            rows, to = pl.ds(row_b, 32), along_y
        elif index < 9:
            rows, to = pl.ds(core * 512 + y * 128, 128), along_y
        elif index < 12:
            rows, to = pl.ds(1024 + core * 512 + x * 128, 128), along_x
        elif index < 16:
            rows, to = pl.ds(core * 512 + (y + index - 12) % 4 * 128, 128), sibling
        else:
            rows, to = pl.ds(1024 + core * 512 + (x + index - 16) % 4 * 128, 128), sibling
        return remote(w2.at[rows], w2.at[rows], ag_send.at[index], ag_recv.at[index], to)

    @pl.when(parity == 0)
    def _():
        down_copy(0).start()
        down_copy(1).start()

    for copy in load_pieces:
        copy.wait()

    @pl.when(parity == 0)
    def _():
        vectors[5:6, :] = qv_bias[layer, 0:1, :]
        vectors[6:7, :] = jnp.zeros((1, WIDTH), F32)
        vectors[7:8, :] = qv_bias[layer, 1:2, :]

    @pl.when(parity == 1)
    def _():
        for j in range(4):
            vectors[5 + j : 6 + j, :] = up_bias[pl.ds(layer, 1), j * WIDTH : (j + 1) * WIDTH]

    def sequence_weight(micro):
        group = group_ids[micro]
        chosen = jnp.float32(0.0)
        for label in range(8):
            chosen = jnp.where(group == label, group_scale[label], chosen)
        weight = jnp.where(micro < live_count[0], chosen, 0.0)
        return jnp.where(last, weight, 1.0)

    small[...] = jnp.zeros_like(small)

    def gather_start():
        for half in (0, 1):
            down_copy(half).wait_recv()
            for index in range(3 * half, 3 * half + 3):
                ag_copy(index).start()
        for half in (0, 1):
            for index in range(3 * half, 3 * half + 3):
                ag_copy(index).wait()
            for index in range(6 + 3 * half, 9 + 3 * half):
                ag_copy(index).start()
            ag_copy(12 + 4 * half).start()
        load_own.wait()

    def gather_end():
        for d in (1, 3, 2):
            for half in (0, 1):
                ag_copy(5 + 3 * half + 4 - d).wait()
                ag_copy(12 + 4 * half + d).start()
        for index in range(12, 20):
            ag_copy(index).wait()

    pl.when(parity == 1)(gather_start)
    pl.when(last)(gather_end)

    @pl.when(parity == 0)
    def _():
        down_copy(0).wait_send()
        down_copy(1).wait_send()

    load_w1.wait()

    @pl.when(first)
    def _():
        load_block.wait()

    @pl.when(last)
    def _():
        load_cot.wait()

    def fwd_copy(micro):
        return remote(
            r_out.at[micro], r_in.at[micro], fwd_send.at[micro], fwd_recv.at[micro],
            device((section + 1) % 4, x, y, core),
        )

    def bwd_copy(micro):
        return remote(
            g_out.at[micro], g_in.at[micro], bwd_send.at[micro], bwd_recv.at[micro],
            device((section + 3) % 4, x, y, core),
        )

    def ig_copy(micro, d):
        to = (section + d) % 4
        return remote(
            g_out.at[micro, :, pl.ds(d * 256, 256)], grad_hbm.at[micro], ig_send.at[micro, d], ig_recv.at[micro],
            device(to, x, y, core),
        )

    def ig_own(micro):
        return pltpu.make_async_copy(g_out.at[micro, :, pl.ds(0, 256)], grad_hbm.at[micro], ig_send.at[micro, 0])

    lanes = lax.broadcasted_iota(jnp.int32, (LEN, 128), 1)
    low_lanes = lanes < 64

    def two_heads(entries):
        zero = jnp.zeros_like(entries)
        return jnp.concatenate([jnp.where(low_lanes, entries, zero), jnp.where(low_lanes, zero, entries)], axis=0)

    def transposes():
        def one(j, carry):
            cut = pl.ds(pl.multiple_of(j * 256, 256), 256)
            w1t[cut, :] = w1[:, cut].T
            return carry

        lax.fori_loop(0, 16, one, 0)

        @pl.when(parity == 1)
        def _():
            def two(j, carry):
                cut = pl.ds(pl.multiple_of(j * 256, 256), 256)
                w2t[:, cut] = w2[cut, :].T
                return carry

            lax.fori_loop(0, 16, two, 0)

    def attention_forward(micro):
        normed = ops[0, micro]
        for j in range(3):
            part = dot(normed, w1[:, j * WIDTH : (j + 1) * WIDTH]) + vectors[5 + j : 6 + j, :]
            ops[6 + j, micro] = part.astype(BF16)
        rows = lax.broadcasted_iota(jnp.int32, (LEN, 256), 0)
        columns = lax.broadcasted_iota(jnp.int32, (LEN, 256), 1) % 128
        causal = rows >= columns
        for p in range(PAIRS):
            cut = slice(p * 128, (p + 1) * 128)
            query, key, value = (ops[6 + j, micro, :, cut] for j in range(3))
            scores = dot_nt(query, two_heads(key)) * 0.125
            scores = jnp.where(causal, scores, -1e9)
            halves = []
            for half in (scores[:, :128], scores[:, 128:]):
                powers = jnp.exp(half - jnp.max(half, axis=-1, keepdims=True))
                halves.append((powers / jnp.sum(powers, axis=-1, keepdims=True)).astype(BF16))
            weights = jnp.concatenate(halves, axis=1)
            ops[3 + p // 4, micro, :, (p % 4) * 256 : (p % 4 + 1) * 256] = weights
            ops[2, micro, :, cut] = dot(weights, two_heads(value)).astype(BF16)
        wide[...] = dot_nt(ops[2, micro], w1[:, 3 * WIDTH :]) + out_bias[...]

    def feed_forward(micro):
        normed = ops[0, micro]
        branch = out_bias[...]
        for j in (2, 3, 0, 1):
            hidden = dot(normed, w1[:, j * WIDTH : (j + 1) * WIDTH]) + vectors[5 + j : 6 + j, :]
            square = hidden * hidden
            along = jnp.tanh(hidden * (GELU_C + (GELU_C * 0.044715) * square))
            above = 0.5 * (1.0 + along)
            slope = above + 0.5 * hidden * (1.0 - along * along) * (GELU_C + (3.0 * GELU_C * 0.044715) * square)
            active = (hidden * above).astype(BF16)
            ops[6 + j, micro] = slope.astype(BF16)
            ops[2 + j, micro] = active
        for j in (2, 3, 0, 1):
            if j == 0:
                pl.when((micro == 0) & (section == 1))(gather_end)
            branch = branch + dot(ops[2 + j, micro], w2[j * WIDTH : (j + 1) * WIDTH, :])
        wide[...] = branch

    def attention_backward(micro):
        ops[9, micro] = dot(ops[1, micro], w1[:, 3 * WIDTH :]).astype(BF16)
        for p in range(PAIRS):
            cut = slice(p * 128, (p + 1) * 128)
            query, key, value = (ops[6 + j, micro, :, cut] for j in range(3))
            grad = ops[9, micro, :, cut]
            weights = ops[3 + p // 4, micro, :, (p % 4) * 256 : (p % 4 + 1) * 256]
            grad_weights = dot_nt(grad, two_heads(value))
            weights_wide = weights.astype(F32)
            product = weights_wide * grad_weights
            left = product[:, :128] - weights_wide[:, :128] * jnp.sum(product[:, :128], axis=-1, keepdims=True)
            right = product[:, 128:] - weights_wide[:, 128:] * jnp.sum(product[:, 128:], axis=-1, keepdims=True)
            grad_scores = jnp.concatenate([left, right], axis=1).astype(BF16)
            grad_query = dot(grad_scores, two_heads(key)) * 0.125
            both = dot_tn(grad_scores, query) * 0.125
            grad_key = jnp.where(low_lanes, both[:128], both[128:])
            both = dot_tn(weights, grad)
            grad_value = jnp.where(low_lanes, both[:128], both[128:])
            for j, part in enumerate((grad_query, grad_key, grad_value)):
                ops[6 + j, micro, :, cut] = part.astype(BF16)
        total = jnp.zeros((LEN, WIDTH), F32)
        for j in range(3):
            part = ops[6 + j, micro]
            total = total + dot(part, w1t[j * WIDTH : (j + 1) * WIDTH, :])
        wide[...] = total

    def feed_backward(micro):
        grad_branch = ops[1, micro]
        total = jnp.zeros((LEN, WIDTH), F32)
        for j in range(4):
            grad = dot(grad_branch, w2t[:, j * WIDTH : (j + 1) * WIDTH])
            grad = (grad * ops[6 + j, micro].astype(F32)).astype(BF16)
            ops[6 + j, micro] = grad
            total = total + dot(grad, w1t[j * WIDTH : (j + 1) * WIDTH, :])
        wide[...] = total

    def swap(block, count, micro, group):
        piece = pl.ds(block, count)
        return remote(ops.at[piece, micro], other.at[piece, micro], swap_send, swap_recv.at[group], sibling)

    def forward(micro):
        @pl.when(jnp.logical_not(first))
        def _():
            fwd_copy(micro).wait_recv()

        residual = r_in[micro].astype(F32)
        mean = jnp.mean(residual, axis=-1, keepdims=True)
        centered = residual - mean
        inverse = lax.rsqrt(jnp.mean(centered * centered, axis=-1, keepdims=True) + NORM_EPS)
        stats[micro, :, 0:1] = mean
        stats[micro, :, 1:2] = inverse
        ops[0, micro] = (centered * inverse * gains[0, 0:1, :] + shifts[0, 0:1, :]).astype(BF16)
        swap(0, 1, micro, 0).start()

        @pl.when(parity == 0)
        def _():
            attention_forward(micro)

        @pl.when(parity == 1)
        def _():
            feed_forward(micro)

        unit, inverse = normalize(wide[...])

        @pl.when(jnp.logical_not(last))
        def _():
            after = r_in[micro].astype(F32) + unit * gains[0, 1:2, :] + shifts[0, 1:2, :]
            r_out[micro] = after.astype(BF16)
            pl.when(micro > 0)(lambda: fwd_copy(micro - 1).wait_send())
            fwd_copy(micro).start()

        units[micro] = unit.astype(BF16)
        stats[micro, :, 2:3] = inverse
        pl.when(parity == 0)(lambda: swap(2, 1, micro, 0).start())
        pl.when(parity == 1)(lambda: swap(2, 4, micro, 0).start())

    def backward(micro):
        @pl.when(jnp.logical_not(last))
        def _():
            bwd_copy(micro).wait_recv()

        weight = sequence_weight(micro)
        incoming = g_in[micro].astype(F32) * weight
        unit = units[micro].astype(F32)
        ops[1, micro] = norm_backward(incoming, unit, stats[micro, :, 2:3], gains[0, 1:2, :]).astype(BF16)
        swap(1, 1, micro, 0).start()

        @pl.when(parity == 0)
        def _():
            attention_backward(micro)

        @pl.when(parity == 1)
        def _():
            feed_backward(micro)

        inverse = stats[micro, :, 1:2]
        unit = (r_in[micro].astype(F32) - stats[micro, :, 0:1]) * inverse
        incoming = g_in[micro].astype(F32) * weight
        grad = incoming + norm_backward(wide[...], unit, inverse, gains[0, 0:1, :])
        g_out[micro] = grad.astype(BF16)

        @pl.when(jnp.logical_not(first))
        def _():
            bwd_copy(micro).start()

        @pl.when(first)
        def _():
            ig_own(micro).start()
            for d in (1, 2, 3):
                ig_copy(micro, d).start()

        r_out[micro] = wide[...].astype(BF16)
        pl.when(parity == 0)(lambda: swap(6, 3, micro, 1).start())
        pl.when(parity == 1)(lambda: swap(6, 4, micro, 1).start())

    def row_sums(micro):
        weight = sequence_weight(micro)
        unit = (r_in[micro].astype(F32) - stats[micro, :, 0:1]) * stats[micro, :, 1:2]
        grad = r_out[micro].astype(F32)
        small[0:1, :] += column_sum(grad * unit)
        small[2:3, :] += column_sum(grad)
        incoming = g_in[micro].astype(F32) * weight
        small[1:2, :] += column_sum(incoming * units[micro].astype(F32))
        small[3:4, :] += column_sum(incoming)
        small[4:5, :] += column_sum(ops[1, micro].astype(F32))
        for j in range(4):
            small[5 + j : 6 + j, :] += column_sum(ops[6 + j, micro].astype(F32))

    turn_at = jnp.where(section >= 2, 0, SLOTS)

    def step(t, carry):
        is_forward = jnp.where(last, (t + 1) % 2, jnp.where(t < SLOTS, 1, 0))
        micro = jnp.where(last, t // 2, t % SLOTS)

        @pl.when((t == SLOTS) & jnp.logical_not(last))
        def _():
            fwd_copy(SLOTS - 1).wait_send()

        @pl.when(t == turn_at)
        def _():
            transposes()

        @pl.when(is_forward == 1)
        def _():
            forward(micro)

        @pl.when(is_forward == 0)
        def _():
            backward(micro)

        return carry

    lax.fori_loop(0, 2 * SLOTS, step, 0)

    def spot(h):
        return (x, y) if h == 0 else (y, x)

    def peer(axis, d):
        if axis == 0:
            return device(section, (x + d) % 4, y, core)
        return device(section, x, (y + d) % 4, core)

    def chunk(q):
        return jnp.where(parity == 1, q, jnp.where(q < 4, 7 - q, q - 4))

    def at(q, h, b1, b2, n, c=None):
        c = core if c is None else c
        row = chunk(q) * 1024 + c * 512 + h * 256 + b1 * 64 + b2 * 16
        return pl.ds(pl.multiple_of(row, 16), n)

    def out_at(q, h, b1, b2, n):
        k = chunk(q)
        k = jnp.where((parity == 1) | (k >= 4), k - 2, k)
        row = k * 1024 + core * 512 + h * 256 + b1 * 64 + b2 * 16
        return pl.ds(pl.multiple_of(row, 16), n)

    left, right = pl.ds(0, 512), pl.ds(512, 512)
    both = [(h, d) for h in (0, 1) for d in (0, 1)]

    def ring(stage, q, source, target, to):
        return remote(source, target, ring_send.at[stage // 4], ring_recv.at[stage, q], to)

    def arrived(like, sem):
        pltpu.make_async_copy(like, like, sem).wait()

    def land_one(q, h, d):
        return w1.at[pl.ds((q * 2 + h) * 64, 64), pl.ds(d * 512, 512)]

    def land_two(q, h, d):
        return w2t.at[pl.ds((q * 2 + h) * 64, 64), pl.ds(d * 1024, 1024)]

    def land_three(q, h, d):
        return w2t.at[pl.ds((q * 2 + h) * 64 + 16, 16), pl.ds(2048 + d * 1024, 512)]

    def land_four(q, h, d):
        return w2t.at[pl.ds((q * 2 + h) * 64, 16), pl.ds(2048 + d * 1024, 1024)]

    def arrived_rows(rows, sem):
        arrived(buffer.at[pl.ds(0, rows)], sem)

    def rs_one(q, h, d):
        p1, _ = spot(h)
        rows = at(q, h, (p1 + 2) % 4, 0, 64)
        return ring(0, q, buffer.at[rows, left if d == 0 else right], land_one(q, h, d), peer(h, 1 - 2 * d))

    def rs_two(q, h, d):
        p1, _ = spot(h)
        step = 1 - 2 * d
        return ring(1, q, buffer.at[at(q, h, (p1 + step) % 4, 0, 64)], land_two(q, h, d), peer(h, step))

    def rs_three(q, h, d):
        p1, p2 = spot(h)
        rows = at(q, h, p1, (p2 + 2) % 4, 16)
        return ring(2, q, buffer.at[rows, left if d == 0 else right], land_three(q, h, d), peer(1 - h, 1 - 2 * d))

    def rs_four(q, h, d):
        p1, p2 = spot(h)
        step = 1 - 2 * d
        return ring(3, q, buffer.at[at(q, h, p1, (p2 + step) % 4, 16)], land_four(q, h, d), peer(1 - h, step))

    def z_copy(k, h):
        p1, p2 = spot(h)
        row = k * 1024 + core * 512 + h * 256 + p1 * 64 + p2 * 16
        return remote(
            buffer.at[pl.ds(pl.multiple_of(row, 16), 16)], z.at[k, h], z_send, z_recv.at[k, h],
            device((section + 3) % 4, x, y, core),
        )

    def own_copy(q, h):
        p1, p2 = spot(h)
        return pltpu.make_async_copy(
            buffer.at[at(q, h, p1, p2, 16)], out_hbm.at[out_at(q, h, p1, p2, 16)], own_sem.at[q]
        )

    def ag_one(q, h, d):
        p1, p2 = spot(h)
        target = out_hbm.at[out_at(q, h, p1, p2, 16)]
        return ring(4, q, buffer.at[at(q, h, p1, p2, 16)], target, peer(1 - h, 1 - 2 * d))

    def ag_two(q, h, d):
        p1, p2 = spot(h)
        step = 1 - 2 * d
        piece = out_hbm.at[out_at(q, h, p1, (p2 - step) % 4, 16), left if d == 0 else right]
        return ring(5, q, piece, piece, peer(1 - h, step))

    def ag_three(q, h, d):
        p1, _ = spot(h)
        piece = out_hbm.at[out_at(q, h, p1, 0, 64)]
        return ring(6, q, piece, piece, peer(h, 1 - 2 * d))

    def ag_four(q, h, d):
        p1, _ = spot(h)
        step = 1 - 2 * d
        piece = out_hbm.at[out_at(q, h, (p1 - step) % 4, 0, 64), left if d == 0 else right]
        return ring(7, q, piece, piece, peer(h, step))

    def last_copy(q, h, d):
        p1, _ = spot(h)
        piece = out_hbm.at[out_at(q, h, (p1 + d) % 4, 0, 64)]
        return remote(piece, piece, last_send, last_recv, sibling)

    def swapped(group):
        counts = ((3, 6), (3, 4))[group]
        pl.when(parity == 0)(lambda: arrived_rows(counts[0] * ROWS, swap_recv.at[group]))
        pl.when(parity == 1)(lambda: arrived_rows(counts[1] * ROWS, swap_recv.at[group]))

    def stage_0(q):
        k = chunk(q)
        feed_down = (parity == 1) & (k < 4)
        from_context = (parity == 0) & (k == 7)
        a = jnp.where(feed_down, 2 + k, jnp.where(from_context, 1, 0))
        b = jnp.where(feed_down, 1, jnp.where(from_context, 2, 2 + k))
        pl.when(q == 0)(lambda: swapped(0))
        pl.when(q == 1 + 3 * parity)(lambda: swapped(1))
        right_own, right_other = ops[b].reshape(ROWS, WIDTH), other[b].reshape(ROWS, WIDTH)
        for cut in range(2):
            columns = pl.ds(pl.multiple_of(core * 512 + cut * 256, 256), 256)
            product = dot_tn(ops[a, :, :, columns].reshape(ROWS, 256), right_own)
            product = product + dot_tn(other[a, :, :, columns].reshape(ROWS, 256), right_other)
            buffer[pl.ds(pl.multiple_of(k * 1024 + core * 512 + cut * 256, 256), 256), :] = product.astype(BF16)
        pl.when(q == 0)(lambda: pl.semaphore_wait(ready, 4))
        for h, d in both:
            rs_one(q, h, d).start()

    def stage_2(q):
        arrived_rows(128, ring_recv.at[0, q])
        for h, d in both:
            p1, _ = spot(h)
            rows = at(q, h, (p1 + 1 - 2 * d) % 4, 0, 64)
            cut = left if d == 0 else right
            buffer[rows, cut] = buffer[rows, cut] + land_one(q, h, d)[...]
            rs_two(q, h, d).start()

    def stage_3(q):
        arrived_rows(256, ring_recv.at[1, q])
        for h in (0, 1):
            p1, _ = spot(h)
            rows = at(q, h, p1, 0, 64)
            total = buffer[rows, :].astype(F32) + land_two(q, h, 0)[...].astype(F32) + land_two(q, h, 1)[...].astype(F32)
            buffer[rows, :] = total.astype(BF16)
            for d in (0, 1):
                rs_three(q, h, d).start()

    def stage_4(q):
        arrived_rows(32, ring_recv.at[2, q])
        for h, d in both:
            p1, p2 = spot(h)
            rows = at(q, h, p1, (p2 + 1 - 2 * d) % 4, 16)
            cut = left if d == 0 else right
            buffer[rows, cut] = buffer[rows, cut] + land_three(q, h, d)[...]
            rs_four(q, h, d).start()

    def stage_5(q):
        @pl.when((parity == 1) | (q < 4))
        def _():
            arrived_rows(64, ring_recv.at[3, q])
            for h in (0, 1):
                p1, p2 = spot(h)
                rows = at(q, h, p1, p2, 16)
                total = buffer[rows, :].astype(F32) + land_four(q, h, 0)[...].astype(F32) + land_four(q, h, 1)[...].astype(F32)
                buffer[rows, :] = total.astype(BF16)

        @pl.when((parity == 1) & (q < 2))
        def _():
            for h in (0, 1):
                z_copy(q, h).start()

        @pl.when((parity == 0) & (q >= 4))
        def _():
            for h in (0, 1):
                p1, p2 = spot(h)
                z_copy(q - 4, h).wait_recv()
                buffer[at(q, h, p1, p2, 16), :] = z[q - 4, h]

        @pl.when((parity == 0) | (q >= 2))
        def _():
            for h in (0, 1):
                own_copy(q, h).start()
                for d in (0, 1):
                    ag_one(q, h, d).start()

    def stage_6(q):
        arrived_rows(64, ring_recv.at[4, q])
        for h, d in both:
            ag_two(q, h, d).start()
        arrived_rows(32, own_sem.at[q])

    def stage_7(q):
        arrived_rows(32, ring_recv.at[5, q])
        for h, d in both:
            ag_three(q, h, d).start()
        for h in (0, 1):
            last_copy(q, h, 0).start()

    def stage_8(q):
        arrived_rows(256, ring_recv.at[6, q])
        for h, d in both:
            ag_four(q, h, d).start()
        for h in (0, 1):
            last_copy(q, h, 1).start()
            last_copy(q, h, 3).start()

    def stage_9(q):
        arrived_rows(128, ring_recv.at[7, q])
        for h in (0, 1):
            last_copy(q, h, 2).start()

    stages = [stage_0, None, stage_2, stage_3, stage_4, stage_5, stage_6, stage_7, stage_8, stage_9]

    def tiny(phase, d):
        if phase == 0:
            return remote(small, sx.at[d - 1], tiny_send.at[d - 1], tiny_recv.at[d - 1], peer(0, d))
        if phase == 1:
            return remote(sums.at[0], sy.at[d - 1], tiny_send.at[d + 2], tiny_recv.at[d + 2], peer(1, d))
        if phase == 2:
            return remote(sums.at[1], ss, tiny_send.at[6], tiny_recv.at[6], sibling)
        return remote(
            sums.at[2], small_hbm.at[section], tiny_send.at[6 + d], tiny_recv.at[6 + d],
            device((section + d) % 4, x, y, core),
        )

    keep_own = [
        pltpu.make_async_copy(sums.at[2], small_hbm.at[section], tiny_send.at[10]),
        pltpu.make_async_copy(sums.at[2], small_hbm.at[SECTIONS], tiny_send.at[11]),
    ]

    def tiny_0():
        for d in (1, 2, 3):
            tiny(0, d).start()

    def tiny_1():
        for d in (1, 2, 3):
            tiny(0, d).wait()
        sums[0] = (small[...] + sx[0]) + (sx[1] + sx[2])
        for d in (1, 2, 3):
            tiny(1, d).start()

    def tiny_2():
        for d in (1, 2, 3):
            tiny(1, d).wait()
        sums[1] = (sums[0] + sy[0]) + (sy[1] + sy[2])
        tiny(2, 1).start()

    def tiny_3():
        tiny(2, 1).wait()
        sums[2] = sums[1] + ss[...]
        for copy in keep_own:
            copy.start()
        for d in (1, 2, 3):
            tiny(3, d).start()

    for axis in (0, 1):
        for d in (1, 3):
            pl.semaphore_signal(ready, inc=1, device_id=peer(axis, d), device_id_type=MESH)

    def slot(t, carry):
        pl.when((t >= 3) & (t < 3 + SLOTS))(lambda: row_sums(t - 3))
        for number, turn in enumerate((tiny_0, tiny_1, tiny_2, tiny_3)):
            pl.when(t == 3 + SLOTS + number)(turn)
        for s in ORDER:
            k = t - jnp.where(parity == 1, OFFSET_FEED[s], OFFSET_ATTEND[s])
            live = (k >= 0) & (k < CHUNKS)
            if s < 5:
                live = live & ((parity == 1) | (k < 4))
            elif s == 5:
                live = live & ((parity == 1) | (k < 6))
            else:
                live = live & jnp.where(parity == 1, k >= 2, k < 6)
            pl.when(live)(lambda turn=stages[s], k=k: turn(k))
        return carry

    lax.fori_loop(0, CHUNKS + max(OFFSET_FEED + OFFSET_ATTEND), slot, 0)

    for d in (1, 2, 3):
        tiny(3, d).wait()
    for copy in keep_own:
        copy.wait()

    def sent(rows, sem):
        arrived(buffer.at[pl.ds(0, rows)], sem)

    @pl.when(parity == 1)
    def _():
        sent(10 * ROWS, swap_send)
        sent(8 * 480, ring_send.at[0])
        sent(2 * 32, z_send)

    @pl.when(parity == 0)
    def _():
        sent(6 * ROWS, swap_send)
        sent(4 * 480, ring_send.at[0])

    sent(6 * 480, ring_send.at[1])
    sent(6 * 512, last_send)
    sent(6 * 512, last_recv)

    @pl.when(jnp.logical_not(first))
    def _():
        for micro in range(SLOTS):
            bwd_copy(micro).wait_send()
            ig_copy(micro, 1).wait_recv()

    @pl.when(first)
    def _():
        for micro in range(SLOTS):
            ig_own(micro).wait()
            for d in (1, 2, 3):
                ig_copy(micro, d).wait_send()


def mega(block, cot, group_ids, live_count, group_scale, gains, shifts, qv_bias, up_bias, out_bias, w1, down):
    any_space = pl.BlockSpec(memory_space=pl.ANY)
    dma = pltpu.SemaphoreType.DMA
    return pl.pallas_call(
        mega_kernel,
        name="mega",
        out_shape=[
            jax.ShapeDtypeStruct((6 * 1024, WIDTH), BF16),
            jax.ShapeDtypeStruct((SECTIONS + 1, 16, WIDTH), F32),
            jax.ShapeDtypeStruct((SLOTS, LEN, 256), BF16),
        ],
        in_specs=[any_space] * 12,
        out_specs=[any_space, any_space, any_space],
        scratch_shapes=[
            pltpu.SMEM((SLOTS,), jnp.int32),
            pltpu.SMEM((1,), jnp.int32),
            pltpu.SMEM((8,), F32),
            pltpu.VMEM((1, 2, WIDTH), F32),
            pltpu.VMEM((1, 2, WIDTH), F32),
            pltpu.VMEM((2, 2, WIDTH), F32),
            pltpu.VMEM((2, FF), F32),
            pltpu.VMEM((1, WIDTH), F32),
            pltpu.VMEM((WIDTH, FF), BF16),
            pltpu.VMEM((2 * FF, WIDTH), BF16),
            pltpu.VMEM((WIDTH, FF), BF16),
            pltpu.VMEM((10, SLOTS, LEN, WIDTH), BF16),
            pltpu.VMEM((10, SLOTS, LEN, WIDTH), BF16),
            pltpu.VMEM((SLOTS, LEN, WIDTH), BF16),
            pltpu.VMEM((SLOTS, LEN, 3), F32),
            pltpu.VMEM((SLOTS, LEN, WIDTH), BF16),
            pltpu.VMEM((SLOTS, LEN, WIDTH), BF16),
            pltpu.VMEM((SLOTS, LEN, WIDTH), BF16),
            pltpu.VMEM((SLOTS, LEN, WIDTH), BF16),
            pltpu.VMEM((LEN, WIDTH), F32),
            pltpu.VMEM((16, WIDTH), F32),
            pltpu.VMEM((16, WIDTH), F32),
            pltpu.VMEM((2, 2, 16, WIDTH), BF16),
            pltpu.VMEM((3, 16, WIDTH), F32),
            pltpu.VMEM((3, 16, WIDTH), F32),
            pltpu.VMEM((16, WIDTH), F32),
            pltpu.VMEM((3, 16, WIDTH), F32),
            dma((12,)), dma((2,)), dma((2,)), dma((20,)), dma((20,)),
            dma((SLOTS,)), dma((SLOTS,)), dma((SLOTS,)), dma((SLOTS,)),
            dma((SLOTS, 4)), dma((SLOTS,)),
            dma, dma((2,)), pltpu.SemaphoreType.REGULAR,
            dma((2,)), dma((8, CHUNKS)), dma, dma((2, 2)), dma((CHUNKS,)), dma, dma,
            dma((12,)), dma((12,)),
        ],
        compiler_params=pltpu.CompilerParams(
            collective_id=0, has_side_effects=True, vmem_limit_bytes=63 * 2**20
        ),
    )(block, cot, group_ids, live_count, group_scale, gains, shifts, qv_bias, up_bias, out_bias, w1, down)


def widen_kernel(
    reduced, sums_hbm, grad_in,
    first_out, down_out, qv_out, up_out, bias_out, gain_out, shift_out, grad_out,
    narrow, wide, sums, qv, up, bias, gain, shift, in_sem, out_sem, small_sem,
):
    rows, depth = wide.shape[1], wide.shape[0]
    count = 6 * 1024 // rows

    def load(i):
        return pltpu.make_async_copy(reduced.at[pl.ds(i * rows, rows)], narrow.at[i % depth], in_sem.at[i % depth])

    def store(i):
        chunk, cut = i * rows // 1024, pl.ds(i * rows % 1024, rows)
        if chunk < 2:
            target = down_out.at[pl.ds(i * rows, rows)]
        else:
            target = first_out.at[0, cut, pl.ds((chunk - 2) * 1024, 1024)]
        return pltpu.make_async_copy(wide.at[i % depth], target, out_sem.at[i % depth])

    for i in range(depth):
        load(i).start()
    load_sums = pltpu.make_async_copy(sums_hbm, sums, small_sem.at[0])
    load_sums.start()
    move_grad = pltpu.make_async_copy(grad_in, grad_out, small_sem.at[1])
    move_grad.start()
    small = [(qv, qv_out), (up, up_out), (bias, bias_out), (gain, gain_out), (shift, shift_out)]
    small = [pltpu.make_async_copy(*piece, small_sem.at[2 + j]) for j, piece in enumerate(small)]
    for i in range(count):
        load(i).wait()
        if i >= depth:
            store(i - depth).wait()
        wide[i % depth] = narrow[i % depth].astype(F32)
        store(i).start()
        if i + depth < count:
            load(i + depth).start()
        if i == 2:
            load_sums.wait()
            for layer in (0, 1):
                qv[layer, 0:1, :] = sums[2 * layer, 5:6, :]
                qv[layer, 1:2, :] = sums[2 * layer, 7:8, :]
                for j in range(4):
                    up[layer : layer + 1, j * WIDTH : (j + 1) * WIDTH] = sums[2 * layer + 1, 5 + j : 6 + j, :]
            bias[...] = sums[SECTIONS, 4:5, :]
            gain[0] = sums[SECTIONS, 0:2, :]
            shift[0] = sums[SECTIONS, 2:4, :]
            for copy in small:
                copy.start()
    for i in range(count - depth, count):
        store(i).wait()
    for copy in small:
        copy.wait()
    move_grad.wait()


def widen(reduced, sums, grad):
    any_space = pl.BlockSpec(memory_space=pl.ANY)
    rows, depth = 512, 4
    dma = pltpu.SemaphoreType.DMA
    shapes = [(2, 2, WIDTH), (2, FF), (1, WIDTH), (1, 2, WIDTH), (1, 2, WIDTH)]
    return pl.pallas_call(
        widen_kernel,
        name="widen",
        out_shape=[
            jax.ShapeDtypeStruct((1, WIDTH, FF), F32),
            jax.ShapeDtypeStruct((2 * WIDTH, WIDTH), F32),
            *[jax.ShapeDtypeStruct(shape, F32) for shape in shapes],
            jax.ShapeDtypeStruct((SLOTS, LEN, 256), BF16),
        ],
        in_specs=[any_space] * 3,
        out_specs=[any_space] * 8,
        scratch_shapes=[
            pltpu.VMEM((depth, rows, WIDTH), BF16),
            pltpu.VMEM((depth, rows, WIDTH), F32),
            pltpu.VMEM((SECTIONS + 1, 16, WIDTH), F32),
            *[pltpu.VMEM(shape, F32) for shape in shapes],
            dma((depth,)), dma((depth,)), dma((7,)),
        ],
        compiler_params=pltpu.CompilerParams(vmem_limit_bytes=63 * 2**20),
    )(reduced, sums, grad)


def on_device(
    block_input, cotangent, group_ids, live_count, group_scale, norm_gain, norm_bias, first_weight,
    qv_bias, up_bias, down_weight, out_bias,
):
    reduced, sums, grad = mega(
        block_input, cotangent, group_ids, live_count, group_scale, norm_gain, norm_bias,
        qv_bias, up_bias, out_bias, first_weight, down_weight,
    )
    first_grad, down_grad, qv_grad, up_grad, bias_grad, gain_grad, shift_grad, input_grad = widen(reduced, sums, grad)
    return input_grad, first_grad, down_grad, qv_grad, up_grad, bias_grad, gain_grad, shift_grad


def solution(mesh):
    in_specs = (
        P("dp", None, None),
        P("dp", None, None),
        P("dp"),
        P("dp"),
        P(),
        P("section", None, None),
        P("section", None, None),
        P("section", None, None),
        P(),
        P(),
        P("section", None),
        P("section", None),
    )
    out_specs = (
        P("dp", None, "section"),
        P("section", None, None),
        P("section", None),
        P(),
        P(),
        P("section", None),
        P("section", None, None),
        P("section", None, None),
    )
    return jax.shard_map(on_device, mesh=mesh, in_specs=in_specs, out_specs=out_specs, check_vma=False)
```

```python
import math

import jax
import jax.numpy as jnp
from jax import lax
from jax.experimental import pallas as pl
from jax.experimental.pallas import tpu as pltpu
from jax.sharding import PartitionSpec as P

MESH = pl.DeviceIdType.MESH
BF16 = jnp.bfloat16
F32 = jnp.float32

WIDTH = 1024
FF = 4096
LEN = 128
SLOTS = 4
ROWS = SLOTS * LEN
PAIRS = 8
SECTIONS = 4
NORM_EPS = 1e-05
GELU_C = math.sqrt(2.0 / math.pi)
CHUNKS = 8
ORDER = (7, 0, 3, 8, 4, 5, 6, 2, 9)
OFFSET_FEED = (0, 0, 1, 3, 4, 5, 6, 8, 10, 12)
OFFSET_ATTEND = (0, 0, 1, 3, 4, 5, 6, 8, 11, 14)


def device(section, x, y, core):
    return (section, x * 8 + y * 2 + core)


def place():
    at = lax.axis_index("dp")
    return lax.axis_index("section"), at // 8, (at // 2) % 4, at % 2


def neighbours(section, x, y, core):
    found = [device(section, x, y, 1 - core)]
    for d in (1, 2, 3):
        found.append(device(section, (x + d) % 4, y, core))
        found.append(device(section, x, (y + d) % 4, core))
        found.append(device((section + d) % 4, x, y, core))
    return found


def greet(section, x, y, core):
    barrier = pltpu.get_barrier_semaphore()
    others = neighbours(section, x, y, core)
    for other in others:
        pl.semaphore_signal(barrier, inc=1, device_id=other, device_id_type=MESH)
    pl.semaphore_wait(barrier, len(others))


def remote(source, target, send_sem, recv_sem, to):
    return pltpu.make_async_remote_copy(
        src_ref=source,
        dst_ref=target,
        send_sem=send_sem,
        recv_sem=recv_sem,
        device_id=to,
        device_id_type=MESH,
    )


def dot(a, b):
    return jnp.dot(a, b, preferred_element_type=F32)


def dot_nt(a, b):
    return lax.dot_general(a, b, (((1,), (1,)), ((), ())), preferred_element_type=F32)


def dot_tn(a, b):
    return lax.dot_general(a, b, (((0,), (0,)), ((), ())), preferred_element_type=F32)


def normalize(entries):
    average = jnp.mean(entries, axis=-1, keepdims=True)
    centered = entries - average
    inverse = lax.rsqrt(jnp.mean(centered * centered, axis=-1, keepdims=True) + NORM_EPS)
    return centered * inverse, inverse


def norm_backward(grad_out, unit, inverse, gain):
    scaled = grad_out * gain
    middle = jnp.mean(scaled, axis=-1, keepdims=True)
    along = jnp.mean(scaled * unit, axis=-1, keepdims=True)
    return inverse * (scaled - middle - unit * along)


def column_sum(entries):
    return jnp.sum(entries, axis=0, keepdims=True)


def mega_kernel(
    block_hbm, cot_hbm, group_hbm, live_hbm, scale_hbm, gains_hbm, shifts_hbm, qv_hbm, up_hbm, bias_hbm, w1_hbm, down_hbm,
    out_hbm, small_hbm, grad_hbm,
    group_ids, live_count, group_scale, gains, shifts, qv_bias, up_bias, out_bias,
    w1, buffer, w2t, ops, other, units, stats, r_in, r_out, g_in, g_out, wide, small, vectors,
    z, sx, sy, ss, sums,
    load_sem, down_send, down_recv, ag_send, ag_recv,
    fwd_send, fwd_recv, bwd_send, bwd_recv, ig_send, ig_recv,
    swap_send, swap_recv, ready, ring_send, ring_recv, z_send, z_recv, export_send, export_recv, own_sem, last_send, last_recv,
    tiny_send, tiny_recv,
):
    section, x, y, core = place()
    parity = section % 2
    layer = section // 2
    last = section == SECTIONS - 1
    first = section == 0
    sibling = device(section, x, y, 1 - core)
    w1t, w2 = buffer.at[pl.ds(0, FF)], buffer.at[pl.ds(FF, FF)]

    load_w1 = pltpu.make_async_copy(w1_hbm.at[0], w1, load_sem.at[0])
    load_own = pltpu.make_async_copy(down_hbm, w2.at[pl.ds(2048, 2048)], load_sem.at[1])
    load_block = pltpu.make_async_copy(block_hbm, r_in, load_sem.at[2])
    load_cot = pltpu.make_async_copy(cot_hbm, g_in, load_sem.at[3])

    pieces = [
        (gains_hbm, gains), (shifts_hbm, shifts), (bias_hbm, out_bias), (qv_hbm, qv_bias), (up_hbm, up_bias),
        (group_hbm, group_ids), (live_hbm, live_count), (scale_hbm, group_scale),
    ]
    load_pieces = [pltpu.make_async_copy(*piece, load_sem.at[4 + j]) for j, piece in enumerate(pieces)]

    @pl.when(first)
    def _():
        load_block.start()

    for copy in load_pieces:
        copy.start()
    load_w1.start()

    @pl.when(parity == 1)
    def _():
        load_own.start()

    @pl.when(last)
    def _():
        load_cot.start()

    greet(section, x, y, core)

    left, right = pl.ds(0, 512), pl.ds(512, 512)
    both = [(h, d) for h in (0, 1) for d in (0, 1)]

    def peer(axis, d):
        if axis == 0:
            return device(section, (x + d) % 4, y, core)
        return device(section, x, (y + d) % 4, core)

    def arrived_rows(rows, sem):
        piece = buffer.at[pl.ds(0, rows)]
        pltpu.make_async_copy(piece, piece, sem).wait()

    def down_rows(h, p, major, minor, n):
        row = h * 1024 + core * 512 + p * 256 + major * 64 + minor * 16
        return pl.ds(pl.multiple_of(row, 16), n)

    def down_spot(h):
        return (y, x) if h == 0 else (x, y)

    def down_copy(p, h):
        rows = down_rows(h, p, *down_spot(h), 16)
        return remote(
            down_hbm.at[rows], w2.at[rows], down_send, down_recv.at[p], device((section + 1) % 4, x, y, core)
        )

    def down_near(p, h, d):
        rows = down_rows(h, p, *down_spot(h), 16)
        return remote(w2.at[rows], w2.at[rows], ag_send, ag_recv.at[0, p], peer(h, d))

    def down_ring(p, h, d):
        rows = down_rows(h, p, down_spot(h)[0], 0, 64)
        return remote(w2.at[rows], w2.at[rows], ag_send, ag_recv.at[1, p], peer(1 - h, 1 - 2 * d))

    def down_pass(p, h, d):
        step = 1 - 2 * d
        rows = down_rows(h, p, (down_spot(h)[0] - step) % 4, 0, 64)
        piece = w2.at[rows, left if d == 0 else right]
        return remote(piece, piece, ag_send, ag_recv.at[2, p], peer(1 - h, step))

    def down_share(p, h, d):
        rows = down_rows(h, p, (down_spot(h)[0] + d) % 4, 0, 64)
        return remote(w2.at[rows], w2.at[rows], ag_send, ag_recv.at[3, 0], sibling)

    @pl.when(parity == 0)
    def _():
        for p in (0, 1):
            for h in (0, 1):
                down_copy(p, h).start()

    for copy in load_pieces:
        copy.wait()

    @pl.when(parity == 0)
    def _():
        vectors[5:6, :] = qv_bias[layer, 0:1, :]
        vectors[6:7, :] = jnp.zeros((1, WIDTH), F32)
        vectors[7:8, :] = qv_bias[layer, 1:2, :]

    @pl.when(parity == 1)
    def _():
        for j in range(4):
            vectors[5 + j : 6 + j, :] = up_bias[pl.ds(layer, 1), j * WIDTH : (j + 1) * WIDTH]

    def sequence_weight(micro):
        group = group_ids[micro]
        chosen = jnp.float32(0.0)
        for label in range(8):
            chosen = jnp.where(group == label, group_scale[label], chosen)
        weight = jnp.where(micro < live_count[0], chosen, 0.0)
        return jnp.where(last, weight, 1.0)

    small[...] = jnp.zeros_like(small)

    def gather_start():
        for p in (0, 1):
            arrived_rows(32, down_recv.at[p])
            for h in (0, 1):
                for d in (1, 3, 2):
                    down_near(p, h, d).start()
        for p in (0, 1):
            arrived_rows(96, ag_recv.at[0, p])
            for h, d in both:
                down_ring(p, h, d).start()
            for h in (0, 1):
                down_share(p, h, 0).start()
        gather_pass(0)
        load_own.wait()

    def gather_pass(p):
        arrived_rows(256, ag_recv.at[1, p])
        for h, d in both:
            down_pass(p, h, d).start()
        for h in (0, 1):
            down_share(p, h, 1).start()
            down_share(p, h, 3).start()

    def gather_end():
        gather_pass(1)
        for p in (0, 1):
            arrived_rows(128, ag_recv.at[2, p])
            for h in (0, 1):
                down_share(p, h, 2).start()
        arrived_rows(1024, ag_recv.at[3, 0])

    pl.when(parity == 1)(gather_start)
    pl.when(last)(gather_end)

    load_w1.wait()

    @pl.when(first)
    def _():
        load_block.wait()

    @pl.when(last)
    def _():
        load_cot.wait()

    def fwd_copy(micro):
        return remote(
            r_out.at[micro], r_in.at[micro], fwd_send.at[micro], fwd_recv.at[micro],
            device((section + 1) % 4, x, y, core),
        )

    def bwd_copy(micro):
        return remote(
            g_out.at[micro], g_in.at[micro], bwd_send.at[micro], bwd_recv.at[micro],
            device((section + 3) % 4, x, y, core),
        )

    def ig_copy(micro, d):
        to = (section + d) % 4
        return remote(
            g_out.at[micro, :, pl.ds(d * 256, 256)], grad_hbm.at[micro], ig_send.at[micro, d], ig_recv.at[micro],
            device(to, x, y, core),
        )

    def ig_own(micro):
        return pltpu.make_async_copy(g_out.at[micro, :, pl.ds(0, 256)], grad_hbm.at[micro], ig_send.at[micro, 0])

    lanes = lax.broadcasted_iota(jnp.int32, (LEN, 128), 1)
    low_lanes = lanes < 64

    def two_heads(entries):
        zero = jnp.zeros_like(entries)
        return jnp.concatenate([jnp.where(low_lanes, entries, zero), jnp.where(low_lanes, zero, entries)], axis=0)

    def transposes():
        def one(j, carry):
            cut = pl.ds(pl.multiple_of(j * 256, 256), 256)
            w1t[cut, :] = w1[:, cut].T
            return carry

        lax.fori_loop(0, 16, one, 0)

        @pl.when(parity == 1)
        def _():
            def two(j, carry):
                cut = pl.ds(pl.multiple_of(j * 256, 256), 256)
                w2t[:, cut] = w2[cut, :].T
                return carry

            lax.fori_loop(0, 16, two, 0)

    def attention_forward(micro):
        normed = ops[0, micro]
        for j in range(3):
            part = dot(normed, w1[:, j * WIDTH : (j + 1) * WIDTH]) + vectors[5 + j : 6 + j, :]
            ops[6 + j, micro] = part.astype(BF16)
        rows = lax.broadcasted_iota(jnp.int32, (LEN, 256), 0)
        columns = lax.broadcasted_iota(jnp.int32, (LEN, 256), 1) % 128
        causal = rows >= columns
        for p in range(PAIRS):
            cut = slice(p * 128, (p + 1) * 128)
            query, key, value = (ops[6 + j, micro, :, cut] for j in range(3))
            scores = dot_nt(query, two_heads(key)) * 0.125
            scores = jnp.where(causal, scores, -1e9)
            halves = []
            for half in (scores[:, :128], scores[:, 128:]):
                powers = jnp.exp(half - jnp.max(half, axis=-1, keepdims=True))
                halves.append((powers / jnp.sum(powers, axis=-1, keepdims=True)).astype(BF16))
            weights = jnp.concatenate(halves, axis=1)
            ops[3 + p // 4, micro, :, (p % 4) * 256 : (p % 4 + 1) * 256] = weights
            ops[2, micro, :, cut] = dot(weights, two_heads(value)).astype(BF16)
        wide[...] = dot_nt(ops[2, micro], w1[:, 3 * WIDTH :]) + out_bias[...]

    def feed_forward(micro):
        normed = ops[0, micro]
        branch = out_bias[...]
        for j in (2, 3, 0, 1):
            hidden = dot(normed, w1[:, j * WIDTH : (j + 1) * WIDTH]) + vectors[5 + j : 6 + j, :]
            square = hidden * hidden
            along = jnp.tanh(hidden * (GELU_C + (GELU_C * 0.044715) * square))
            above = 0.5 * (1.0 + along)
            slope = above + 0.5 * hidden * (1.0 - along * along) * (GELU_C + (3.0 * GELU_C * 0.044715) * square)
            active = (hidden * above).astype(BF16)
            ops[6 + j, micro] = slope.astype(BF16)
            ops[2 + j, micro] = active
        for j in (2, 3, 0, 1):
            if j == 0:
                pl.when((micro == 0) & (section == 1))(gather_end)
            branch = branch + dot(ops[2 + j, micro], w2[j * WIDTH : (j + 1) * WIDTH, :])
        wide[...] = branch

    def attention_backward(micro):
        ops[9, micro] = dot(ops[1, micro], w1[:, 3 * WIDTH :]).astype(BF16)
        for p in range(PAIRS):
            cut = slice(p * 128, (p + 1) * 128)
            query, key, value = (ops[6 + j, micro, :, cut] for j in range(3))
            grad = ops[9, micro, :, cut]
            weights = ops[3 + p // 4, micro, :, (p % 4) * 256 : (p % 4 + 1) * 256]
            grad_weights = dot_nt(grad, two_heads(value))
            weights_wide = weights.astype(F32)
            product = weights_wide * grad_weights
            left = product[:, :128] - weights_wide[:, :128] * jnp.sum(product[:, :128], axis=-1, keepdims=True)
            right = product[:, 128:] - weights_wide[:, 128:] * jnp.sum(product[:, 128:], axis=-1, keepdims=True)
            grad_scores = jnp.concatenate([left, right], axis=1).astype(BF16)
            grad_query = dot(grad_scores, two_heads(key)) * 0.125
            both = dot_tn(grad_scores, query) * 0.125
            grad_key = jnp.where(low_lanes, both[:128], both[128:])
            both = dot_tn(weights, grad)
            grad_value = jnp.where(low_lanes, both[:128], both[128:])
            for j, part in enumerate((grad_query, grad_key, grad_value)):
                ops[6 + j, micro, :, cut] = part.astype(BF16)
        total = jnp.zeros((LEN, WIDTH), F32)
        for j in range(3):
            part = ops[6 + j, micro]
            total = total + dot(part, w1t[j * WIDTH : (j + 1) * WIDTH, :])
        wide[...] = total

    def feed_backward(micro):
        grad_branch = ops[1, micro]
        total = jnp.zeros((LEN, WIDTH), F32)
        for j in range(4):
            grad = dot(grad_branch, w2t[:, j * WIDTH : (j + 1) * WIDTH])
            grad = (grad * ops[6 + j, micro].astype(F32)).astype(BF16)
            ops[6 + j, micro] = grad
            total = total + dot(grad, w1t[j * WIDTH : (j + 1) * WIDTH, :])
        wide[...] = total

    def swap(block, count, micro, group):
        piece = pl.ds(block, count)
        return remote(ops.at[piece, micro], other.at[piece, micro], swap_send, swap_recv.at[group], sibling)

    def forward(micro):
        @pl.when(jnp.logical_not(first))
        def _():
            fwd_copy(micro).wait_recv()

        residual = r_in[micro].astype(F32)
        mean = jnp.mean(residual, axis=-1, keepdims=True)
        centered = residual - mean
        inverse = lax.rsqrt(jnp.mean(centered * centered, axis=-1, keepdims=True) + NORM_EPS)
        stats[micro, :, 0:1] = mean
        stats[micro, :, 1:2] = inverse
        ops[0, micro] = (centered * inverse * gains[0, 0:1, :] + shifts[0, 0:1, :]).astype(BF16)
        swap(0, 1, micro, 0).start()

        @pl.when(parity == 0)
        def _():
            attention_forward(micro)

        @pl.when(parity == 1)
        def _():
            feed_forward(micro)

        unit, inverse = normalize(wide[...])

        @pl.when(jnp.logical_not(last))
        def _():
            after = r_in[micro].astype(F32) + unit * gains[0, 1:2, :] + shifts[0, 1:2, :]
            r_out[micro] = after.astype(BF16)
            pl.when(micro > 0)(lambda: fwd_copy(micro - 1).wait_send())
            fwd_copy(micro).start()

        units[micro] = unit.astype(BF16)
        stats[micro, :, 2:3] = inverse
        pl.when(parity == 0)(lambda: swap(2, 1, micro, 0).start())
        pl.when(parity == 1)(lambda: swap(2, 4, micro, 0).start())

    def backward(micro):
        @pl.when(jnp.logical_not(last))
        def _():
            bwd_copy(micro).wait_recv()

        weight = sequence_weight(micro)
        incoming = g_in[micro].astype(F32) * weight
        unit = units[micro].astype(F32)
        ops[1, micro] = norm_backward(incoming, unit, stats[micro, :, 2:3], gains[0, 1:2, :]).astype(BF16)
        swap(1, 1, micro, 0).start()

        @pl.when(parity == 0)
        def _():
            attention_backward(micro)

        @pl.when(parity == 1)
        def _():
            feed_backward(micro)

        inverse = stats[micro, :, 1:2]
        unit = (r_in[micro].astype(F32) - stats[micro, :, 0:1]) * inverse
        incoming = g_in[micro].astype(F32) * weight
        grad = incoming + norm_backward(wide[...], unit, inverse, gains[0, 0:1, :])
        g_out[micro] = grad.astype(BF16)

        @pl.when(jnp.logical_not(first))
        def _():
            bwd_copy(micro).start()

        @pl.when(first)
        def _():
            ig_own(micro).start()
            for d in (1, 2, 3):
                ig_copy(micro, d).start()

        r_out[micro] = wide[...].astype(BF16)
        pl.when(parity == 0)(lambda: swap(6, 3, micro, 1).start())
        pl.when(parity == 1)(lambda: swap(6, 4, micro, 1).start())

    def row_sums(micro):
        weight = sequence_weight(micro)
        unit = (r_in[micro].astype(F32) - stats[micro, :, 0:1]) * stats[micro, :, 1:2]
        grad = r_out[micro].astype(F32)
        small[0:1, :] += column_sum(grad * unit)
        small[2:3, :] += column_sum(grad)
        incoming = g_in[micro].astype(F32) * weight
        small[1:2, :] += column_sum(incoming * units[micro].astype(F32))
        small[3:4, :] += column_sum(incoming)
        small[4:5, :] += column_sum(ops[1, micro].astype(F32))
        for j in range(4):
            small[5 + j : 6 + j, :] += column_sum(ops[6 + j, micro].astype(F32))

    turn_at = jnp.where(section >= 2, 0, SLOTS)

    def step(t, carry):
        is_forward = jnp.where(last, (t + 1) % 2, jnp.where(t < SLOTS, 1, 0))
        micro = jnp.where(last, t // 2, t % SLOTS)

        @pl.when((t == SLOTS) & jnp.logical_not(last))
        def _():
            fwd_copy(SLOTS - 1).wait_send()

        @pl.when(t == turn_at)
        def _():
            transposes()

        @pl.when(is_forward == 1)
        def _():
            forward(micro)

        @pl.when(is_forward == 0)
        def _():
            backward(micro)

        return carry

    lax.fori_loop(0, 2 * SLOTS, step, 0)

    def spot(h):
        return (x, y) if h == 0 else (y, x)

    sends_out = section == 1
    takes_in = section == 2

    def chunk(q):
        late = jnp.where(takes_in, jnp.where(q == 7, 2, q - 4), jnp.where(q == 4, 1, 0))
        return jnp.where(parity == 1, q, jnp.where(q < 4, 7 - q, late))

    def exported(q):
        return sends_out & (q == 0)

    def imported(q):
        return takes_in & (q == 7)

    def multiplies(q):
        return (parity == 1) | (q < 4)

    def reduces(q):
        return (multiplies(q) & jnp.logical_not(exported(q))) | imported(q)

    def hands_over(q):
        return ((section == 3) & (q < 2)) | (sends_out & (q == 1)) | imported(q)

    def takes_over(q):
        return ((section == 0) & ((q == 4) | (q == 6))) | (takes_in & ((q == 4) | (q == 5)))

    def gathers(q):
        return ((parity == 1) & (q >= 2)) | ((parity == 0) & (q < 4)) | takes_over(q)

    def at(q, h, b1, b2, n):
        row = chunk(q) * 1024 + core * 512 + h * 256 + b1 * 64 + b2 * 16
        return pl.ds(pl.multiple_of(row, 16), n)

    def export_copy():
        return remote(
            buffer.at[pl.ds(pl.multiple_of(core * 512, 512), 512)],
            buffer.at[pl.ds(pl.multiple_of(2048 + core * 512, 512), 512)],
            export_send, export_recv, device((section + 1) % 4, x, y, core),
        )

    def out_at(q, h, b1, b2, n):
        k = chunk(q)
        k = jnp.where((parity == 1) | (k >= 4), k - 2, k)
        row = k * 1024 + core * 512 + h * 256 + b1 * 64 + b2 * 16
        return pl.ds(pl.multiple_of(row, 16), n)

    def ring(stage, q, source, target, to):
        return remote(source, target, ring_send.at[stage // 4], ring_recv.at[stage, q], to)

    def land_one(q, h, d):
        return w1.at[pl.ds((q * 2 + h) * 64, 64), pl.ds(d * 512, 512)]

    def land_two(q, h, d):
        return w2t.at[pl.ds((q * 2 + h) * 64, 64), pl.ds(d * 1024, 1024)]

    def land_three(q, h, d):
        return w2t.at[pl.ds((q * 2 + h) * 64 + 16, 16), pl.ds(2048 + d * 1024, 512)]

    def land_four(q, h, d):
        return w2t.at[pl.ds((q * 2 + h) * 64, 16), pl.ds(2048 + d * 1024, 1024)]

    def rs_one(q, h, d):
        p1, _ = spot(h)
        rows = at(q, h, (p1 + 2) % 4, 0, 64)
        return ring(0, q, buffer.at[rows, left if d == 0 else right], land_one(q, h, d), peer(h, 1 - 2 * d))

    def rs_two(q, h, d):
        p1, _ = spot(h)
        step = 1 - 2 * d
        return ring(1, q, buffer.at[at(q, h, (p1 + step) % 4, 0, 64)], land_two(q, h, d), peer(h, step))

    def rs_three(q, h, d):
        p1, p2 = spot(h)
        rows = at(q, h, p1, (p2 + 2) % 4, 16)
        return ring(2, q, buffer.at[rows, left if d == 0 else right], land_three(q, h, d), peer(1 - h, 1 - 2 * d))

    def rs_four(q, h, d):
        p1, p2 = spot(h)
        step = 1 - 2 * d
        return ring(3, q, buffer.at[at(q, h, p1, (p2 + step) % 4, 16)], land_four(q, h, d), peer(1 - h, step))

    def z_copy(q, h):
        p1, p2 = spot(h)
        to = jnp.where(takes_in, 0, section - 1)
        slot = jnp.where(takes_in, 0, chunk(q))
        return remote(
            buffer.at[at(q, h, p1, p2, 16)], z.at[slot, h], z_send, z_recv.at[slot, h], device(to, x, y, core)
        )

    def z_arrival(q, h):
        return remote(z.at[chunk(q), h], z.at[chunk(q), h], z_send, z_recv.at[chunk(q), h], sibling)

    def own_copy(q, h):
        p1, p2 = spot(h)
        return pltpu.make_async_copy(
            buffer.at[at(q, h, p1, p2, 16)], out_hbm.at[out_at(q, h, p1, p2, 16)], own_sem.at[q]
        )

    def ag_one(q, h, d):
        p1, p2 = spot(h)
        target = out_hbm.at[out_at(q, h, p1, p2, 16)]
        return ring(4, q, buffer.at[at(q, h, p1, p2, 16)], target, peer(1 - h, 1 - 2 * d))

    def ag_two(q, h, d):
        p1, p2 = spot(h)
        step = 1 - 2 * d
        piece = out_hbm.at[out_at(q, h, p1, (p2 - step) % 4, 16), left if d == 0 else right]
        return ring(5, q, piece, piece, peer(1 - h, step))

    def ag_three(q, h, d):
        p1, _ = spot(h)
        piece = out_hbm.at[out_at(q, h, p1, 0, 64)]
        return ring(6, q, piece, piece, peer(h, 1 - 2 * d))

    def ag_four(q, h, d):
        p1, _ = spot(h)
        step = 1 - 2 * d
        piece = out_hbm.at[out_at(q, h, (p1 - step) % 4, 0, 64), left if d == 0 else right]
        return ring(7, q, piece, piece, peer(h, step))

    def last_copy(q, h, d):
        p1, _ = spot(h)
        piece = out_hbm.at[out_at(q, h, (p1 + d) % 4, 0, 64)]
        return remote(piece, piece, last_send, last_recv, sibling)

    def swapped(group):
        counts = ((3, 6), (3, 4))[group]
        pl.when(parity == 0)(lambda: arrived_rows(counts[0] * ROWS, swap_recv.at[group]))
        pl.when(parity == 1)(lambda: arrived_rows(counts[1] * ROWS, swap_recv.at[group]))

    def multiply(q):
        k = chunk(q)
        feed_down = (parity == 1) & (k < 4)
        from_context = (parity == 0) & (k == 7)
        a = jnp.where(feed_down, 2 + k, jnp.where(from_context, 1, 0))
        b = jnp.where(feed_down, 1, jnp.where(from_context, 2, 2 + k))
        pl.when(q == 0)(lambda: swapped(0))
        pl.when(q == 1 + 3 * parity)(lambda: swapped(1))
        right_own, right_other = ops[b].reshape(ROWS, WIDTH), other[b].reshape(ROWS, WIDTH)
        for cut in range(2):
            columns = pl.ds(pl.multiple_of(core * 512 + cut * 256, 256), 256)
            product = dot_tn(ops[a, :, :, columns].reshape(ROWS, 256), right_own)
            product = product + dot_tn(other[a, :, :, columns].reshape(ROWS, 256), right_other)
            buffer[pl.ds(pl.multiple_of(k * 1024 + core * 512 + cut * 256, 256), 256), :] = product.astype(BF16)

    def stage_0(q):
        pl.when(multiplies(q))(lambda: multiply(q))
        pl.when(exported(q))(lambda: export_copy().start())
        pl.when(imported(q))(lambda: export_copy().wait_recv())

        @pl.when(reduces(q))
        def _():
            pl.when(q == jnp.where(sends_out, 1, 0))(lambda: pl.semaphore_wait(ready, 4))
            for h, d in both:
                rs_one(q, h, d).start()

    def stage_2(q):
        arrived_rows(128, ring_recv.at[0, q])
        for h, d in both:
            p1, _ = spot(h)
            rows = at(q, h, (p1 + 1 - 2 * d) % 4, 0, 64)
            cut = left if d == 0 else right
            buffer[rows, cut] = buffer[rows, cut] + land_one(q, h, d)[...]
            rs_two(q, h, d).start()

    def stage_3(q):
        arrived_rows(256, ring_recv.at[1, q])
        for h in (0, 1):
            p1, _ = spot(h)
            rows = at(q, h, p1, 0, 64)
            total = buffer[rows, :].astype(F32) + land_two(q, h, 0)[...].astype(F32) + land_two(q, h, 1)[...].astype(F32)
            buffer[rows, :] = total.astype(BF16)
            for d in (0, 1):
                rs_three(q, h, d).start()

    def stage_4(q):
        arrived_rows(32, ring_recv.at[2, q])
        for h, d in both:
            p1, p2 = spot(h)
            rows = at(q, h, p1, (p2 + 1 - 2 * d) % 4, 16)
            cut = left if d == 0 else right
            buffer[rows, cut] = buffer[rows, cut] + land_three(q, h, d)[...]
            rs_four(q, h, d).start()

    def stage_5(q):
        @pl.when(reduces(q))
        def _():
            arrived_rows(64, ring_recv.at[3, q])
            for h in (0, 1):
                p1, p2 = spot(h)
                rows = at(q, h, p1, p2, 16)
                arrival = land_four(q, h, 0)[...].astype(F32) + land_four(q, h, 1)[...].astype(F32)
                buffer[rows, :] = (buffer[rows, :].astype(F32) + arrival).astype(BF16)

        @pl.when(hands_over(q))
        def _():
            for h in (0, 1):
                z_copy(q, h).start()

        @pl.when(takes_over(q))
        def _():
            for h in (0, 1):
                p1, p2 = spot(h)
                z_arrival(q, h).wait_recv()
                buffer[at(q, h, p1, p2, 16), :] = z[chunk(q), h]

        @pl.when(gathers(q))
        def _():
            for h in (0, 1):
                own_copy(q, h).start()
                for d in (0, 1):
                    ag_one(q, h, d).start()

    def stage_6(q):
        arrived_rows(64, ring_recv.at[4, q])
        for h, d in both:
            ag_two(q, h, d).start()
        arrived_rows(32, own_sem.at[q])

    def stage_7(q):
        arrived_rows(32, ring_recv.at[5, q])
        for h, d in both:
            ag_three(q, h, d).start()
        for h in (0, 1):
            last_copy(q, h, 0).start()

    def stage_8(q):
        arrived_rows(256, ring_recv.at[6, q])
        for h, d in both:
            ag_four(q, h, d).start()
        for h in (0, 1):
            last_copy(q, h, 1).start()
            last_copy(q, h, 3).start()

    def stage_9(q):
        arrived_rows(128, ring_recv.at[7, q])
        for h in (0, 1):
            last_copy(q, h, 2).start()

    stages = [stage_0, None, stage_2, stage_3, stage_4, stage_5, stage_6, stage_7, stage_8, stage_9]

    def tiny(phase, d):
        if phase == 0:
            return remote(small, sx.at[d - 1], tiny_send.at[d - 1], tiny_recv.at[d - 1], peer(0, d))
        if phase == 1:
            return remote(sums.at[0], sy.at[d - 1], tiny_send.at[d + 2], tiny_recv.at[d + 2], peer(1, d))
        if phase == 2:
            return remote(sums.at[1], ss, tiny_send.at[6], tiny_recv.at[6], sibling)
        return remote(
            sums.at[2], small_hbm.at[section], tiny_send.at[6 + d], tiny_recv.at[6 + d],
            device((section + d) % 4, x, y, core),
        )

    keep_own = [
        pltpu.make_async_copy(sums.at[2], small_hbm.at[section], tiny_send.at[10]),
        pltpu.make_async_copy(sums.at[2], small_hbm.at[SECTIONS], tiny_send.at[11]),
    ]

    def tiny_0():
        for d in (1, 2, 3):
            tiny(0, d).start()

    def tiny_1():
        for d in (1, 2, 3):
            tiny(0, d).wait()
        sums[0] = (small[...] + sx[0]) + (sx[1] + sx[2])
        for d in (1, 2, 3):
            tiny(1, d).start()

    def tiny_2():
        for d in (1, 2, 3):
            tiny(1, d).wait()
        sums[1] = (sums[0] + sy[0]) + (sy[1] + sy[2])
        tiny(2, 1).start()

    def tiny_3():
        tiny(2, 1).wait()
        sums[2] = sums[1] + ss[...]
        for copy in keep_own:
            copy.start()
        for d in (1, 2, 3):
            tiny(3, d).start()

    pl.when(parity == 1)(lambda: arrived_rows(1984, ag_send))
    for axis in (0, 1):
        for d in (1, 3):
            pl.semaphore_signal(ready, inc=1, device_id=peer(axis, d), device_id_type=MESH)

    def slot(t, carry):
        pl.when((t >= 3) & (t < 3 + SLOTS))(lambda: row_sums(t - 3))
        for number, turn in enumerate((tiny_0, tiny_1, tiny_2, tiny_3)):
            pl.when(t == 3 + SLOTS + number)(turn)
        for s in ORDER:
            k = t - jnp.where(parity == 1, OFFSET_FEED[s], OFFSET_ATTEND[s])
            live = (k >= 0) & (k < CHUNKS)
            if s == 0:
                live = live & (multiplies(k) | imported(k))
            elif s < 5:
                live = live & reduces(k)
            elif s == 5:
                live = live & (reduces(k) | gathers(k))
            else:
                live = live & gathers(k)
            pl.when(live)(lambda turn=stages[s], k=k: turn(k))
        return carry

    lax.fori_loop(0, CHUNKS + max(OFFSET_FEED + OFFSET_ATTEND), slot, 0)

    for d in (1, 2, 3):
        tiny(3, d).wait()
    for copy in keep_own:
        copy.wait()

    def sent(rows, sem):
        arrived_rows(rows, sem)

    pl.when(parity == 1)(lambda: sent(10 * ROWS, swap_send))
    pl.when(parity == 0)(lambda: sent(6 * ROWS, swap_send))
    pl.when(parity == 0)(lambda: sent(64, down_send))
    for number, (ring_count, z_count) in enumerate(((4, 0), (7, 1), (5, 1), (8, 2))):
        @pl.when(section == number)
        def _():
            sent(ring_count * 480, ring_send.at[0])
            if z_count:
                sent(z_count * 32, z_send)

    pl.when(sends_out)(lambda: export_copy().wait_send())
    sent(6 * 480, ring_send.at[1])
    sent(6 * 512, last_send)
    sent(6 * 512, last_recv)

    @pl.when(jnp.logical_not(first))
    def _():
        for micro in range(SLOTS):
            bwd_copy(micro).wait_send()
            ig_copy(micro, 1).wait_recv()

    @pl.when(first)
    def _():
        for micro in range(SLOTS):
            ig_own(micro).wait()
            for d in (1, 2, 3):
                ig_copy(micro, d).wait_send()


def mega(block, cot, group_ids, live_count, group_scale, gains, shifts, qv_bias, up_bias, out_bias, w1, down):
    any_space = pl.BlockSpec(memory_space=pl.ANY)
    dma = pltpu.SemaphoreType.DMA
    return pl.pallas_call(
        mega_kernel,
        name="mega",
        out_shape=[
            jax.ShapeDtypeStruct((6 * 1024, WIDTH), BF16),
            jax.ShapeDtypeStruct((SECTIONS + 1, 16, WIDTH), F32),
            jax.ShapeDtypeStruct((SLOTS, LEN, 256), BF16),
        ],
        in_specs=[any_space] * 12,
        out_specs=[any_space, any_space, any_space],
        scratch_shapes=[
            pltpu.SMEM((SLOTS,), jnp.int32),
            pltpu.SMEM((1,), jnp.int32),
            pltpu.SMEM((8,), F32),
            pltpu.VMEM((1, 2, WIDTH), F32),
            pltpu.VMEM((1, 2, WIDTH), F32),
            pltpu.VMEM((2, 2, WIDTH), F32),
            pltpu.VMEM((2, FF), F32),
            pltpu.VMEM((1, WIDTH), F32),
            pltpu.VMEM((WIDTH, FF), BF16),
            pltpu.VMEM((2 * FF, WIDTH), BF16),
            pltpu.VMEM((WIDTH, FF), BF16),
            pltpu.VMEM((10, SLOTS, LEN, WIDTH), BF16),
            pltpu.VMEM((10, SLOTS, LEN, WIDTH), BF16),
            pltpu.VMEM((SLOTS, LEN, WIDTH), BF16),
            pltpu.VMEM((SLOTS, LEN, 3), F32),
            pltpu.VMEM((SLOTS, LEN, WIDTH), BF16),
            pltpu.VMEM((SLOTS, LEN, WIDTH), BF16),
            pltpu.VMEM((SLOTS, LEN, WIDTH), BF16),
            pltpu.VMEM((SLOTS, LEN, WIDTH), BF16),
            pltpu.VMEM((LEN, WIDTH), F32),
            pltpu.VMEM((16, WIDTH), F32),
            pltpu.VMEM((16, WIDTH), F32),
            pltpu.VMEM((2, 2, 16, WIDTH), BF16),
            pltpu.VMEM((3, 16, WIDTH), F32),
            pltpu.VMEM((3, 16, WIDTH), F32),
            pltpu.VMEM((16, WIDTH), F32),
            pltpu.VMEM((3, 16, WIDTH), F32),
            dma((12,)), dma, dma((2,)), dma, dma((4, 2)),
            dma((SLOTS,)), dma((SLOTS,)), dma((SLOTS,)), dma((SLOTS,)),
            dma((SLOTS, 4)), dma((SLOTS,)),
            dma, dma((2,)), pltpu.SemaphoreType.REGULAR,
            dma((2,)), dma((8, CHUNKS)), dma, dma((2, 2)), dma, dma, dma((CHUNKS,)), dma, dma,
            dma((12,)), dma((12,)),
        ],
        compiler_params=pltpu.CompilerParams(
            collective_id=0, has_side_effects=True, vmem_limit_bytes=63 * 2**20
        ),
    )(block, cot, group_ids, live_count, group_scale, gains, shifts, qv_bias, up_bias, out_bias, w1, down)


def widen_kernel(
    reduced, sums_hbm, grad_in,
    first_out, down_out, qv_out, up_out, bias_out, gain_out, shift_out, grad_out,
    narrow, wide, sums, qv, up, bias, gain, shift, in_sem, out_sem, small_sem,
):
    rows, depth = wide.shape[1], wide.shape[0]
    count = 6 * 1024 // rows

    def load(i):
        return pltpu.make_async_copy(reduced.at[pl.ds(i * rows, rows)], narrow.at[i % depth], in_sem.at[i % depth])

    def store(i):
        chunk, cut = i * rows // 1024, pl.ds(i * rows % 1024, rows)
        if chunk < 2:
            target = down_out.at[pl.ds(i * rows, rows)]
        else:
            target = first_out.at[0, cut, pl.ds((chunk - 2) * 1024, 1024)]
        return pltpu.make_async_copy(wide.at[i % depth], target, out_sem.at[i % depth])

    for i in range(depth):
        load(i).start()
    load_sums = pltpu.make_async_copy(sums_hbm, sums, small_sem.at[0])
    load_sums.start()
    move_grad = pltpu.make_async_copy(grad_in, grad_out, small_sem.at[1])
    move_grad.start()
    small = [(qv, qv_out), (up, up_out), (bias, bias_out), (gain, gain_out), (shift, shift_out)]
    small = [pltpu.make_async_copy(*piece, small_sem.at[2 + j]) for j, piece in enumerate(small)]
    for i in range(count):
        load(i).wait()
        if i >= depth:
            store(i - depth).wait()
        wide[i % depth] = narrow[i % depth].astype(F32)
        store(i).start()
        if i + depth < count:
            load(i + depth).start()
        if i == 2:
            load_sums.wait()
            for layer in (0, 1):
                qv[layer, 0:1, :] = sums[2 * layer, 5:6, :]
                qv[layer, 1:2, :] = sums[2 * layer, 7:8, :]
                for j in range(4):
                    up[layer : layer + 1, j * WIDTH : (j + 1) * WIDTH] = sums[2 * layer + 1, 5 + j : 6 + j, :]
            bias[...] = sums[SECTIONS, 4:5, :]
            gain[0] = sums[SECTIONS, 0:2, :]
            shift[0] = sums[SECTIONS, 2:4, :]
            for copy in small:
                copy.start()
    for i in range(count - depth, count):
        store(i).wait()
    for copy in small:
        copy.wait()
    move_grad.wait()


def widen(reduced, sums, grad):
    any_space = pl.BlockSpec(memory_space=pl.ANY)
    rows, depth = 512, 4
    dma = pltpu.SemaphoreType.DMA
    shapes = [(2, 2, WIDTH), (2, FF), (1, WIDTH), (1, 2, WIDTH), (1, 2, WIDTH)]
    return pl.pallas_call(
        widen_kernel,
        name="widen",
        out_shape=[
            jax.ShapeDtypeStruct((1, WIDTH, FF), F32),
            jax.ShapeDtypeStruct((2 * WIDTH, WIDTH), F32),
            *[jax.ShapeDtypeStruct(shape, F32) for shape in shapes],
            jax.ShapeDtypeStruct((SLOTS, LEN, 256), BF16),
        ],
        in_specs=[any_space] * 3,
        out_specs=[any_space] * 8,
        scratch_shapes=[
            pltpu.VMEM((depth, rows, WIDTH), BF16),
            pltpu.VMEM((depth, rows, WIDTH), F32),
            pltpu.VMEM((SECTIONS + 1, 16, WIDTH), F32),
            *[pltpu.VMEM(shape, F32) for shape in shapes],
            dma((depth,)), dma((depth,)), dma((7,)),
        ],
        compiler_params=pltpu.CompilerParams(vmem_limit_bytes=63 * 2**20),
    )(reduced, sums, grad)


def on_device(
    block_input, cotangent, group_ids, live_count, group_scale, norm_gain, norm_bias, first_weight,
    qv_bias, up_bias, down_weight, out_bias,
):
    reduced, sums, grad = mega(
        block_input, cotangent, group_ids, live_count, group_scale, norm_gain, norm_bias,
        qv_bias, up_bias, out_bias, first_weight, down_weight,
    )
    first_grad, down_grad, qv_grad, up_grad, bias_grad, gain_grad, shift_grad, input_grad = widen(reduced, sums, grad)
    return input_grad, first_grad, down_grad, qv_grad, up_grad, bias_grad, gain_grad, shift_grad


def solution(mesh):
    in_specs = (
        P("dp", None, None),
        P("dp", None, None),
        P("dp"),
        P("dp"),
        P(),
        P("section", None, None),
        P("section", None, None),
        P("section", None, None),
        P(),
        P(),
        P("section", None),
        P("section", None),
    )
    out_specs = (
        P("dp", None, "section"),
        P("section", None, None),
        P("section", None),
        P(),
        P(),
        P("section", None),
        P("section", None, None),
        P("section", None, None),
    )
    return jax.shard_map(on_device, mesh=mesh, in_specs=in_specs, out_specs=out_specs, check_vma=False)
```

```python
import math

import jax
import jax.numpy as jnp
from jax import lax
from jax.experimental import pallas as pl
from jax.experimental.pallas import tpu as pltpu
from jax.sharding import PartitionSpec as P

MESH = pl.DeviceIdType.MESH
BF16 = jnp.bfloat16
F32 = jnp.float32

WIDTH = 1024
FF = 4096
LEN = 128
SLOTS = 4
ROWS = SLOTS * LEN
PAIRS = 8
SECTIONS = 4
NORM_EPS = 1e-05
GELU_C = math.sqrt(2.0 / math.pi)
CHUNKS = 8
ORDER = (7, 0, 3, 8, 4, 5, 6, 2, 9)
OFFSET_FEED = (0, 0, 1, 3, 4, 5, 6, 8, 10, 12)
OFFSET_ATTEND = (0, 0, 1, 3, 4, 5, 6, 8, 11, 14)


def device(section, x, y, core):
    return (section, x * 8 + y * 2 + core)


def place():
    at = lax.axis_index("dp")
    return lax.axis_index("section"), at // 8, (at // 2) % 4, at % 2


def neighbours(section, x, y, core):
    found = [device(section, x, y, 1 - core)]
    for d in (1, 2, 3):
        found.append(device(section, (x + d) % 4, y, core))
        found.append(device(section, x, (y + d) % 4, core))
        found.append(device((section + d) % 4, x, y, core))
    return found


def greet(section, x, y, core):
    barrier = pltpu.get_barrier_semaphore()
    others = neighbours(section, x, y, core)
    for other in others:
        pl.semaphore_signal(barrier, inc=1, device_id=other, device_id_type=MESH)
    pl.semaphore_wait(barrier, len(others))


def remote(source, target, send_sem, recv_sem, to):
    return pltpu.make_async_remote_copy(
        src_ref=source,
        dst_ref=target,
        send_sem=send_sem,
        recv_sem=recv_sem,
        device_id=to,
        device_id_type=MESH,
    )


def dot(a, b):
    return jnp.dot(a, b, preferred_element_type=F32)


def dot_nt(a, b):
    return lax.dot_general(a, b, (((1,), (1,)), ((), ())), preferred_element_type=F32)


def dot_tn(a, b):
    return lax.dot_general(a, b, (((0,), (0,)), ((), ())), preferred_element_type=F32)


def normalize(entries):
    average = jnp.mean(entries, axis=-1, keepdims=True)
    centered = entries - average
    inverse = lax.rsqrt(jnp.mean(centered * centered, axis=-1, keepdims=True) + NORM_EPS)
    return centered * inverse, inverse


def norm_backward(grad_out, unit, inverse, gain):
    scaled = grad_out * gain
    middle = jnp.mean(scaled, axis=-1, keepdims=True)
    along = jnp.mean(scaled * unit, axis=-1, keepdims=True)
    return inverse * (scaled - middle - unit * along)


def column_sum(entries):
    return jnp.sum(entries, axis=0, keepdims=True)


def mega_kernel(
    block_hbm, cot_hbm, group_hbm, live_hbm, scale_hbm, gains_hbm, shifts_hbm, qv_hbm, up_hbm, bias_hbm, w1_hbm, down_hbm,
    out_hbm, small_hbm, grad_hbm,
    group_ids, live_count, group_scale, gains, shifts, qv_bias, up_bias, out_bias,
    w1, buffer, w2t, ops, other, units, stats, r_in, r_out, g_in, g_out, wide, small, vectors,
    z, sx, sy, ss, sums,
    load_sem, down_send, down_recv, ag_send, ag_recv,
    fwd_send, fwd_recv, bwd_send, bwd_recv, ig_send, ig_recv, token,
    swap_send, swap_recv, ready, ring_send, ring_recv, z_send, z_recv, export_send, export_recv, own_sem, last_send, last_recv,
    tiny_send, tiny_recv,
):
    section, x, y, core = place()
    parity = section % 2
    layer = section // 2
    last = section == SECTIONS - 1
    first = section == 0
    sibling = device(section, x, y, 1 - core)
    w1t, w2 = buffer.at[pl.ds(0, FF)], buffer.at[pl.ds(FF, FF)]

    load_w1 = pltpu.make_async_copy(w1_hbm.at[0], w1, load_sem.at[0])
    load_own = pltpu.make_async_copy(down_hbm, w2.at[pl.ds(2048, 2048)], load_sem.at[1])
    load_block = pltpu.make_async_copy(block_hbm, r_in, load_sem.at[2])
    load_cot = pltpu.make_async_copy(cot_hbm, g_in, load_sem.at[3])

    pieces = [
        (gains_hbm, gains), (shifts_hbm, shifts), (bias_hbm, out_bias), (qv_hbm, qv_bias), (up_hbm, up_bias),
        (group_hbm, group_ids), (live_hbm, live_count), (scale_hbm, group_scale),
    ]
    load_pieces = [pltpu.make_async_copy(*piece, load_sem.at[4 + j]) for j, piece in enumerate(pieces)]

    @pl.when(first)
    def _():
        load_block.start()

    for copy in load_pieces:
        copy.start()
    load_w1.start()

    @pl.when(parity == 1)
    def _():
        load_own.start()

    @pl.when(last)
    def _():
        load_cot.start()

    greet(section, x, y, core)

    left, right = pl.ds(0, 512), pl.ds(512, 512)
    both = [(h, d) for h in (0, 1) for d in (0, 1)]

    def peer(axis, d):
        if axis == 0:
            return device(section, (x + d) % 4, y, core)
        return device(section, x, (y + d) % 4, core)

    def arrived_rows(rows, sem):
        piece = buffer.at[pl.ds(0, rows)]
        pltpu.make_async_copy(piece, piece, sem).wait()

    def down_rows(h, p, major, minor, n):
        row = h * 1024 + core * 512 + p * 256 + major * 64 + minor * 16
        return pl.ds(pl.multiple_of(row, 16), n)

    def down_spot(h):
        return (y, x) if h == 0 else (x, y)

    def down_copy(p, h):
        rows = down_rows(h, p, *down_spot(h), 16)
        return remote(
            down_hbm.at[rows], w2.at[rows], down_send, down_recv.at[p], device((section + 1) % 4, x, y, core)
        )

    def down_near(p, h, d):
        rows = down_rows(h, p, *down_spot(h), 16)
        return remote(w2.at[rows], w2.at[rows], ag_send, ag_recv.at[0, p], peer(h, d))

    def down_ring(p, h, d):
        rows = down_rows(h, p, down_spot(h)[0], 0, 64)
        return remote(w2.at[rows], w2.at[rows], ag_send, ag_recv.at[1, p], peer(1 - h, 1 - 2 * d))

    def down_pass(p, h, d):
        step = 1 - 2 * d
        rows = down_rows(h, p, (down_spot(h)[0] - step) % 4, 0, 64)
        piece = w2.at[rows, left if d == 0 else right]
        return remote(piece, piece, ag_send, ag_recv.at[2, p], peer(1 - h, step))

    def down_share(p, h, d):
        rows = down_rows(h, p, (down_spot(h)[0] + d) % 4, 0, 64)
        return remote(w2.at[rows], w2.at[rows], ag_send, ag_recv.at[3, 0], sibling)

    @pl.when(parity == 0)
    def _():
        for p in (0, 1):
            for h in (0, 1):
                down_copy(p, h).start()

    for copy in load_pieces:
        copy.wait()

    @pl.when(parity == 0)
    def _():
        vectors[5:6, :] = qv_bias[layer, 0:1, :]
        vectors[6:7, :] = jnp.zeros((1, WIDTH), F32)
        vectors[7:8, :] = qv_bias[layer, 1:2, :]

    @pl.when(parity == 1)
    def _():
        for j in range(4):
            vectors[5 + j : 6 + j, :] = up_bias[pl.ds(layer, 1), j * WIDTH : (j + 1) * WIDTH]

    def sequence_weight(micro):
        group = group_ids[micro]
        chosen = jnp.float32(0.0)
        for label in range(8):
            chosen = jnp.where(group == label, group_scale[label], chosen)
        weight = jnp.where(micro < live_count[0], chosen, 0.0)
        return jnp.where(last, weight, 1.0)

    small[...] = jnp.zeros_like(small)

    def gather_start():
        for p in (0, 1):
            arrived_rows(32, down_recv.at[p])
            for h in (0, 1):
                for d in (1, 3, 2):
                    down_near(p, h, d).start()
        for p in (0, 1):
            arrived_rows(96, ag_recv.at[0, p])
            for h, d in both:
                down_ring(p, h, d).start()
            for h in (0, 1):
                down_share(p, h, 0).start()
        gather_pass(0)
        gather_pass(1)
        load_own.wait()

    def gather_pass(p):
        arrived_rows(256, ag_recv.at[1, p])
        for h, d in both:
            down_pass(p, h, d).start()
        for h in (0, 1):
            down_share(p, h, 1).start()
            down_share(p, h, 3).start()

    def gather_end():
        for p in (0, 1):
            arrived_rows(128, ag_recv.at[2, p])
            for h in (0, 1):
                down_share(p, h, 2).start()
        arrived_rows(1024, ag_recv.at[3, 0])

    pl.when(parity == 1)(gather_start)
    pl.when(last)(gather_end)

    load_w1.wait()

    @pl.when(first)
    def _():
        load_block.wait()

    @pl.when(last)
    def _():
        load_cot.wait()

    def fwd_copy(micro):
        return remote(
            r_out.at[micro], r_in.at[micro], fwd_send.at[micro], fwd_recv.at[micro],
            device((section + 1) % 4, x, y, core),
        )

    def bwd_copy(micro):
        return remote(
            g_out.at[micro], g_in.at[micro], bwd_send.at[micro], bwd_recv.at[micro],
            device((section + 3) % 4, x, y, core),
        )

    def ig_copy(micro, d):
        to = (section + d) % 4
        return remote(
            g_out.at[micro, :, pl.ds(d * 256, 256)], grad_hbm.at[micro], ig_send.at[micro, d], ig_recv.at[micro],
            device(to, x, y, core),
        )

    def ig_own(micro):
        return pltpu.make_async_copy(g_out.at[micro, :, pl.ds(0, 256)], grad_hbm.at[micro], ig_send.at[micro, 0])

    lanes = lax.broadcasted_iota(jnp.int32, (LEN, 128), 1)
    low_lanes = lanes < 64

    def two_heads(entries):
        zero = jnp.zeros_like(entries)
        return jnp.concatenate([jnp.where(low_lanes, entries, zero), jnp.where(low_lanes, zero, entries)], axis=0)

    def transposes():
        def one(j, carry):
            cut = pl.ds(pl.multiple_of(j * 256, 256), 256)
            w1t[cut, :] = w1[:, cut].T
            return carry

        lax.fori_loop(0, 16, one, 0)

        @pl.when(parity == 1)
        def _():
            def two(j, carry):
                cut = pl.ds(pl.multiple_of(j * 256, 256), 256)
                w2t[:, cut] = w2[cut, :].T
                return carry

            lax.fori_loop(0, 16, two, 0)

    def attention_forward(micro):
        normed = ops[0, micro]
        for j in range(3):
            part = dot(normed, w1[:, j * WIDTH : (j + 1) * WIDTH]) + vectors[5 + j : 6 + j, :]
            ops[6 + j, micro] = part.astype(BF16)
        rows = lax.broadcasted_iota(jnp.int32, (LEN, LEN), 0)
        columns = lax.broadcasted_iota(jnp.int32, (LEN, LEN), 1)
        causal = rows <= columns
        for p in range(PAIRS):
            cut = slice(p * 128, (p + 1) * 128)
            query, key, value = (ops[6 + j, micro, :, cut] for j in range(3))
            scores = dot_nt(two_heads(key), query) * 0.125
            parts = []
            for head in (0, 1):
                part = jnp.where(causal, scores[head * LEN : (head + 1) * LEN], -1e9)
                powers = jnp.exp(part - jnp.max(part, axis=0, keepdims=True))
                part = (powers / jnp.sum(powers, axis=0, keepdims=True)).astype(BF16)
                ops[3 + p // 4, micro, :, (p % 4 * 2 + head) * 128 : (p % 4 * 2 + head + 1) * 128] = part
                parts.append(part)
            ops[2, micro, :, cut] = dot_tn(jnp.concatenate(parts, axis=0), two_heads(value)).astype(BF16)
        wide[...] = dot_nt(ops[2, micro], w1[:, 3 * WIDTH :]) + out_bias[...]

    def feed_forward(micro):
        normed = ops[0, micro]
        branch = out_bias[...]
        def product(j):
            b, cut = j * 256 // WIDTH, slice(j * 256 % WIDTH, j * 256 % WIDTH + 256)
            return dot(normed, w1[:, j * 256 : (j + 1) * 256]) + vectors[5 + b : 6 + b, cut]

        def gate(j, hidden):
            b, cut = j * 256 // WIDTH, slice(j * 256 % WIDTH, j * 256 % WIDTH + 256)
            square = hidden * hidden
            above = 0.5 + 0.5 * jnp.tanh(hidden * (GELU_C + (GELU_C * 0.044715) * square))
            active = hidden * above
            slope = above + (active - active * above) * (2.0 * GELU_C + (6.0 * GELU_C * 0.044715) * square)
            ops[6 + b, micro, :, cut] = slope.astype(BF16)
            ops[2 + b, micro, :, cut] = active.astype(BF16)

        order = (8, 9, 10, 11, 12, 13, 14, 15, 0, 1, 2, 3, 4, 5, 6, 7)
        hidden = product(order[0])
        for step, j in enumerate(order):
            ahead = product(order[step + 1]) if step + 1 < len(order) else None
            gate(j, hidden)
            hidden = ahead
        branch = out_bias[...]
        for j in (2, 3, 0, 1):
            if j == 0:
                pl.when((micro == 0) & (section == 1))(gather_end)
            branch = branch + dot(ops[2 + j, micro], w2[j * WIDTH : (j + 1) * WIDTH, :])
        wide[...] = branch

    def attention_backward(micro):
        ops[9, micro] = dot(ops[1, micro], w1[:, 3 * WIDTH :]).astype(BF16)
        for p in range(PAIRS):
            cut = slice(p * 128, (p + 1) * 128)
            query, key, value = (ops[6 + j, micro, :, cut] for j in range(3))
            grad = ops[9, micro, :, cut]
            parts = [ops[3 + p // 4, micro, :, (p % 4 * 2 + h) * 128 : (p % 4 * 2 + h + 1) * 128] for h in (0, 1)]
            grad_weights = dot_nt(two_heads(value), grad)
            grad_scores = []
            for head in (0, 1):
                part = parts[head].astype(F32)
                product = part * grad_weights[head * LEN : (head + 1) * LEN]
                grad_scores.append((product - part * jnp.sum(product, axis=0, keepdims=True)).astype(BF16))
            grad_scores = jnp.concatenate(grad_scores, axis=0)
            grad_query = dot_tn(grad_scores, two_heads(key)) * 0.125
            both_heads = dot(grad_scores, query) * 0.125
            grad_key = jnp.where(low_lanes, both_heads[:LEN], both_heads[LEN:])
            both_heads = dot(jnp.concatenate(parts, axis=0), grad)
            grad_value = jnp.where(low_lanes, both_heads[:LEN], both_heads[LEN:])
            for j, part in enumerate((grad_query, grad_key, grad_value)):
                ops[6 + j, micro, :, cut] = part.astype(BF16)
        total = jnp.zeros((LEN, WIDTH), F32)
        for j in range(3):
            part = ops[6 + j, micro]
            total = total + dot(part, w1t[j * WIDTH : (j + 1) * WIDTH, :])
        wide[...] = total

    def feed_backward(micro):
        grad_branch = ops[1, micro]
        total = jnp.zeros((LEN, WIDTH), F32)
        for j in range(4):
            grad = dot(grad_branch, w2t[:, j * WIDTH : (j + 1) * WIDTH])
            grad = (grad * ops[6 + j, micro].astype(F32)).astype(BF16)
            ops[6 + j, micro] = grad
            total = total + dot(grad, w1t[j * WIDTH : (j + 1) * WIDTH, :])
        wide[...] = total

    def swap(block, count, micro, group):
        piece = pl.ds(block, count)
        return remote(ops.at[piece, micro], other.at[piece, micro], swap_send, swap_recv.at[group], sibling)

    def forward(micro):
        @pl.when(jnp.logical_not(first))
        def _():
            fwd_copy(micro).wait_recv()

        residual = r_in[micro].astype(F32)
        mean = jnp.mean(residual, axis=-1, keepdims=True)
        centered = residual - mean
        inverse = lax.rsqrt(jnp.mean(centered * centered, axis=-1, keepdims=True) + NORM_EPS)
        stats[micro, :, 0:1] = mean
        stats[micro, :, 1:2] = inverse
        ops[0, micro] = (centered * inverse * gains[0, 0:1, :] + shifts[0, 0:1, :]).astype(BF16)
        swap(0, 1, micro, 0).start()

        @pl.when(parity == 0)
        def _():
            attention_forward(micro)

        @pl.when(parity == 1)
        def _():
            feed_forward(micro)

        unit, inverse = normalize(wide[...])

        @pl.when(jnp.logical_not(last))
        def _():
            after = r_in[micro].astype(F32) + unit * gains[0, 1:2, :] + shifts[0, 1:2, :]
            r_out[micro] = after.astype(BF16)
            leads = (section == 1) & (core == 1)
            follows = (section == 1) & (core == 0)
            pl.when(micro > jnp.where(leads, 1, 0))(lambda: fwd_copy(micro - 1).wait_send())
            pl.when(follows & (micro == 0))(lambda: pl.semaphore_wait(token, 1))
            fwd_copy(micro).start()

            @pl.when(leads & (micro == 0))
            def _():
                fwd_copy(micro).wait_send()
                pl.semaphore_signal(token, inc=1, device_id=sibling, device_id_type=MESH)

        units[micro] = unit.astype(BF16)
        stats[micro, :, 2:3] = inverse
        pl.when(parity == 0)(lambda: swap(2, 1, micro, 0).start())
        pl.when(parity == 1)(lambda: swap(2, 4, micro, 0).start())

    def backward(micro):
        @pl.when(jnp.logical_not(last))
        def _():
            bwd_copy(micro).wait_recv()

        weight = sequence_weight(micro)
        incoming = g_in[micro].astype(F32) * weight
        unit = units[micro].astype(F32)
        ops[1, micro] = norm_backward(incoming, unit, stats[micro, :, 2:3], gains[0, 1:2, :]).astype(BF16)
        swap(1, 1, micro, 0).start()

        @pl.when(parity == 0)
        def _():
            attention_backward(micro)

        @pl.when(parity == 1)
        def _():
            feed_backward(micro)

        inverse = stats[micro, :, 1:2]
        unit = (r_in[micro].astype(F32) - stats[micro, :, 0:1]) * inverse
        incoming = g_in[micro].astype(F32) * weight
        grad = incoming + norm_backward(wide[...], unit, inverse, gains[0, 0:1, :])
        g_out[micro] = grad.astype(BF16)

        @pl.when(jnp.logical_not(first))
        def _():
            bwd_copy(micro).start()

        @pl.when(first)
        def _():
            ig_own(micro).start()
            for d in (1, 2, 3):
                ig_copy(micro, d).start()

        r_out[micro] = wide[...].astype(BF16)
        pl.when(parity == 0)(lambda: swap(6, 3, micro, 1).start())
        pl.when(parity == 1)(lambda: swap(6, 4, micro, 1).start())

    def row_sums(micro):
        weight = sequence_weight(micro)
        unit = (r_in[micro].astype(F32) - stats[micro, :, 0:1]) * stats[micro, :, 1:2]
        grad = r_out[micro].astype(F32)
        small[0:1, :] += column_sum(grad * unit)
        small[2:3, :] += column_sum(grad)
        incoming = g_in[micro].astype(F32) * weight
        small[1:2, :] += column_sum(incoming * units[micro].astype(F32))
        small[3:4, :] += column_sum(incoming)
        small[4:5, :] += column_sum(ops[1, micro].astype(F32))
        for j in range(4):
            small[5 + j : 6 + j, :] += column_sum(ops[6 + j, micro].astype(F32))

    turn_at = jnp.where(section >= 2, 0, SLOTS)

    def step(t, carry):
        is_forward = jnp.where(last, (t + 1) % 2, jnp.where(t < SLOTS, 1, 0))
        micro = jnp.where(last, t // 2, t % SLOTS)

        @pl.when((t == SLOTS) & jnp.logical_not(last))
        def _():
            fwd_copy(SLOTS - 1).wait_send()

        @pl.when(t == turn_at)
        def _():
            transposes()

        @pl.when(is_forward == 1)
        def _():
            forward(micro)

        @pl.when(is_forward == 0)
        def _():
            backward(micro)

        return carry

    lax.fori_loop(0, 2 * SLOTS, step, 0)

    def spot(h):
        return (x, y) if h == 0 else (y, x)

    sends_out = section == 1
    takes_in = section == 2

    def chunk(q):
        late = jnp.where(takes_in, jnp.where(q == 7, 2, q - 4), jnp.where(q == 4, 1, 0))
        return jnp.where(parity == 1, q, jnp.where(q < 4, 7 - q, late))

    def exported(q):
        return sends_out & (q == 0)

    def imported(q):
        return takes_in & (q == 7)

    def multiplies(q):
        return (parity == 1) | (q < 4)

    def reduces(q):
        return (multiplies(q) & jnp.logical_not(exported(q))) | imported(q)

    def hands_over(q):
        return ((section == 3) & (q < 2)) | (sends_out & (q == 1)) | imported(q)

    def takes_over(q):
        return ((section == 0) & ((q == 4) | (q == 6))) | (takes_in & ((q == 4) | (q == 5)))

    def gathers(q):
        return ((parity == 1) & (q >= 2)) | ((parity == 0) & (q < 4)) | takes_over(q)

    def at(q, h, b1, b2, n):
        row = chunk(q) * 1024 + core * 512 + h * 256 + b1 * 64 + b2 * 16
        return pl.ds(pl.multiple_of(row, 16), n)

    def export_copy():
        return remote(
            buffer.at[pl.ds(pl.multiple_of(core * 512, 512), 512)],
            buffer.at[pl.ds(pl.multiple_of(2048 + core * 512, 512), 512)],
            export_send, export_recv, device((section + 1) % 4, x, y, core),
        )

    def out_at(q, h, b1, b2, n):
        k = chunk(q)
        k = jnp.where((parity == 1) | (k >= 4), k - 2, k)
        row = k * 1024 + core * 512 + h * 256 + b1 * 64 + b2 * 16
        return pl.ds(pl.multiple_of(row, 16), n)

    def ring(stage, q, source, target, to):
        return remote(source, target, ring_send.at[stage // 4], ring_recv.at[stage, q], to)

    def land_one(q, h, d):
        return w1.at[pl.ds((q * 2 + h) * 64, 64), pl.ds(d * 512, 512)]

    def land_two(q, h, d):
        return w2t.at[pl.ds((q * 2 + h) * 64, 64), pl.ds(d * 1024, 1024)]

    def land_three(q, h, d):
        return w2t.at[pl.ds((q * 2 + h) * 64 + 16, 16), pl.ds(2048 + d * 1024, 512)]

    def land_four(q, h, d):
        return w2t.at[pl.ds((q * 2 + h) * 64, 16), pl.ds(2048 + d * 1024, 1024)]

    def rs_one(q, h, d):
        p1, _ = spot(h)
        rows = at(q, h, (p1 + 2) % 4, 0, 64)
        return ring(0, q, buffer.at[rows, left if d == 0 else right], land_one(q, h, d), peer(h, 1 - 2 * d))

    def rs_two(q, h, d):
        p1, _ = spot(h)
        step = 1 - 2 * d
        return ring(1, q, buffer.at[at(q, h, (p1 + step) % 4, 0, 64)], land_two(q, h, d), peer(h, step))

    def rs_three(q, h, d):
        p1, p2 = spot(h)
        rows = at(q, h, p1, (p2 + 2) % 4, 16)
        return ring(2, q, buffer.at[rows, left if d == 0 else right], land_three(q, h, d), peer(1 - h, 1 - 2 * d))

    def rs_four(q, h, d):
        p1, p2 = spot(h)
        step = 1 - 2 * d
        return ring(3, q, buffer.at[at(q, h, p1, (p2 + step) % 4, 16)], land_four(q, h, d), peer(1 - h, step))

    def z_copy(q, h):
        p1, p2 = spot(h)
        to = jnp.where(takes_in, 0, section - 1)
        slot = jnp.where(takes_in, 0, chunk(q))
        return remote(
            buffer.at[at(q, h, p1, p2, 16)], z.at[slot, h], z_send, z_recv.at[slot, h], device(to, x, y, core)
        )

    def z_arrival(q, h):
        return remote(z.at[chunk(q), h], z.at[chunk(q), h], z_send, z_recv.at[chunk(q), h], sibling)

    def own_copy(q, h):
        p1, p2 = spot(h)
        return pltpu.make_async_copy(
            buffer.at[at(q, h, p1, p2, 16)], out_hbm.at[out_at(q, h, p1, p2, 16)], own_sem.at[q]
        )

    def ag_one(q, h, d):
        p1, p2 = spot(h)
        target = out_hbm.at[out_at(q, h, p1, p2, 16)]
        return ring(4, q, buffer.at[at(q, h, p1, p2, 16)], target, peer(1 - h, 1 - 2 * d))

    def ag_two(q, h, d):
        p1, p2 = spot(h)
        step = 1 - 2 * d
        piece = out_hbm.at[out_at(q, h, p1, (p2 - step) % 4, 16), left if d == 0 else right]
        return ring(5, q, piece, piece, peer(1 - h, step))

    def ag_three(q, h, d):
        p1, _ = spot(h)
        piece = out_hbm.at[out_at(q, h, p1, 0, 64)]
        return ring(6, q, piece, piece, peer(h, 1 - 2 * d))

    def ag_four(q, h, d):
        p1, _ = spot(h)
        step = 1 - 2 * d
        piece = out_hbm.at[out_at(q, h, (p1 - step) % 4, 0, 64), left if d == 0 else right]
        return ring(7, q, piece, piece, peer(h, step))

    def last_copy(q, h, d):
        p1, _ = spot(h)
        piece = out_hbm.at[out_at(q, h, (p1 + d) % 4, 0, 64)]
        return remote(piece, piece, last_send, last_recv, sibling)

    def swapped(group):
        counts = ((3, 6), (3, 4))[group]
        pl.when(parity == 0)(lambda: arrived_rows(counts[0] * ROWS, swap_recv.at[group]))
        pl.when(parity == 1)(lambda: arrived_rows(counts[1] * ROWS, swap_recv.at[group]))

    def multiply(q):
        k = chunk(q)
        feed_down = (parity == 1) & (k < 4)
        from_context = (parity == 0) & (k == 7)
        a = jnp.where(feed_down, 2 + k, jnp.where(from_context, 1, 0))
        b = jnp.where(feed_down, 1, jnp.where(from_context, 2, 2 + k))
        pl.when(q == 0)(lambda: swapped(0))
        pl.when(q == 1 + 3 * parity)(lambda: swapped(1))
        right_own, right_other = ops[b].reshape(ROWS, WIDTH), other[b].reshape(ROWS, WIDTH)
        for cut in range(2):
            columns = pl.ds(pl.multiple_of(core * 512 + cut * 256, 256), 256)
            product = dot_tn(ops[a, :, :, columns].reshape(ROWS, 256), right_own)
            product = product + dot_tn(other[a, :, :, columns].reshape(ROWS, 256), right_other)
            buffer[pl.ds(pl.multiple_of(k * 1024 + core * 512 + cut * 256, 256), 256), :] = product.astype(BF16)

    def stage_0(q):
        pl.when(multiplies(q))(lambda: multiply(q))
        pl.when(exported(q))(lambda: export_copy().start())
        pl.when(imported(q))(lambda: export_copy().wait_recv())

        @pl.when(reduces(q))
        def _():
            pl.when(q == jnp.where(sends_out, 1, 0))(lambda: pl.semaphore_wait(ready, 4))
            for h, d in both:
                rs_one(q, h, d).start()

    def stage_2(q):
        arrived_rows(128, ring_recv.at[0, q])
        for h, d in both:
            p1, _ = spot(h)
            rows = at(q, h, (p1 + 1 - 2 * d) % 4, 0, 64)
            cut = left if d == 0 else right
            buffer[rows, cut] = buffer[rows, cut] + land_one(q, h, d)[...]
            rs_two(q, h, d).start()

    def stage_3(q):
        arrived_rows(256, ring_recv.at[1, q])
        for h in (0, 1):
            p1, _ = spot(h)
            rows = at(q, h, p1, 0, 64)
            total = buffer[rows, :].astype(F32) + land_two(q, h, 0)[...].astype(F32) + land_two(q, h, 1)[...].astype(F32)
            buffer[rows, :] = total.astype(BF16)
            for d in (0, 1):
                rs_three(q, h, d).start()

    def stage_4(q):
        arrived_rows(32, ring_recv.at[2, q])
        for h, d in both:
            p1, p2 = spot(h)
            rows = at(q, h, p1, (p2 + 1 - 2 * d) % 4, 16)
            cut = left if d == 0 else right
            buffer[rows, cut] = buffer[rows, cut] + land_three(q, h, d)[...]
            rs_four(q, h, d).start()

    def stage_5(q):
        @pl.when(reduces(q))
        def _():
            arrived_rows(64, ring_recv.at[3, q])
            for h in (0, 1):
                p1, p2 = spot(h)
                rows = at(q, h, p1, p2, 16)
                arrival = land_four(q, h, 0)[...].astype(F32) + land_four(q, h, 1)[...].astype(F32)
                buffer[rows, :] = (buffer[rows, :].astype(F32) + arrival).astype(BF16)

        @pl.when(hands_over(q))
        def _():
            for h in (0, 1):
                z_copy(q, h).start()

        @pl.when(takes_over(q))
        def _():
            for h in (0, 1):
                p1, p2 = spot(h)
                z_arrival(q, h).wait_recv()
                buffer[at(q, h, p1, p2, 16), :] = z[chunk(q), h]

        @pl.when(gathers(q))
        def _():
            for h in (0, 1):
                own_copy(q, h).start()
                for d in (0, 1):
                    ag_one(q, h, d).start()

    def stage_6(q):
        arrived_rows(64, ring_recv.at[4, q])
        for h, d in both:
            ag_two(q, h, d).start()
        arrived_rows(32, own_sem.at[q])

    def stage_7(q):
        arrived_rows(32, ring_recv.at[5, q])
        for h, d in both:
            ag_three(q, h, d).start()
        for h in (0, 1):
            last_copy(q, h, 0).start()

    def stage_8(q):
        arrived_rows(256, ring_recv.at[6, q])
        for h, d in both:
            ag_four(q, h, d).start()
        for h in (0, 1):
            last_copy(q, h, 1).start()
            last_copy(q, h, 3).start()

    def stage_9(q):
        arrived_rows(128, ring_recv.at[7, q])
        for h in (0, 1):
            last_copy(q, h, 2).start()

    stages = [stage_0, None, stage_2, stage_3, stage_4, stage_5, stage_6, stage_7, stage_8, stage_9]

    def tiny(phase, d):
        if phase == 0:
            return remote(small, sx.at[d - 1], tiny_send.at[d - 1], tiny_recv.at[d - 1], peer(0, d))
        if phase == 1:
            return remote(sums.at[0], sy.at[d - 1], tiny_send.at[d + 2], tiny_recv.at[d + 2], peer(1, d))
        if phase == 2:
            return remote(sums.at[1], ss, tiny_send.at[6], tiny_recv.at[6], sibling)
        return remote(
            sums.at[2], small_hbm.at[section], tiny_send.at[6 + d], tiny_recv.at[6 + d],
            device((section + d) % 4, x, y, core),
        )

    keep_own = [
        pltpu.make_async_copy(sums.at[2], small_hbm.at[section], tiny_send.at[10]),
        pltpu.make_async_copy(sums.at[2], small_hbm.at[SECTIONS], tiny_send.at[11]),
    ]

    def tiny_0():
        for d in (1, 2, 3):
            tiny(0, d).start()

    def tiny_1():
        for d in (1, 2, 3):
            tiny(0, d).wait()
        sums[0] = (small[...] + sx[0]) + (sx[1] + sx[2])
        for d in (1, 2, 3):
            tiny(1, d).start()

    def tiny_2():
        for d in (1, 2, 3):
            tiny(1, d).wait()
        sums[1] = (sums[0] + sy[0]) + (sy[1] + sy[2])
        tiny(2, 1).start()

    def tiny_3():
        tiny(2, 1).wait()
        sums[2] = sums[1] + ss[...]
        for copy in keep_own:
            copy.start()
        for d in (1, 2, 3):
            tiny(3, d).start()

    pl.when(parity == 1)(lambda: arrived_rows(1984, ag_send))
    for axis in (0, 1):
        for d in (1, 3):
            pl.semaphore_signal(ready, inc=1, device_id=peer(axis, d), device_id_type=MESH)

    def slot(t, carry):
        pl.when((t >= 3) & (t < 3 + SLOTS))(lambda: row_sums(t - 3))
        for number, turn in enumerate((tiny_0, tiny_1, tiny_2, tiny_3)):
            pl.when(t == 3 + SLOTS + number)(turn)
        for s in ORDER:
            k = t - jnp.where(parity == 1, OFFSET_FEED[s], OFFSET_ATTEND[s])
            live = (k >= 0) & (k < CHUNKS)
            if s == 0:
                live = live & (multiplies(k) | imported(k))
            elif s < 5:
                live = live & reduces(k)
            elif s == 5:
                live = live & (reduces(k) | gathers(k))
            else:
                live = live & gathers(k)
            pl.when(live)(lambda turn=stages[s], k=k: turn(k))
        return carry

    lax.fori_loop(0, CHUNKS + max(OFFSET_FEED + OFFSET_ATTEND), slot, 0)

    for d in (1, 2, 3):
        tiny(3, d).wait()
    for copy in keep_own:
        copy.wait()

    def sent(rows, sem):
        arrived_rows(rows, sem)

    pl.when(parity == 1)(lambda: sent(10 * ROWS, swap_send))
    pl.when(parity == 0)(lambda: sent(6 * ROWS, swap_send))
    pl.when(parity == 0)(lambda: sent(64, down_send))
    for number, (ring_count, z_count) in enumerate(((4, 0), (7, 1), (5, 1), (8, 2))):
        @pl.when(section == number)
        def _():
            sent(ring_count * 480, ring_send.at[0])
            if z_count:
                sent(z_count * 32, z_send)

    pl.when(sends_out)(lambda: export_copy().wait_send())
    sent(6 * 480, ring_send.at[1])
    sent(6 * 512, last_send)
    sent(6 * 512, last_recv)

    @pl.when(jnp.logical_not(first))
    def _():
        for micro in range(SLOTS):
            bwd_copy(micro).wait_send()
            ig_copy(micro, 1).wait_recv()

    @pl.when(first)
    def _():
        for micro in range(SLOTS):
            ig_own(micro).wait()
            for d in (1, 2, 3):
                ig_copy(micro, d).wait_send()


def mega(block, cot, group_ids, live_count, group_scale, gains, shifts, qv_bias, up_bias, out_bias, w1, down):
    any_space = pl.BlockSpec(memory_space=pl.ANY)
    dma = pltpu.SemaphoreType.DMA
    return pl.pallas_call(
        mega_kernel,
        name="mega",
        out_shape=[
            jax.ShapeDtypeStruct((6 * 1024, WIDTH), BF16),
            jax.ShapeDtypeStruct((SECTIONS + 1, 16, WIDTH), F32),
            jax.ShapeDtypeStruct((SLOTS, LEN, 256), BF16),
        ],
        in_specs=[any_space] * 12,
        out_specs=[any_space, any_space, any_space],
        scratch_shapes=[
            pltpu.SMEM((SLOTS,), jnp.int32),
            pltpu.SMEM((1,), jnp.int32),
            pltpu.SMEM((8,), F32),
            pltpu.VMEM((1, 2, WIDTH), F32),
            pltpu.VMEM((1, 2, WIDTH), F32),
            pltpu.VMEM((2, 2, WIDTH), F32),
            pltpu.VMEM((2, FF), F32),
            pltpu.VMEM((1, WIDTH), F32),
            pltpu.VMEM((WIDTH, FF), BF16),
            pltpu.VMEM((2 * FF, WIDTH), BF16),
            pltpu.VMEM((WIDTH, FF), BF16),
            pltpu.VMEM((10, SLOTS, LEN, WIDTH), BF16),
            pltpu.VMEM((10, SLOTS, LEN, WIDTH), BF16),
            pltpu.VMEM((SLOTS, LEN, WIDTH), BF16),
            pltpu.VMEM((SLOTS, LEN, 3), F32),
            pltpu.VMEM((SLOTS, LEN, WIDTH), BF16),
            pltpu.VMEM((SLOTS, LEN, WIDTH), BF16),
            pltpu.VMEM((SLOTS, LEN, WIDTH), BF16),
            pltpu.VMEM((SLOTS, LEN, WIDTH), BF16),
            pltpu.VMEM((LEN, WIDTH), F32),
            pltpu.VMEM((16, WIDTH), F32),
            pltpu.VMEM((16, WIDTH), F32),
            pltpu.VMEM((2, 2, 16, WIDTH), BF16),
            pltpu.VMEM((3, 16, WIDTH), F32),
            pltpu.VMEM((3, 16, WIDTH), F32),
            pltpu.VMEM((16, WIDTH), F32),
            pltpu.VMEM((3, 16, WIDTH), F32),
            dma((12,)), dma, dma((2,)), dma, dma((4, 2)),
            dma((SLOTS,)), dma((SLOTS,)), dma((SLOTS,)), dma((SLOTS,)),
            dma((SLOTS, 4)), dma((SLOTS,)), pltpu.SemaphoreType.REGULAR,
            dma, dma((2,)), pltpu.SemaphoreType.REGULAR,
            dma((2,)), dma((8, CHUNKS)), dma, dma((2, 2)), dma, dma, dma((CHUNKS,)), dma, dma,
            dma((12,)), dma((12,)),
        ],
        compiler_params=pltpu.CompilerParams(
            collective_id=0, has_side_effects=True, vmem_limit_bytes=63 * 2**20
        ),
    )(block, cot, group_ids, live_count, group_scale, gains, shifts, qv_bias, up_bias, out_bias, w1, down)


def widen_kernel(
    reduced, sums_hbm, grad_in,
    first_out, down_out, qv_out, up_out, bias_out, gain_out, shift_out, grad_out,
    narrow, wide, sums, qv, up, bias, gain, shift, in_sem, out_sem, small_sem,
):
    rows, depth = wide.shape[1], wide.shape[0]
    count = 6 * 1024 // rows

    def load(i):
        return pltpu.make_async_copy(reduced.at[pl.ds(i * rows, rows)], narrow.at[i % depth], in_sem.at[i % depth])

    def store(i):
        chunk, cut = i * rows // 1024, pl.ds(i * rows % 1024, rows)
        if chunk < 2:
            target = down_out.at[pl.ds(i * rows, rows)]
        else:
            target = first_out.at[0, cut, pl.ds((chunk - 2) * 1024, 1024)]
        return pltpu.make_async_copy(wide.at[i % depth], target, out_sem.at[i % depth])

    for i in range(depth):
        load(i).start()
    load_sums = pltpu.make_async_copy(sums_hbm, sums, small_sem.at[0])
    load_sums.start()
    move_grad = pltpu.make_async_copy(grad_in, grad_out, small_sem.at[1])
    move_grad.start()
    small = [(qv, qv_out), (up, up_out), (bias, bias_out), (gain, gain_out), (shift, shift_out)]
    small = [pltpu.make_async_copy(*piece, small_sem.at[2 + j]) for j, piece in enumerate(small)]
    for i in range(count):
        load(i).wait()
        if i >= depth:
            store(i - depth).wait()
        wide[i % depth] = narrow[i % depth].astype(F32)
        store(i).start()
        if i + depth < count:
            load(i + depth).start()
        if i == 2:
            load_sums.wait()
            for layer in (0, 1):
                qv[layer, 0:1, :] = sums[2 * layer, 5:6, :]
                qv[layer, 1:2, :] = sums[2 * layer, 7:8, :]
                for j in range(4):
                    up[layer : layer + 1, j * WIDTH : (j + 1) * WIDTH] = sums[2 * layer + 1, 5 + j : 6 + j, :]
            bias[...] = sums[SECTIONS, 4:5, :]
            gain[0] = sums[SECTIONS, 0:2, :]
            shift[0] = sums[SECTIONS, 2:4, :]
            for copy in small:
                copy.start()
    for i in range(count - depth, count):
        store(i).wait()
    for copy in small:
        copy.wait()
    move_grad.wait()


def widen(reduced, sums, grad):
    any_space = pl.BlockSpec(memory_space=pl.ANY)
    rows, depth = 1024, 3
    dma = pltpu.SemaphoreType.DMA
    shapes = [(2, 2, WIDTH), (2, FF), (1, WIDTH), (1, 2, WIDTH), (1, 2, WIDTH)]
    return pl.pallas_call(
        widen_kernel,
        name="widen",
        out_shape=[
            jax.ShapeDtypeStruct((1, WIDTH, FF), F32),
            jax.ShapeDtypeStruct((2 * WIDTH, WIDTH), F32),
            *[jax.ShapeDtypeStruct(shape, F32) for shape in shapes],
            jax.ShapeDtypeStruct((SLOTS, LEN, 256), BF16),
        ],
        in_specs=[any_space] * 3,
        out_specs=[any_space] * 8,
        scratch_shapes=[
            pltpu.VMEM((depth, rows, WIDTH), BF16),
            pltpu.VMEM((depth, rows, WIDTH), F32),
            pltpu.VMEM((SECTIONS + 1, 16, WIDTH), F32),
            *[pltpu.VMEM(shape, F32) for shape in shapes],
            dma((depth,)), dma((depth,)), dma((7,)),
        ],
        compiler_params=pltpu.CompilerParams(vmem_limit_bytes=63 * 2**20),
    )(reduced, sums, grad)


def on_device(
    block_input, cotangent, group_ids, live_count, group_scale, norm_gain, norm_bias, first_weight,
    qv_bias, up_bias, down_weight, out_bias,
):
    reduced, sums, grad = mega(
        block_input, cotangent, group_ids, live_count, group_scale, norm_gain, norm_bias,
        qv_bias, up_bias, out_bias, first_weight, down_weight,
    )
    first_grad, down_grad, qv_grad, up_grad, bias_grad, gain_grad, shift_grad, input_grad = widen(reduced, sums, grad)
    return input_grad, first_grad, down_grad, qv_grad, up_grad, bias_grad, gain_grad, shift_grad


def solution(mesh):
    in_specs = (
        P("dp", None, None),
        P("dp", None, None),
        P("dp"),
        P("dp"),
        P(),
        P("section", None, None),
        P("section", None, None),
        P("section", None, None),
        P(),
        P(),
        P("section", None),
        P("section", None),
    )
    out_specs = (
        P("dp", None, "section"),
        P("section", None, None),
        P("section", None),
        P(),
        P(),
        P("section", None),
        P("section", None, None),
        P("section", None, None),
    )
    return jax.shard_map(on_device, mesh=mesh, in_specs=in_specs, out_specs=out_specs, check_vma=False)
```

```python
import math

import jax
import jax.numpy as jnp
from jax import lax
from jax.experimental import pallas as pl
from jax.experimental.pallas import tpu as pltpu
from jax.sharding import PartitionSpec as P

MESH = pl.DeviceIdType.MESH
BF16 = jnp.bfloat16
F32 = jnp.float32

WIDTH = 1024
FF = 4096
LEN = 128
SLOTS = 4
ROWS = SLOTS * LEN
PAIRS = 8
SECTIONS = 4
NORM_EPS = 1e-05
GELU_C = math.sqrt(2.0 / math.pi)
CHUNKS = 8
ORDER = (7, 0, 3, 8, 4, 5, 6, 2, 9)
OFFSET_FEED = (0, 0, 1, 3, 4, 5, 6, 8, 10, 12)
OFFSET_ATTEND = (0, 0, 1, 3, 4, 5, 6, 8, 11, 14)


def device(section, x, y, core):
    return (section, x * 8 + y * 2 + core)


def place():
    at = lax.axis_index("dp")
    return lax.axis_index("section"), at // 8, (at // 2) % 4, at % 2


def greet(section, x, y, core, here):
    barrier = pltpu.get_barrier_semaphore()
    others = [device(section, x, y, 1 - core), device(section + 1 - 2 * (section % 2), x, y, core)]
    for d in (1, 2, 3):
        others.append(device(section, (x + d) % 4, y, core))
        others.append(device(section, x, (y + d) % 4, core))
    for other in others:
        pl.semaphore_signal(barrier, inc=1, device_id=other, device_id_type=MESH)

    @pl.when(section < 2)
    def _():
        for high in (2, 3):
            pl.semaphore_signal(barrier, inc=1, device_id=device(high, x, y, core), device_id_type=MESH)

    pl.semaphore_wait(barrier, jnp.where(section < 2, 8, 10))

    @pl.when(section >= 2)
    def _():
        for low in (0, 1):
            pl.semaphore_signal(here, inc=1, device_id=device(low, x, y, core), device_id_type=MESH)


def remote(source, target, send_sem, recv_sem, to):
    return pltpu.make_async_remote_copy(
        src_ref=source,
        dst_ref=target,
        send_sem=send_sem,
        recv_sem=recv_sem,
        device_id=to,
        device_id_type=MESH,
    )


def dot(a, b):
    return jnp.dot(a, b, preferred_element_type=F32)


def dot_nt(a, b):
    return lax.dot_general(a, b, (((1,), (1,)), ((), ())), preferred_element_type=F32)


def dot_tn(a, b):
    return lax.dot_general(a, b, (((0,), (0,)), ((), ())), preferred_element_type=F32)


def normalize(entries):
    average = jnp.mean(entries, axis=-1, keepdims=True)
    centered = entries - average
    inverse = lax.rsqrt(jnp.mean(centered * centered, axis=-1, keepdims=True) + NORM_EPS)
    return centered * inverse, inverse


def norm_backward(grad_out, unit, inverse, gain):
    scaled = grad_out * gain
    middle = jnp.mean(scaled, axis=-1, keepdims=True)
    along = jnp.mean(scaled * unit, axis=-1, keepdims=True)
    return inverse * (scaled - middle - unit * along)


def column_sum(entries):
    return jnp.sum(entries, axis=0, keepdims=True)


def mega_kernel(
    block_hbm, cot_hbm, group_hbm, live_hbm, scale_hbm, gains_hbm, shifts_hbm, qv_hbm, up_hbm, bias_hbm, w1_hbm, down_hbm,
    out_hbm, small_hbm, grad_hbm,
    group_ids, live_count, group_scale, gains, shifts, qv_bias, up_bias, out_bias,
    w1, buffer, w2t, ops, other, units, stats, r_in, r_out, g_in, g_out, wide, small, vectors,
    z, sx, sy, ss, sums,
    load_sem, down_send, down_recv, ag_send, ag_recv,
    fwd_send, fwd_recv, bwd_send, bwd_recv, ig_send, ig_recv, token, here,
    swap_send, swap_recv, ready, ring_send, ring_recv, z_send, z_recv, export_send, export_recv, own_sem, last_send, last_recv,
    tiny_send, tiny_recv,
):
    section, x, y, core = place()
    parity = section % 2
    layer = section // 2
    last = section == SECTIONS - 1
    first = section == 0
    sibling = device(section, x, y, 1 - core)
    w1t, w2 = buffer.at[pl.ds(0, FF)], buffer.at[pl.ds(FF, FF)]

    load_w1 = pltpu.make_async_copy(w1_hbm.at[0], w1, load_sem.at[0])
    load_own = pltpu.make_async_copy(down_hbm, w2.at[pl.ds(2048, 2048)], load_sem.at[1])
    load_block = pltpu.make_async_copy(block_hbm, r_in, load_sem.at[2])
    load_cot = pltpu.make_async_copy(cot_hbm, g_in, load_sem.at[3])

    pieces = [
        (gains_hbm, gains), (shifts_hbm, shifts), (bias_hbm, out_bias), (qv_hbm, qv_bias), (up_hbm, up_bias),
        (group_hbm, group_ids), (live_hbm, live_count), (scale_hbm, group_scale),
    ]
    load_pieces = [pltpu.make_async_copy(*piece, load_sem.at[4 + j]) for j, piece in enumerate(pieces)]

    @pl.when(first)
    def _():
        load_block.start()

    for copy in load_pieces:
        copy.start()
    load_w1.start()

    @pl.when(parity == 1)
    def _():
        load_own.start()

    @pl.when(last)
    def _():
        load_cot.start()

    greet(section, x, y, core, here)

    left, right = pl.ds(0, 512), pl.ds(512, 512)
    both = [(h, d) for h in (0, 1) for d in (0, 1)]

    def peer(axis, d):
        if axis == 0:
            return device(section, (x + d) % 4, y, core)
        return device(section, x, (y + d) % 4, core)

    def arrived_rows(rows, sem):
        piece = buffer.at[pl.ds(0, rows)]
        pltpu.make_async_copy(piece, piece, sem).wait()

    def down_rows(h, p, major, minor, n):
        row = h * 1024 + core * 512 + p * 256 + major * 64 + minor * 16
        return pl.ds(pl.multiple_of(row, 16), n)

    def down_spot(h):
        return (y, x) if h == 0 else (x, y)

    def down_copy(p, h):
        rows = down_rows(h, p, *down_spot(h), 16)
        return remote(
            down_hbm.at[rows], w2.at[rows], down_send, down_recv.at[p], device((section + 1) % 4, x, y, core)
        )

    def down_near(p, h, d):
        rows = down_rows(h, p, *down_spot(h), 16)
        return remote(w2.at[rows], w2.at[rows], ag_send, ag_recv.at[0, p], peer(h, d))

    def down_ring(p, h, d):
        rows = down_rows(h, p, down_spot(h)[0], 0, 64)
        return remote(w2.at[rows], w2.at[rows], ag_send, ag_recv.at[1, p], peer(1 - h, 1 - 2 * d))

    def down_pass(p, h, d):
        step = 1 - 2 * d
        rows = down_rows(h, p, (down_spot(h)[0] - step) % 4, 0, 64)
        piece = w2.at[rows, left if d == 0 else right]
        return remote(piece, piece, ag_send, ag_recv.at[2, p], peer(1 - h, step))

    def down_share(p, h, d):
        rows = down_rows(h, p, (down_spot(h)[0] + d) % 4, 0, 64)
        return remote(w2.at[rows], w2.at[rows], ag_send, ag_recv.at[3, 0], sibling)

    @pl.when(parity == 0)
    def _():
        for p in (0, 1):
            for h in (0, 1):
                down_copy(p, h).start()

    for copy in load_pieces:
        copy.wait()

    @pl.when(parity == 0)
    def _():
        vectors[5:6, :] = qv_bias[layer, 0:1, :]
        vectors[6:7, :] = jnp.zeros((1, WIDTH), F32)
        vectors[7:8, :] = qv_bias[layer, 1:2, :]

    @pl.when(parity == 1)
    def _():
        for j in range(4):
            vectors[5 + j : 6 + j, :] = up_bias[pl.ds(layer, 1), j * WIDTH : (j + 1) * WIDTH]

    def sequence_weight(micro):
        group = group_ids[micro]
        chosen = jnp.float32(0.0)
        for label in range(8):
            chosen = jnp.where(group == label, group_scale[label], chosen)
        weight = jnp.where(micro < live_count[0], chosen, 0.0)
        return jnp.where(last, weight, 1.0)

    small[...] = jnp.zeros_like(small)

    def gather_start():
        for p in (0, 1):
            arrived_rows(32, down_recv.at[p])
            for h in (0, 1):
                for d in (1, 3, 2):
                    down_near(p, h, d).start()
        for p in (0, 1):
            arrived_rows(96, ag_recv.at[0, p])
            for h, d in both:
                down_ring(p, h, d).start()
            for h in (0, 1):
                down_share(p, h, 0).start()
        gather_pass(0)
        gather_pass(1)
        load_own.wait()

    def gather_pass(p):
        arrived_rows(256, ag_recv.at[1, p])
        for h, d in both:
            down_pass(p, h, d).start()
        for h in (0, 1):
            down_share(p, h, 1).start()
            down_share(p, h, 3).start()

    def gather_end():
        for p in (0, 1):
            arrived_rows(128, ag_recv.at[2, p])
            for h in (0, 1):
                down_share(p, h, 2).start()
        arrived_rows(1024, ag_recv.at[3, 0])

    pl.when(parity == 1)(gather_start)
    pl.when(last)(gather_end)

    load_w1.wait()

    @pl.when(first)
    def _():
        load_block.wait()

    @pl.when(last)
    def _():
        load_cot.wait()

    def fwd_copy(micro):
        return remote(
            r_out.at[micro], r_in.at[micro], fwd_send.at[micro], fwd_recv.at[micro],
            device((section + 1) % 4, x, y, core),
        )

    def bwd_copy(micro):
        return remote(
            g_out.at[micro], g_in.at[micro], bwd_send.at[micro], bwd_recv.at[micro],
            device((section + 3) % 4, x, y, core),
        )

    def ig_copy(micro, d):
        to = (section + d) % 4
        return remote(
            g_out.at[micro, :, pl.ds(d * 256, 256)], grad_hbm.at[micro], ig_send.at[micro, d], ig_recv.at[micro],
            device(to, x, y, core),
        )

    def ig_own(micro):
        return pltpu.make_async_copy(g_out.at[micro, :, pl.ds(0, 256)], grad_hbm.at[micro], ig_send.at[micro, 0])

    lanes = lax.broadcasted_iota(jnp.int32, (LEN, 128), 1)
    low_lanes = lanes < 64

    def two_heads(entries):
        zero = jnp.zeros_like(entries)
        return jnp.concatenate([jnp.where(low_lanes, entries, zero), jnp.where(low_lanes, zero, entries)], axis=0)

    def transposes():
        def one(j, carry):
            cut = pl.ds(pl.multiple_of(j * 256, 256), 256)
            w1t[cut, :] = w1[:, cut].T
            return carry

        lax.fori_loop(0, 16, one, 0)

        @pl.when(parity == 1)
        def _():
            def two(j, carry):
                cut = pl.ds(pl.multiple_of(j * 256, 256), 256)
                w2t[:, cut] = w2[cut, :].T
                return carry

            lax.fori_loop(0, 16, two, 0)

    def attention_forward(micro):
        normed = ops[0, micro]
        for j in range(3):
            part = dot(normed, w1[:, j * WIDTH : (j + 1) * WIDTH]) + vectors[5 + j : 6 + j, :]
            ops[6 + j, micro] = part.astype(BF16)
        rows = lax.broadcasted_iota(jnp.int32, (LEN, LEN), 0)
        columns = lax.broadcasted_iota(jnp.int32, (LEN, LEN), 1)
        causal = rows <= columns
        for p in range(PAIRS):
            cut = slice(p * 128, (p + 1) * 128)
            query, key, value = (ops[6 + j, micro, :, cut] for j in range(3))
            scores = dot_nt(two_heads(key), query) * 0.125
            parts = []
            for head in (0, 1):
                part = jnp.where(causal, scores[head * LEN : (head + 1) * LEN], -1e9)
                powers = jnp.exp(part - jnp.max(part, axis=0, keepdims=True))
                part = (powers / jnp.sum(powers, axis=0, keepdims=True)).astype(BF16)
                ops[3 + p // 4, micro, :, (p % 4 * 2 + head) * 128 : (p % 4 * 2 + head + 1) * 128] = part
                parts.append(part)
            ops[2, micro, :, cut] = dot_tn(jnp.concatenate(parts, axis=0), two_heads(value)).astype(BF16)
        wide[...] = dot_nt(ops[2, micro], w1[:, 3 * WIDTH :]) + out_bias[...]

    def feed_forward(micro):
        normed = ops[0, micro]
        branch = out_bias[...]
        def product(j):
            b, cut = j * 256 // WIDTH, slice(j * 256 % WIDTH, j * 256 % WIDTH + 256)
            return dot(normed, w1[:, j * 256 : (j + 1) * 256]) + vectors[5 + b : 6 + b, cut]

        def gate(j, hidden):
            b, cut = j * 256 // WIDTH, slice(j * 256 % WIDTH, j * 256 % WIDTH + 256)
            square = hidden * hidden
            above = 0.5 + 0.5 * jnp.tanh(hidden * (GELU_C + (GELU_C * 0.044715) * square))
            active = hidden * above
            slope = above + (active - active * above) * (2.0 * GELU_C + (6.0 * GELU_C * 0.044715) * square)
            ops[6 + b, micro, :, cut] = slope.astype(BF16)
            ops[2 + b, micro, :, cut] = active.astype(BF16)

        order = (8, 9, 10, 11, 12, 13, 14, 15, 0, 1, 2, 3, 4, 5, 6, 7)
        hidden = product(order[0])
        for step, j in enumerate(order):
            ahead = product(order[step + 1]) if step + 1 < len(order) else None
            gate(j, hidden)
            hidden = ahead
        branch = out_bias[...]
        for j in (2, 3, 0, 1):
            if j == 0:
                pl.when((micro == 0) & (section == 1))(gather_end)
            branch = branch + dot(ops[2 + j, micro], w2[j * WIDTH : (j + 1) * WIDTH, :])
        wide[...] = branch

    def attention_backward(micro):
        ops[9, micro] = dot(ops[1, micro], w1[:, 3 * WIDTH :]).astype(BF16)
        for p in range(PAIRS):
            cut = slice(p * 128, (p + 1) * 128)
            query, key, value = (ops[6 + j, micro, :, cut] for j in range(3))
            grad = ops[9, micro, :, cut]
            parts = [ops[3 + p // 4, micro, :, (p % 4 * 2 + h) * 128 : (p % 4 * 2 + h + 1) * 128] for h in (0, 1)]
            grad_weights = dot_nt(two_heads(value), grad)
            grad_scores = []
            for head in (0, 1):
                part = parts[head].astype(F32)
                product = part * grad_weights[head * LEN : (head + 1) * LEN]
                grad_scores.append((product - part * jnp.sum(product, axis=0, keepdims=True)).astype(BF16))
            grad_scores = jnp.concatenate(grad_scores, axis=0)
            grad_query = dot_tn(grad_scores, two_heads(key)) * 0.125
            both_heads = dot(grad_scores, query) * 0.125
            grad_key = jnp.where(low_lanes, both_heads[:LEN], both_heads[LEN:])
            both_heads = dot(jnp.concatenate(parts, axis=0), grad)
            grad_value = jnp.where(low_lanes, both_heads[:LEN], both_heads[LEN:])
            for j, part in enumerate((grad_query, grad_key, grad_value)):
                ops[6 + j, micro, :, cut] = part.astype(BF16)
        total = jnp.zeros((LEN, WIDTH), F32)
        for j in range(3):
            part = ops[6 + j, micro]
            total = total + dot(part, w1t[j * WIDTH : (j + 1) * WIDTH, :])
        wide[...] = total

    def feed_backward(micro):
        grad_branch = ops[1, micro]
        total = jnp.zeros((LEN, WIDTH), F32)
        for j in range(4):
            grad = dot(grad_branch, w2t[:, j * WIDTH : (j + 1) * WIDTH])
            grad = (grad * ops[6 + j, micro].astype(F32)).astype(BF16)
            ops[6 + j, micro] = grad
            total = total + dot(grad, w1t[j * WIDTH : (j + 1) * WIDTH, :])
        wide[...] = total

    def swap(block, count, micro, group):
        piece = pl.ds(block, count)
        return remote(ops.at[piece, micro], other.at[piece, micro], swap_send, swap_recv.at[group], sibling)

    def forward(micro):
        @pl.when(jnp.logical_not(first))
        def _():
            fwd_copy(micro).wait_recv()

        residual = r_in[micro].astype(F32)
        mean = jnp.mean(residual, axis=-1, keepdims=True)
        centered = residual - mean
        inverse = lax.rsqrt(jnp.mean(centered * centered, axis=-1, keepdims=True) + NORM_EPS)
        stats[micro, :, 0:1] = mean
        stats[micro, :, 1:2] = inverse
        ops[0, micro] = (centered * inverse * gains[0, 0:1, :] + shifts[0, 0:1, :]).astype(BF16)
        swap(0, 1, micro, 0).start()

        @pl.when(parity == 0)
        def _():
            attention_forward(micro)

        @pl.when(parity == 1)
        def _():
            feed_forward(micro)

        unit, inverse = normalize(wide[...])

        @pl.when(jnp.logical_not(last))
        def _():
            after = r_in[micro].astype(F32) + unit * gains[0, 1:2, :] + shifts[0, 1:2, :]
            r_out[micro] = after.astype(BF16)
            leads = (section == 1) & (core == 1)
            follows = (section == 1) & (core == 0)
            pl.when(micro > jnp.where(leads, 1, 0))(lambda: fwd_copy(micro - 1).wait_send())
            pl.when((section < 2) & (micro == 0))(lambda: pl.semaphore_wait(here, 2))
            pl.when(follows & (micro == 0))(lambda: pl.semaphore_wait(token, 1))
            fwd_copy(micro).start()

            @pl.when(leads & (micro == 0))
            def _():
                fwd_copy(micro).wait_send()
                pl.semaphore_signal(token, inc=1, device_id=sibling, device_id_type=MESH)

        units[micro] = unit.astype(BF16)
        stats[micro, :, 2:3] = inverse
        pl.when(parity == 0)(lambda: swap(2, 1, micro, 0).start())
        pl.when(parity == 1)(lambda: swap(2, 4, micro, 0).start())

    def backward(micro):
        @pl.when(jnp.logical_not(last))
        def _():
            bwd_copy(micro).wait_recv()

        weight = sequence_weight(micro)
        incoming = g_in[micro].astype(F32) * weight
        unit = units[micro].astype(F32)
        ops[1, micro] = norm_backward(incoming, unit, stats[micro, :, 2:3], gains[0, 1:2, :]).astype(BF16)
        swap(1, 1, micro, 0).start()

        @pl.when(parity == 0)
        def _():
            attention_backward(micro)

        @pl.when(parity == 1)
        def _():
            feed_backward(micro)

        inverse = stats[micro, :, 1:2]
        unit = (r_in[micro].astype(F32) - stats[micro, :, 0:1]) * inverse
        incoming = g_in[micro].astype(F32) * weight
        grad = incoming + norm_backward(wide[...], unit, inverse, gains[0, 0:1, :])
        g_out[micro] = grad.astype(BF16)

        @pl.when(jnp.logical_not(first))
        def _():
            bwd_copy(micro).start()

        @pl.when(first)
        def _():
            ig_own(micro).start()
            for d in (1, 2, 3):
                ig_copy(micro, d).start()

        r_out[micro] = wide[...].astype(BF16)
        pl.when(parity == 0)(lambda: swap(6, 3, micro, 1).start())
        pl.when(parity == 1)(lambda: swap(6, 4, micro, 1).start())

    def row_sums(micro):
        weight = sequence_weight(micro)
        unit = (r_in[micro].astype(F32) - stats[micro, :, 0:1]) * stats[micro, :, 1:2]
        grad = r_out[micro].astype(F32)
        small[0:1, :] += column_sum(grad * unit)
        small[2:3, :] += column_sum(grad)
        incoming = g_in[micro].astype(F32) * weight
        small[1:2, :] += column_sum(incoming * units[micro].astype(F32))
        small[3:4, :] += column_sum(incoming)
        small[4:5, :] += column_sum(ops[1, micro].astype(F32))
        for j in range(4):
            small[5 + j : 6 + j, :] += column_sum(ops[6 + j, micro].astype(F32))

    turn_at = jnp.where(section >= 2, 0, SLOTS)

    def step(t, carry):
        is_forward = jnp.where(last, (t + 1) % 2, jnp.where(t < SLOTS, 1, 0))
        micro = jnp.where(last, t // 2, t % SLOTS)

        @pl.when((t == SLOTS) & jnp.logical_not(last))
        def _():
            fwd_copy(SLOTS - 1).wait_send()

        @pl.when(t == turn_at)
        def _():
            transposes()

        @pl.when(is_forward == 1)
        def _():
            forward(micro)

        @pl.when(is_forward == 0)
        def _():
            backward(micro)

        return carry

    lax.fori_loop(0, 2 * SLOTS, step, 0)

    def spot(h):
        return (x, y) if h == 0 else (y, x)

    sends_out = section == 1
    takes_in = section == 2

    def chunk(q):
        late = jnp.where(takes_in, jnp.where(q == 7, 2, q - 4), jnp.where(q == 4, 1, 0))
        return jnp.where(parity == 1, q, jnp.where(q < 4, 7 - q, late))

    def exported(q):
        return sends_out & (q == 0)

    def imported(q):
        return takes_in & (q == 7)

    def multiplies(q):
        return (parity == 1) | (q < 4)

    def reduces(q):
        return (multiplies(q) & jnp.logical_not(exported(q))) | imported(q)

    def hands_over(q):
        return ((section == 3) & (q < 2)) | (sends_out & (q == 1)) | imported(q)

    def takes_over(q):
        return ((section == 0) & ((q == 4) | (q == 6))) | (takes_in & ((q == 4) | (q == 5)))

    def gathers(q):
        return ((parity == 1) & (q >= 2)) | ((parity == 0) & (q < 4)) | takes_over(q)

    def at(q, h, b1, b2, n):
        row = chunk(q) * 1024 + core * 512 + h * 256 + b1 * 64 + b2 * 16
        return pl.ds(pl.multiple_of(row, 16), n)

    def export_copy():
        return remote(
            buffer.at[pl.ds(pl.multiple_of(core * 512, 512), 512)],
            buffer.at[pl.ds(pl.multiple_of(2048 + core * 512, 512), 512)],
            export_send, export_recv, device((section + 1) % 4, x, y, core),
        )

    def out_at(q, h, b1, b2, n):
        k = chunk(q)
        k = jnp.where((parity == 1) | (k >= 4), k - 2, k)
        row = k * 1024 + core * 512 + h * 256 + b1 * 64 + b2 * 16
        return pl.ds(pl.multiple_of(row, 16), n)

    def ring(stage, q, source, target, to):
        return remote(source, target, ring_send.at[stage // 4], ring_recv.at[stage, q], to)

    def land_one(q, h, d):
        return w1.at[pl.ds((q * 2 + h) * 64, 64), pl.ds(d * 512, 512)]

    def land_two(q, h, d):
        return w2t.at[pl.ds((q * 2 + h) * 64, 64), pl.ds(d * 1024, 1024)]

    def land_three(q, h, d):
        return w2t.at[pl.ds((q * 2 + h) * 64 + 16, 16), pl.ds(2048 + d * 1024, 512)]

    def land_four(q, h, d):
        return w2t.at[pl.ds((q * 2 + h) * 64, 16), pl.ds(2048 + d * 1024, 1024)]

    def rs_one(q, h, d):
        p1, _ = spot(h)
        rows = at(q, h, (p1 + 2) % 4, 0, 64)
        return ring(0, q, buffer.at[rows, left if d == 0 else right], land_one(q, h, d), peer(h, 1 - 2 * d))

    def rs_two(q, h, d):
        p1, _ = spot(h)
        step = 1 - 2 * d
        return ring(1, q, buffer.at[at(q, h, (p1 + step) % 4, 0, 64)], land_two(q, h, d), peer(h, step))

    def rs_three(q, h, d):
        p1, p2 = spot(h)
        rows = at(q, h, p1, (p2 + 2) % 4, 16)
        return ring(2, q, buffer.at[rows, left if d == 0 else right], land_three(q, h, d), peer(1 - h, 1 - 2 * d))

    def rs_four(q, h, d):
        p1, p2 = spot(h)
        step = 1 - 2 * d
        return ring(3, q, buffer.at[at(q, h, p1, (p2 + step) % 4, 16)], land_four(q, h, d), peer(1 - h, step))

    def z_copy(q, h):
        p1, p2 = spot(h)
        to = jnp.where(takes_in, 0, section - 1)
        slot = jnp.where(takes_in, 0, chunk(q))
        return remote(
            buffer.at[at(q, h, p1, p2, 16)], z.at[slot, h], z_send, z_recv.at[slot, h], device(to, x, y, core)
        )

    def z_arrival(q, h):
        return remote(z.at[chunk(q), h], z.at[chunk(q), h], z_send, z_recv.at[chunk(q), h], sibling)

    def own_copy(q, h):
        p1, p2 = spot(h)
        return pltpu.make_async_copy(
            buffer.at[at(q, h, p1, p2, 16)], out_hbm.at[out_at(q, h, p1, p2, 16)], own_sem.at[q]
        )

    def ag_one(q, h, d):
        p1, p2 = spot(h)
        target = out_hbm.at[out_at(q, h, p1, p2, 16)]
        return ring(4, q, buffer.at[at(q, h, p1, p2, 16)], target, peer(1 - h, 1 - 2 * d))

    def ag_two(q, h, d):
        p1, p2 = spot(h)
        step = 1 - 2 * d
        piece = out_hbm.at[out_at(q, h, p1, (p2 - step) % 4, 16), left if d == 0 else right]
        return ring(5, q, piece, piece, peer(1 - h, step))

    def ag_three(q, h, d):
        p1, _ = spot(h)
        piece = out_hbm.at[out_at(q, h, p1, 0, 64)]
        return ring(6, q, piece, piece, peer(h, 1 - 2 * d))

    def ag_four(q, h, d):
        p1, _ = spot(h)
        step = 1 - 2 * d
        piece = out_hbm.at[out_at(q, h, (p1 - step) % 4, 0, 64), left if d == 0 else right]
        return ring(7, q, piece, piece, peer(h, step))

    def last_copy(q, h, d):
        p1, _ = spot(h)
        piece = out_hbm.at[out_at(q, h, (p1 + d) % 4, 0, 64)]
        return remote(piece, piece, last_send, last_recv, sibling)

    def swapped(group):
        counts = ((3, 6), (3, 4))[group]
        pl.when(parity == 0)(lambda: arrived_rows(counts[0] * ROWS, swap_recv.at[group]))
        pl.when(parity == 1)(lambda: arrived_rows(counts[1] * ROWS, swap_recv.at[group]))

    def multiply(q):
        k = chunk(q)
        feed_down = (parity == 1) & (k < 4)
        from_context = (parity == 0) & (k == 7)
        a = jnp.where(feed_down, 2 + k, jnp.where(from_context, 1, 0))
        b = jnp.where(feed_down, 1, jnp.where(from_context, 2, 2 + k))
        pl.when(q == 0)(lambda: swapped(0))
        pl.when(q == 1 + 3 * parity)(lambda: swapped(1))
        right_own, right_other = ops[b].reshape(ROWS, WIDTH), other[b].reshape(ROWS, WIDTH)
        for cut in range(2):
            columns = pl.ds(pl.multiple_of(core * 512 + cut * 256, 256), 256)
            product = dot_tn(ops[a, :, :, columns].reshape(ROWS, 256), right_own)
            product = product + dot_tn(other[a, :, :, columns].reshape(ROWS, 256), right_other)
            buffer[pl.ds(pl.multiple_of(k * 1024 + core * 512 + cut * 256, 256), 256), :] = product.astype(BF16)

    def stage_0(q):
        pl.when(multiplies(q))(lambda: multiply(q))
        pl.when(exported(q))(lambda: export_copy().start())
        pl.when(imported(q))(lambda: export_copy().wait_recv())

        @pl.when(reduces(q))
        def _():
            pl.when(q == jnp.where(sends_out, 1, 0))(lambda: pl.semaphore_wait(ready, 4))
            for h, d in both:
                rs_one(q, h, d).start()

    def stage_2(q):
        arrived_rows(128, ring_recv.at[0, q])
        for h, d in both:
            p1, _ = spot(h)
            rows = at(q, h, (p1 + 1 - 2 * d) % 4, 0, 64)
            cut = left if d == 0 else right
            buffer[rows, cut] = buffer[rows, cut] + land_one(q, h, d)[...]
            rs_two(q, h, d).start()

    def stage_3(q):
        arrived_rows(256, ring_recv.at[1, q])
        for h in (0, 1):
            p1, _ = spot(h)
            rows = at(q, h, p1, 0, 64)
            total = buffer[rows, :].astype(F32) + land_two(q, h, 0)[...].astype(F32) + land_two(q, h, 1)[...].astype(F32)
            buffer[rows, :] = total.astype(BF16)
            for d in (0, 1):
                rs_three(q, h, d).start()

    def stage_4(q):
        arrived_rows(32, ring_recv.at[2, q])
        for h, d in both:
            p1, p2 = spot(h)
            rows = at(q, h, p1, (p2 + 1 - 2 * d) % 4, 16)
            cut = left if d == 0 else right
            buffer[rows, cut] = buffer[rows, cut] + land_three(q, h, d)[...]
            rs_four(q, h, d).start()

    def stage_5(q):
        @pl.when(reduces(q))
        def _():
            arrived_rows(64, ring_recv.at[3, q])
            for h in (0, 1):
                p1, p2 = spot(h)
                rows = at(q, h, p1, p2, 16)
                arrival = land_four(q, h, 0)[...].astype(F32) + land_four(q, h, 1)[...].astype(F32)
                buffer[rows, :] = (buffer[rows, :].astype(F32) + arrival).astype(BF16)

        @pl.when(hands_over(q))
        def _():
            for h in (0, 1):
                z_copy(q, h).start()

        @pl.when(takes_over(q))
        def _():
            for h in (0, 1):
                p1, p2 = spot(h)
                z_arrival(q, h).wait_recv()
                buffer[at(q, h, p1, p2, 16), :] = z[chunk(q), h]

        @pl.when(gathers(q))
        def _():
            for h in (0, 1):
                own_copy(q, h).start()
                for d in (0, 1):
                    ag_one(q, h, d).start()

    def stage_6(q):
        arrived_rows(64, ring_recv.at[4, q])
        for h, d in both:
            ag_two(q, h, d).start()
        arrived_rows(32, own_sem.at[q])

    def stage_7(q):
        arrived_rows(32, ring_recv.at[5, q])
        for h, d in both:
            ag_three(q, h, d).start()
        for h in (0, 1):
            last_copy(q, h, 0).start()

    def stage_8(q):
        arrived_rows(256, ring_recv.at[6, q])
        for h, d in both:
            ag_four(q, h, d).start()
        for h in (0, 1):
            last_copy(q, h, 1).start()
            last_copy(q, h, 3).start()

    def stage_9(q):
        arrived_rows(128, ring_recv.at[7, q])
        for h in (0, 1):
            last_copy(q, h, 2).start()

    stages = [stage_0, None, stage_2, stage_3, stage_4, stage_5, stage_6, stage_7, stage_8, stage_9]

    def tiny(phase, d):
        if phase == 0:
            return remote(small, sx.at[d - 1], tiny_send.at[d - 1], tiny_recv.at[d - 1], peer(0, d))
        if phase == 1:
            return remote(sums.at[0], sy.at[d - 1], tiny_send.at[d + 2], tiny_recv.at[d + 2], peer(1, d))
        if phase == 2:
            return remote(sums.at[1], ss, tiny_send.at[6], tiny_recv.at[6], sibling)
        return remote(
            sums.at[2], small_hbm.at[section], tiny_send.at[6 + d], tiny_recv.at[6 + d],
            device((section + d) % 4, x, y, core),
        )

    keep_own = [
        pltpu.make_async_copy(sums.at[2], small_hbm.at[section], tiny_send.at[10]),
        pltpu.make_async_copy(sums.at[2], small_hbm.at[SECTIONS], tiny_send.at[11]),
    ]

    def tiny_0():
        for d in (1, 2, 3):
            tiny(0, d).start()

    def tiny_1():
        for d in (1, 2, 3):
            tiny(0, d).wait()
        sums[0] = (small[...] + sx[0]) + (sx[1] + sx[2])
        for d in (1, 2, 3):
            tiny(1, d).start()

    def tiny_2():
        for d in (1, 2, 3):
            tiny(1, d).wait()
        sums[1] = (sums[0] + sy[0]) + (sy[1] + sy[2])
        tiny(2, 1).start()

    def tiny_3():
        tiny(2, 1).wait()
        sums[2] = sums[1] + ss[...]
        for copy in keep_own:
            copy.start()
        for d in (1, 2, 3):
            tiny(3, d).start()

    pl.when(parity == 1)(lambda: arrived_rows(1984, ag_send))
    for axis in (0, 1):
        for d in (1, 3):
            pl.semaphore_signal(ready, inc=1, device_id=peer(axis, d), device_id_type=MESH)

    def slot(t, carry):
        pl.when((t >= 3) & (t < 3 + SLOTS))(lambda: row_sums(t - 3))
        for number, turn in enumerate((tiny_0, tiny_1, tiny_2, tiny_3)):
            pl.when(t == 3 + SLOTS + number)(turn)
        for s in ORDER:
            k = t - jnp.where(parity == 1, OFFSET_FEED[s], OFFSET_ATTEND[s])
            live = (k >= 0) & (k < CHUNKS)
            if s == 0:
                live = live & (multiplies(k) | imported(k))
            elif s < 5:
                live = live & reduces(k)
            elif s == 5:
                live = live & (reduces(k) | gathers(k))
            else:
                live = live & gathers(k)
            pl.when(live)(lambda turn=stages[s], k=k: turn(k))
        return carry

    lax.fori_loop(0, CHUNKS + max(OFFSET_FEED + OFFSET_ATTEND), slot, 0)

    for d in (1, 2, 3):
        tiny(3, d).wait()
    for copy in keep_own:
        copy.wait()

    def sent(rows, sem):
        arrived_rows(rows, sem)

    pl.when(parity == 1)(lambda: sent(10 * ROWS, swap_send))
    pl.when(parity == 0)(lambda: sent(6 * ROWS, swap_send))
    pl.when(parity == 0)(lambda: sent(64, down_send))
    for number, (ring_count, z_count) in enumerate(((4, 0), (7, 1), (5, 1), (8, 2))):
        @pl.when(section == number)
        def _():
            sent(ring_count * 480, ring_send.at[0])
            if z_count:
                sent(z_count * 32, z_send)

    pl.when(sends_out)(lambda: export_copy().wait_send())
    sent(6 * 480, ring_send.at[1])
    sent(6 * 512, last_send)
    sent(6 * 512, last_recv)

    @pl.when(jnp.logical_not(first))
    def _():
        for micro in range(SLOTS):
            bwd_copy(micro).wait_send()
            ig_copy(micro, 1).wait_recv()

    @pl.when(first)
    def _():
        for micro in range(SLOTS):
            ig_own(micro).wait()
            for d in (1, 2, 3):
                ig_copy(micro, d).wait_send()


def mega(block, cot, group_ids, live_count, group_scale, gains, shifts, qv_bias, up_bias, out_bias, w1, down):
    any_space = pl.BlockSpec(memory_space=pl.ANY)
    dma = pltpu.SemaphoreType.DMA
    return pl.pallas_call(
        mega_kernel,
        name="mega",
        out_shape=[
            jax.ShapeDtypeStruct((6 * 1024, WIDTH), BF16),
            jax.ShapeDtypeStruct((SECTIONS + 1, 16, WIDTH), F32),
            jax.ShapeDtypeStruct((SLOTS, LEN, 256), BF16),
        ],
        in_specs=[any_space] * 12,
        out_specs=[any_space, any_space, any_space],
        scratch_shapes=[
            pltpu.SMEM((SLOTS,), jnp.int32),
            pltpu.SMEM((1,), jnp.int32),
            pltpu.SMEM((8,), F32),
            pltpu.VMEM((1, 2, WIDTH), F32),
            pltpu.VMEM((1, 2, WIDTH), F32),
            pltpu.VMEM((2, 2, WIDTH), F32),
            pltpu.VMEM((2, FF), F32),
            pltpu.VMEM((1, WIDTH), F32),
            pltpu.VMEM((WIDTH, FF), BF16),
            pltpu.VMEM((2 * FF, WIDTH), BF16),
            pltpu.VMEM((WIDTH, FF), BF16),
            pltpu.VMEM((10, SLOTS, LEN, WIDTH), BF16),
            pltpu.VMEM((10, SLOTS, LEN, WIDTH), BF16),
            pltpu.VMEM((SLOTS, LEN, WIDTH), BF16),
            pltpu.VMEM((SLOTS, LEN, 3), F32),
            pltpu.VMEM((SLOTS, LEN, WIDTH), BF16),
            pltpu.VMEM((SLOTS, LEN, WIDTH), BF16),
            pltpu.VMEM((SLOTS, LEN, WIDTH), BF16),
            pltpu.VMEM((SLOTS, LEN, WIDTH), BF16),
            pltpu.VMEM((LEN, WIDTH), F32),
            pltpu.VMEM((16, WIDTH), F32),
            pltpu.VMEM((16, WIDTH), F32),
            pltpu.VMEM((2, 2, 16, WIDTH), BF16),
            pltpu.VMEM((3, 16, WIDTH), F32),
            pltpu.VMEM((3, 16, WIDTH), F32),
            pltpu.VMEM((16, WIDTH), F32),
            pltpu.VMEM((3, 16, WIDTH), F32),
            dma((12,)), dma, dma((2,)), dma, dma((4, 2)),
            dma((SLOTS,)), dma((SLOTS,)), dma((SLOTS,)), dma((SLOTS,)),
            dma((SLOTS, 4)), dma((SLOTS,)), pltpu.SemaphoreType.REGULAR, pltpu.SemaphoreType.REGULAR,
            dma, dma((2,)), pltpu.SemaphoreType.REGULAR,
            dma((2,)), dma((8, CHUNKS)), dma, dma((2, 2)), dma, dma, dma((CHUNKS,)), dma, dma,
            dma((12,)), dma((12,)),
        ],
        compiler_params=pltpu.CompilerParams(
            collective_id=0, has_side_effects=True, vmem_limit_bytes=63 * 2**20
        ),
    )(block, cot, group_ids, live_count, group_scale, gains, shifts, qv_bias, up_bias, out_bias, w1, down)


def widen_kernel(
    reduced, sums_hbm, grad_in,
    first_out, down_out, qv_out, up_out, bias_out, gain_out, shift_out, grad_out,
    narrow, wide, sums, qv, up, bias, gain, shift, in_sem, out_sem, small_sem,
):
    rows, depth = wide.shape[1], wide.shape[0]
    count = 6 * 1024 // rows

    def load(i):
        return pltpu.make_async_copy(reduced.at[pl.ds(i * rows, rows)], narrow.at[i % depth], in_sem.at[i % depth])

    def store(i):
        chunk, cut = i * rows // 1024, pl.ds(i * rows % 1024, rows)
        if chunk < 2:
            target = down_out.at[pl.ds(i * rows, rows)]
        else:
            target = first_out.at[0, cut, pl.ds((chunk - 2) * 1024, 1024)]
        return pltpu.make_async_copy(wide.at[i % depth], target, out_sem.at[i % depth])

    for i in range(depth):
        load(i).start()
    load_sums = pltpu.make_async_copy(sums_hbm, sums, small_sem.at[0])
    load_sums.start()
    move_grad = pltpu.make_async_copy(grad_in, grad_out, small_sem.at[1])
    move_grad.start()
    small = [(qv, qv_out), (up, up_out), (bias, bias_out), (gain, gain_out), (shift, shift_out)]
    small = [pltpu.make_async_copy(*piece, small_sem.at[2 + j]) for j, piece in enumerate(small)]
    for i in range(count):
        load(i).wait()
        if i >= depth:
            store(i - depth).wait()
        wide[i % depth] = narrow[i % depth].astype(F32)
        store(i).start()
        if i + depth < count:
            load(i + depth).start()
        if i == 2:
            load_sums.wait()
            for layer in (0, 1):
                qv[layer, 0:1, :] = sums[2 * layer, 5:6, :]
                qv[layer, 1:2, :] = sums[2 * layer, 7:8, :]
                for j in range(4):
                    up[layer : layer + 1, j * WIDTH : (j + 1) * WIDTH] = sums[2 * layer + 1, 5 + j : 6 + j, :]
            bias[...] = sums[SECTIONS, 4:5, :]
            gain[0] = sums[SECTIONS, 0:2, :]
            shift[0] = sums[SECTIONS, 2:4, :]
            for copy in small:
                copy.start()
    for i in range(count - depth, count):
        store(i).wait()
    for copy in small:
        copy.wait()
    move_grad.wait()


def widen(reduced, sums, grad):
    any_space = pl.BlockSpec(memory_space=pl.ANY)
    rows, depth = 1024, 3
    dma = pltpu.SemaphoreType.DMA
    shapes = [(2, 2, WIDTH), (2, FF), (1, WIDTH), (1, 2, WIDTH), (1, 2, WIDTH)]
    return pl.pallas_call(
        widen_kernel,
        name="widen",
        out_shape=[
            jax.ShapeDtypeStruct((1, WIDTH, FF), F32),
            jax.ShapeDtypeStruct((2 * WIDTH, WIDTH), F32),
            *[jax.ShapeDtypeStruct(shape, F32) for shape in shapes],
            jax.ShapeDtypeStruct((SLOTS, LEN, 256), BF16),
        ],
        in_specs=[any_space] * 3,
        out_specs=[any_space] * 8,
        scratch_shapes=[
            pltpu.VMEM((depth, rows, WIDTH), BF16),
            pltpu.VMEM((depth, rows, WIDTH), F32),
            pltpu.VMEM((SECTIONS + 1, 16, WIDTH), F32),
            *[pltpu.VMEM(shape, F32) for shape in shapes],
            dma((depth,)), dma((depth,)), dma((7,)),
        ],
        compiler_params=pltpu.CompilerParams(vmem_limit_bytes=63 * 2**20),
    )(reduced, sums, grad)


def on_device(
    block_input, cotangent, group_ids, live_count, group_scale, norm_gain, norm_bias, first_weight,
    qv_bias, up_bias, down_weight, out_bias,
):
    reduced, sums, grad = mega(
        block_input, cotangent, group_ids, live_count, group_scale, norm_gain, norm_bias,
        qv_bias, up_bias, out_bias, first_weight, down_weight,
    )
    first_grad, down_grad, qv_grad, up_grad, bias_grad, gain_grad, shift_grad, input_grad = widen(reduced, sums, grad)
    return input_grad, first_grad, down_grad, qv_grad, up_grad, bias_grad, gain_grad, shift_grad


def solution(mesh):
    in_specs = (
        P("dp", None, None),
        P("dp", None, None),
        P("dp"),
        P("dp"),
        P(),
        P("section", None, None),
        P("section", None, None),
        P("section", None, None),
        P(),
        P(),
        P("section", None),
        P("section", None),
    )
    out_specs = (
        P("dp", None, "section"),
        P("section", None, None),
        P("section", None),
        P(),
        P(),
        P("section", None),
        P("section", None, None),
        P("section", None, None),
    )
    return jax.shard_map(on_device, mesh=mesh, in_specs=in_specs, out_specs=out_specs, check_vma=False)
```

```python
import math

import jax
import jax.numpy as jnp
from jax import lax
from jax.experimental import pallas as pl
from jax.experimental.pallas import tpu as pltpu
from jax.sharding import PartitionSpec as P

MESH = pl.DeviceIdType.MESH
BF16 = jnp.bfloat16
F32 = jnp.float32

WIDTH = 1024
FF = 4096
LEN = 128
SLOTS = 4
ROWS = SLOTS * LEN
PAIRS = 8
SECTIONS = 4
NORM_EPS = 1e-05
GELU_C = math.sqrt(2.0 / math.pi)
CHUNKS = 8
ORDER = (7, 0, 3, 8, 4, 5, 6, 2, 9)
OFFSET_FEED = (0, 0, 1, 3, 4, 5, 6, 8, 10, 12)
OFFSET_ATTEND = (0, 0, 1, 3, 4, 5, 6, 8, 11, 14)


def device(section, x, y, core):
    return (section, x * 8 + y * 2 + core)


def place():
    at = lax.axis_index("dp")
    return lax.axis_index("section"), at // 8, (at // 2) % 4, at % 2


def greet(section, x, y, core, here):
    barrier = pltpu.get_barrier_semaphore()
    others = [device(section, x, y, 1 - core), device(section + 1 - 2 * (section % 2), x, y, core)]
    for d in (1, 2, 3):
        others.append(device(section, (x + d) % 4, y, core))
        others.append(device(section, x, (y + d) % 4, core))
    for other in others:
        pl.semaphore_signal(barrier, inc=1, device_id=other, device_id_type=MESH)

    @pl.when(section < 2)
    def _():
        for high in (2, 3):
            pl.semaphore_signal(barrier, inc=1, device_id=device(high, x, y, core), device_id_type=MESH)

    def wait():
        pl.semaphore_wait(barrier, jnp.where(section < 2, 8, 10))

        @pl.when(section >= 2)
        def _():
            for low in (0, 1):
                pl.semaphore_signal(here, inc=1, device_id=device(low, x, y, core), device_id_type=MESH)

    return wait


def remote(source, target, send_sem, recv_sem, to):
    return pltpu.make_async_remote_copy(
        src_ref=source,
        dst_ref=target,
        send_sem=send_sem,
        recv_sem=recv_sem,
        device_id=to,
        device_id_type=MESH,
    )


def dot(a, b):
    return jnp.dot(a, b, preferred_element_type=F32)


def dot_nt(a, b):
    return lax.dot_general(a, b, (((1,), (1,)), ((), ())), preferred_element_type=F32)


def dot_tn(a, b):
    return lax.dot_general(a, b, (((0,), (0,)), ((), ())), preferred_element_type=F32)


def normalize(entries):
    average = jnp.mean(entries, axis=-1, keepdims=True)
    centered = entries - average
    inverse = lax.rsqrt(jnp.mean(centered * centered, axis=-1, keepdims=True) + NORM_EPS)
    return centered * inverse, inverse


def norm_backward(grad_out, unit, inverse, gain):
    scaled = grad_out * gain
    middle = jnp.mean(scaled, axis=-1, keepdims=True)
    along = jnp.mean(scaled * unit, axis=-1, keepdims=True)
    return inverse * (scaled - middle - unit * along)


def column_sum(entries):
    return jnp.sum(entries, axis=0, keepdims=True)


def mega_kernel(
    block_hbm, cot_hbm, group_hbm, live_hbm, scale_hbm, gains_hbm, shifts_hbm, qv_hbm, up_hbm, bias_hbm, w1_hbm, down_hbm,
    out_hbm, small_hbm, grad_hbm,
    group_ids, live_count, group_scale, gains, shifts, qv_bias, up_bias, out_bias,
    w1, buffer, w2t, ops, other, units, stats, r_in, r_out, g_in, g_out, wide, small, vectors,
    z, sx, sy, ss, sums,
    load_sem, down_send, down_recv, ag_send, ag_recv,
    fwd_send, fwd_recv, bwd_send, bwd_recv, ig_send, ig_recv, token, here,
    swap_send, swap_recv, ready, ring_send, ring_recv, z_send, z_recv, export_send, export_recv, own_sem, last_send, last_recv,
    tiny_send, tiny_recv,
):
    section, x, y, core = place()
    parity = section % 2
    layer = section // 2
    last = section == SECTIONS - 1
    first = section == 0
    sibling = device(section, x, y, 1 - core)
    w1t, w2 = buffer.at[pl.ds(0, FF)], buffer.at[pl.ds(FF, FF)]

    meet = greet(section, x, y, core, here)
    load_w1 = pltpu.make_async_copy(w1_hbm.at[0], w1, load_sem.at[0])
    load_own = pltpu.make_async_copy(down_hbm, w2.at[pl.ds(2048, 2048)], load_sem.at[1])
    load_block = pltpu.make_async_copy(block_hbm, r_in, load_sem.at[2])
    load_cot = pltpu.make_async_copy(cot_hbm, g_in, load_sem.at[3])

    pieces = [
        (gains_hbm, gains), (shifts_hbm, shifts), (bias_hbm, out_bias), (qv_hbm, qv_bias), (up_hbm, up_bias),
        (group_hbm, group_ids), (live_hbm, live_count), (scale_hbm, group_scale),
    ]
    load_pieces = [pltpu.make_async_copy(*piece, load_sem.at[4 + j]) for j, piece in enumerate(pieces)]

    @pl.when(first)
    def _():
        load_block.start()

    for copy in load_pieces:
        copy.start()
    load_w1.start()

    @pl.when(parity == 1)
    def _():
        load_own.start()

    @pl.when(last)
    def _():
        load_cot.start()

    meet()

    left, right = pl.ds(0, 512), pl.ds(512, 512)
    both = [(h, d) for h in (0, 1) for d in (0, 1)]

    def peer(axis, d):
        if axis == 0:
            return device(section, (x + d) % 4, y, core)
        return device(section, x, (y + d) % 4, core)

    def arrived_rows(rows, sem):
        piece = buffer.at[pl.ds(0, rows)]
        pltpu.make_async_copy(piece, piece, sem).wait()

    def down_rows(h, p, major, minor, n):
        row = h * 1024 + core * 512 + p * 256 + major * 64 + minor * 16
        return pl.ds(pl.multiple_of(row, 16), n)

    def down_spot(h):
        return (y, x) if h == 0 else (x, y)

    def down_copy(p, h):
        rows = down_rows(h, p, *down_spot(h), 16)
        return remote(
            down_hbm.at[rows], w2.at[rows], down_send, down_recv.at[p], device((section + 1) % 4, x, y, core)
        )

    def down_near(p, h, d):
        rows = down_rows(h, p, *down_spot(h), 16)
        return remote(w2.at[rows], w2.at[rows], ag_send, ag_recv.at[0, p], peer(h, d))

    def down_ring(p, h, d):
        rows = down_rows(h, p, down_spot(h)[0], 0, 64)
        return remote(w2.at[rows], w2.at[rows], ag_send, ag_recv.at[1, p], peer(1 - h, 1 - 2 * d))

    def down_pass(p, h, d):
        step = 1 - 2 * d
        rows = down_rows(h, p, (down_spot(h)[0] - step) % 4, 0, 64)
        piece = w2.at[rows, left if d == 0 else right]
        return remote(piece, piece, ag_send, ag_recv.at[2, p], peer(1 - h, step))

    def down_share(p, h, d):
        rows = down_rows(h, p, (down_spot(h)[0] + d) % 4, 0, 64)
        return remote(w2.at[rows], w2.at[rows], ag_send, ag_recv.at[3, 0], sibling)

    @pl.when(parity == 0)
    def _():
        for p in (0, 1):
            for h in (0, 1):
                down_copy(p, h).start()

    for copy in load_pieces:
        copy.wait()

    @pl.when(parity == 0)
    def _():
        vectors[5:6, :] = qv_bias[layer, 0:1, :]
        vectors[6:7, :] = jnp.zeros((1, WIDTH), F32)
        vectors[7:8, :] = qv_bias[layer, 1:2, :]

    @pl.when(parity == 1)
    def _():
        for j in range(4):
            vectors[5 + j : 6 + j, :] = up_bias[pl.ds(layer, 1), j * WIDTH : (j + 1) * WIDTH]

    def sequence_weight(micro):
        group = group_ids[micro]
        chosen = jnp.float32(0.0)
        for label in range(8):
            chosen = jnp.where(group == label, group_scale[label], chosen)
        weight = jnp.where(micro < live_count[0], chosen, 0.0)
        return jnp.where(last, weight, 1.0)

    small[...] = jnp.zeros_like(small)

    def gather_start():
        for p in (0, 1):
            arrived_rows(32, down_recv.at[p])
            for h in (0, 1):
                for d in (1, 3, 2):
                    down_near(p, h, d).start()
        for p in (0, 1):
            arrived_rows(96, ag_recv.at[0, p])
            for h, d in both:
                down_ring(p, h, d).start()
            for h in (0, 1):
                down_share(p, h, 0).start()
        gather_pass(0)
        gather_pass(1)
        load_own.wait()

    def gather_pass(p):
        arrived_rows(256, ag_recv.at[1, p])
        for h, d in both:
            down_pass(p, h, d).start()
        for h in (0, 1):
            down_share(p, h, 1).start()
            down_share(p, h, 3).start()

    def gather_end():
        for p in (0, 1):
            arrived_rows(128, ag_recv.at[2, p])
            for h in (0, 1):
                down_share(p, h, 2).start()
        arrived_rows(1024, ag_recv.at[3, 0])

    pl.when(parity == 1)(gather_start)
    pl.when(last)(gather_end)

    load_w1.wait()

    @pl.when(first)
    def _():
        load_block.wait()

    @pl.when(last)
    def _():
        load_cot.wait()

    def fwd_copy(micro):
        return remote(
            r_out.at[micro], r_in.at[micro], fwd_send.at[micro], fwd_recv.at[micro],
            device((section + 1) % 4, x, y, core),
        )

    def bwd_copy(micro):
        return remote(
            g_out.at[micro], g_in.at[micro], bwd_send.at[micro], bwd_recv.at[micro],
            device((section + 3) % 4, x, y, core),
        )

    def ig_copy(micro, d):
        to = (section + d) % 4
        return remote(
            g_out.at[micro, :, pl.ds(d * 256, 256)], grad_hbm.at[micro], ig_send.at[micro, d], ig_recv.at[micro],
            device(to, x, y, core),
        )

    def ig_own(micro):
        return pltpu.make_async_copy(g_out.at[micro, :, pl.ds(0, 256)], grad_hbm.at[micro], ig_send.at[micro, 0])

    lanes = lax.broadcasted_iota(jnp.int32, (LEN, 128), 1)
    low_lanes = lanes < 64

    def two_heads(entries):
        zero = jnp.zeros_like(entries)
        return jnp.concatenate([jnp.where(low_lanes, entries, zero), jnp.where(low_lanes, zero, entries)], axis=0)

    def transposes():
        def one(j, carry):
            cut = pl.ds(pl.multiple_of(j * 256, 256), 256)
            w1t[cut, :] = w1[:, cut].T
            return carry

        lax.fori_loop(0, 16, one, 0)

        @pl.when(parity == 1)
        def _():
            def two(j, carry):
                cut = pl.ds(pl.multiple_of(j * 256, 256), 256)
                w2t[:, cut] = w2[cut, :].T
                return carry

            lax.fori_loop(0, 16, two, 0)

    def attention_forward(micro):
        normed = ops[0, micro]
        for j in range(3):
            part = dot(normed, w1[:, j * WIDTH : (j + 1) * WIDTH]) + vectors[5 + j : 6 + j, :]
            ops[6 + j, micro] = part.astype(BF16)
        rows = lax.broadcasted_iota(jnp.int32, (LEN, LEN), 0)
        columns = lax.broadcasted_iota(jnp.int32, (LEN, LEN), 1)
        causal = rows <= columns
        for p in range(PAIRS):
            cut = slice(p * 128, (p + 1) * 128)
            query, key, value = (ops[6 + j, micro, :, cut] for j in range(3))
            scores = dot_nt(two_heads(key), query) * 0.125
            parts = []
            for head in (0, 1):
                part = jnp.where(causal, scores[head * LEN : (head + 1) * LEN], -1e9)
                powers = jnp.exp(part - jnp.max(part, axis=0, keepdims=True))
                part = (powers / jnp.sum(powers, axis=0, keepdims=True)).astype(BF16)
                ops[3 + p // 4, micro, :, (p % 4 * 2 + head) * 128 : (p % 4 * 2 + head + 1) * 128] = part
                parts.append(part)
            ops[2, micro, :, cut] = dot_tn(jnp.concatenate(parts, axis=0), two_heads(value)).astype(BF16)

        @pl.when(section == 2)
        def _():
            wide[...] = dot(ops[2, micro], w1t[3 * WIDTH :, :]) + out_bias[...]

        @pl.when(section != 2)
        def _():
            wide[...] = dot_nt(ops[2, micro], w1[:, 3 * WIDTH :]) + out_bias[...]

    def feed_forward(micro):
        normed = ops[0, micro]
        branch = out_bias[...]
        def product(j):
            b, cut = j * 256 // WIDTH, slice(j * 256 % WIDTH, j * 256 % WIDTH + 256)
            return dot(normed, w1[:, j * 256 : (j + 1) * 256]) + vectors[5 + b : 6 + b, cut]

        def gate(j, hidden):
            b, cut = j * 256 // WIDTH, slice(j * 256 % WIDTH, j * 256 % WIDTH + 256)
            square = hidden * hidden
            above = 0.5 + 0.5 * jnp.tanh(hidden * (GELU_C + (GELU_C * 0.044715) * square))
            active = hidden * above
            slope = above + (active - active * above) * (2.0 * GELU_C + (6.0 * GELU_C * 0.044715) * square)
            ops[6 + b, micro, :, cut] = slope.astype(BF16)
            ops[2 + b, micro, :, cut] = active.astype(BF16)

        order = (8, 9, 10, 11, 12, 13, 14, 15, 0, 1, 2, 3, 4, 5, 6, 7)
        hidden = product(order[0])
        for step, j in enumerate(order):
            ahead = product(order[step + 1]) if step + 1 < len(order) else None
            gate(j, hidden)
            hidden = ahead
        branch = out_bias[...]
        for j in (2, 3, 0, 1):
            if j == 0:
                pl.when((micro == 0) & (section == 1))(gather_end)
            branch = branch + dot(ops[2 + j, micro], w2[j * WIDTH : (j + 1) * WIDTH, :])
        wide[...] = branch

    def attention_backward(micro):
        ops[9, micro] = dot(ops[1, micro], w1[:, 3 * WIDTH :]).astype(BF16)
        for p in range(PAIRS):
            cut = slice(p * 128, (p + 1) * 128)
            query, key, value = (ops[6 + j, micro, :, cut] for j in range(3))
            grad = ops[9, micro, :, cut]
            parts = [ops[3 + p // 4, micro, :, (p % 4 * 2 + h) * 128 : (p % 4 * 2 + h + 1) * 128] for h in (0, 1)]
            grad_weights = dot_nt(two_heads(value), grad)
            grad_scores = []
            for head in (0, 1):
                part = parts[head].astype(F32)
                product = part * grad_weights[head * LEN : (head + 1) * LEN]
                grad_scores.append((product - part * jnp.sum(product, axis=0, keepdims=True)).astype(BF16))
            grad_scores = jnp.concatenate(grad_scores, axis=0)
            grad_query = dot_tn(grad_scores, two_heads(key)) * 0.125
            both_heads = dot(grad_scores, query) * 0.125
            grad_key = jnp.where(low_lanes, both_heads[:LEN], both_heads[LEN:])
            both_heads = dot(jnp.concatenate(parts, axis=0), grad)
            grad_value = jnp.where(low_lanes, both_heads[:LEN], both_heads[LEN:])
            for j, part in enumerate((grad_query, grad_key, grad_value)):
                ops[6 + j, micro, :, cut] = part.astype(BF16)
        total = jnp.zeros((LEN, WIDTH), F32)
        for j in range(3):
            part = ops[6 + j, micro]
            total = total + dot(part, w1t[j * WIDTH : (j + 1) * WIDTH, :])
        wide[...] = total

    def feed_backward(micro):
        grad_branch = ops[1, micro]
        total = jnp.zeros((LEN, WIDTH), F32)
        for j in range(4):
            grad = dot(grad_branch, w2t[:, j * WIDTH : (j + 1) * WIDTH])
            grad = (grad * ops[6 + j, micro].astype(F32)).astype(BF16)
            ops[6 + j, micro] = grad
            total = total + dot(grad, w1t[j * WIDTH : (j + 1) * WIDTH, :])
        wide[...] = total

    def swap(block, count, micro, group):
        piece = pl.ds(block, count)
        return remote(ops.at[piece, micro], other.at[piece, micro], swap_send, swap_recv.at[group], sibling)

    def forward(micro):
        @pl.when(jnp.logical_not(first))
        def _():
            fwd_copy(micro).wait_recv()

        residual = r_in[micro].astype(F32)
        mean = jnp.mean(residual, axis=-1, keepdims=True)
        centered = residual - mean
        inverse = lax.rsqrt(jnp.mean(centered * centered, axis=-1, keepdims=True) + NORM_EPS)
        stats[micro, :, 0:1] = mean
        stats[micro, :, 1:2] = inverse
        ops[0, micro] = (centered * inverse * gains[0, 0:1, :] + shifts[0, 0:1, :]).astype(BF16)
        pl.when(jnp.logical_not(last))(lambda: swap(0, 1, micro, 0).start())

        @pl.when(parity == 0)
        def _():
            attention_forward(micro)

        @pl.when(parity == 1)
        def _():
            feed_forward(micro)

        unit, inverse = normalize(wide[...])

        @pl.when(jnp.logical_not(last))
        def _():
            after = r_in[micro].astype(F32) + unit * gains[0, 1:2, :] + shifts[0, 1:2, :]
            r_out[micro] = after.astype(BF16)
            leads = (section == 1) & (core == 1)
            follows = (section == 1) & (core == 0)
            pl.when(micro > jnp.where(leads, 1, 0))(lambda: fwd_copy(micro - 1).wait_send())
            pl.when((section < 2) & (micro == 0))(lambda: pl.semaphore_wait(here, 2))
            pl.when(follows & (micro == 0))(lambda: pl.semaphore_wait(token, 1))
            fwd_copy(micro).start()

            @pl.when(leads & (micro == 0))
            def _():
                fwd_copy(micro).wait_send()
                pl.semaphore_signal(token, inc=1, device_id=sibling, device_id_type=MESH)

        units[micro] = unit.astype(BF16)
        stats[micro, :, 2:3] = inverse
        pl.when(parity == 0)(lambda: swap(2, 1, micro, 0).start())
        pl.when(section == 1)(lambda: swap(2, 4, micro, 0).start())

    def backward(micro):
        @pl.when(jnp.logical_not(last))
        def _():
            bwd_copy(micro).wait_recv()

        weight = sequence_weight(micro)
        incoming = g_in[micro].astype(F32) * weight
        unit = units[micro].astype(F32)
        ops[1, micro] = norm_backward(incoming, unit, stats[micro, :, 2:3], gains[0, 1:2, :]).astype(BF16)
        pl.when(jnp.logical_not(last))(lambda: swap(1, 1, micro, 0).start())

        @pl.when(parity == 0)
        def _():
            attention_backward(micro)

        @pl.when(parity == 1)
        def _():
            feed_backward(micro)

        inverse = stats[micro, :, 1:2]
        unit = (r_in[micro].astype(F32) - stats[micro, :, 0:1]) * inverse
        incoming = g_in[micro].astype(F32) * weight
        grad = incoming + norm_backward(wide[...], unit, inverse, gains[0, 0:1, :])
        g_out[micro] = grad.astype(BF16)

        @pl.when(jnp.logical_not(first))
        def _():
            bwd_copy(micro).start()

        @pl.when(first)
        def _():
            ig_own(micro).start()
            for d in (1, 2, 3):
                ig_copy(micro, d).start()

        r_out[micro] = wide[...].astype(BF16)
        pl.when(parity == 0)(lambda: swap(6, 3, micro, 1).start())
        pl.when(section == 1)(lambda: swap(6, 4, micro, 1).start())

    def row_sums(micro):
        weight = sequence_weight(micro)
        unit = (r_in[micro].astype(F32) - stats[micro, :, 0:1]) * stats[micro, :, 1:2]
        grad = r_out[micro].astype(F32)
        small[0:1, :] += column_sum(grad * unit)
        small[2:3, :] += column_sum(grad)
        incoming = g_in[micro].astype(F32) * weight
        small[1:2, :] += column_sum(incoming * units[micro].astype(F32))
        small[3:4, :] += column_sum(incoming)
        small[4:5, :] += column_sum(ops[1, micro].astype(F32))
        for j in range(4):
            small[5 + j : 6 + j, :] += column_sum(ops[6 + j, micro].astype(F32))

    turn_at = jnp.where(section >= 2, 0, SLOTS)

    def step(t, carry):
        is_forward = jnp.where(last, (t + 1) % 2, jnp.where(t < SLOTS, 1, 0))
        micro = jnp.where(last, t // 2, t % SLOTS)

        @pl.when((t == SLOTS) & jnp.logical_not(last))
        def _():
            fwd_copy(SLOTS - 1).wait_send()

        @pl.when(t == turn_at)
        def _():
            transposes()

        @pl.when(is_forward == 1)
        def _():
            forward(micro)

        @pl.when(is_forward == 0)
        def _():
            backward(micro)

        return carry

    lax.fori_loop(0, 2 * SLOTS, step, 0)

    @pl.when(last)
    def _():
        for block, count, group in ((0, 6, 0), (6, 4, 1)):
            piece = pl.ds(block, count)
            remote(ops.at[piece], other.at[piece], swap_send, swap_recv.at[group], sibling).start()

    def spot(h):
        return (x, y) if h == 0 else (y, x)

    sends_out = section == 1
    takes_in = section == 2

    def chunk(q):
        late = jnp.where(takes_in, jnp.where(q == 6, 2, q - 4), jnp.where(q == 4, 1, 0))
        return jnp.where(parity == 1, q, jnp.where(q < 4, 7 - q, late))

    def exported(q):
        return sends_out & (q == 0)

    def imported(q):
        return takes_in & (q == 6)

    def multiplies(q):
        return (parity == 1) | (q < 4)

    def reduces(q):
        return (multiplies(q) & jnp.logical_not(exported(q))) | imported(q)

    def hands_over(q):
        return ((section == 3) & (q < 2)) | (sends_out & (q == 1)) | imported(q)

    def takes_over(q):
        return ((section == 0) & ((q == 4) | (q == 6))) | (takes_in & ((q == 4) | (q == 5)))

    def gathers(q):
        return ((parity == 1) & (q >= 2)) | ((parity == 0) & (q < 4)) | takes_over(q)

    def at(q, h, b1, b2, n):
        row = chunk(q) * 1024 + core * 512 + h * 256 + b1 * 64 + b2 * 16
        return pl.ds(pl.multiple_of(row, 16), n)

    def export_copy():
        return remote(
            buffer.at[pl.ds(pl.multiple_of(core * 512, 512), 512)],
            buffer.at[pl.ds(pl.multiple_of(2048 + core * 512, 512), 512)],
            export_send, export_recv, device((section + 1) % 4, x, y, core),
        )

    def out_at(q, h, b1, b2, n):
        k = chunk(q)
        k = jnp.where((parity == 1) | (k >= 4), k - 2, k)
        row = k * 1024 + core * 512 + h * 256 + b1 * 64 + b2 * 16
        return pl.ds(pl.multiple_of(row, 16), n)

    def ring(stage, q, source, target, to):
        return remote(source, target, ring_send.at[stage // 4], ring_recv.at[stage, q], to)

    def land_one(q, h, d):
        return w1.at[pl.ds((q * 2 + h) * 64, 64), pl.ds(d * 512, 512)]

    def land_two(q, h, d):
        return w2t.at[pl.ds((q * 2 + h) * 64, 64), pl.ds(d * 1024, 1024)]

    def land_three(q, h, d):
        return w2t.at[pl.ds((q * 2 + h) * 64 + 16, 16), pl.ds(2048 + d * 1024, 512)]

    def land_four(q, h, d):
        return w2t.at[pl.ds((q * 2 + h) * 64, 16), pl.ds(2048 + d * 1024, 1024)]

    def rs_one(q, h, d):
        p1, _ = spot(h)
        rows = at(q, h, (p1 + 2) % 4, 0, 64)
        return ring(0, q, buffer.at[rows, left if d == 0 else right], land_one(q, h, d), peer(h, 1 - 2 * d))

    def rs_two(q, h, d):
        p1, _ = spot(h)
        step = 1 - 2 * d
        return ring(1, q, buffer.at[at(q, h, (p1 + step) % 4, 0, 64)], land_two(q, h, d), peer(h, step))

    def rs_three(q, h, d):
        p1, p2 = spot(h)
        rows = at(q, h, p1, (p2 + 2) % 4, 16)
        return ring(2, q, buffer.at[rows, left if d == 0 else right], land_three(q, h, d), peer(1 - h, 1 - 2 * d))

    def rs_four(q, h, d):
        p1, p2 = spot(h)
        step = 1 - 2 * d
        return ring(3, q, buffer.at[at(q, h, p1, (p2 + step) % 4, 16)], land_four(q, h, d), peer(1 - h, step))

    def z_copy(q, h):
        p1, p2 = spot(h)
        to = jnp.where(takes_in, 0, section - 1)
        slot = jnp.where(takes_in, 0, chunk(q))
        return remote(
            buffer.at[at(q, h, p1, p2, 16)], z.at[slot, h], z_send, z_recv.at[slot, h], device(to, x, y, core)
        )

    def z_arrival(q, h):
        return remote(z.at[chunk(q), h], z.at[chunk(q), h], z_send, z_recv.at[chunk(q), h], sibling)

    def own_copy(q, h):
        p1, p2 = spot(h)
        return pltpu.make_async_copy(
            buffer.at[at(q, h, p1, p2, 16)], out_hbm.at[out_at(q, h, p1, p2, 16)], own_sem.at[q]
        )

    def ag_one(q, h, d):
        p1, p2 = spot(h)
        target = out_hbm.at[out_at(q, h, p1, p2, 16)]
        return ring(4, q, buffer.at[at(q, h, p1, p2, 16)], target, peer(1 - h, 1 - 2 * d))

    def ag_two(q, h, d):
        p1, p2 = spot(h)
        step = 1 - 2 * d
        piece = out_hbm.at[out_at(q, h, p1, (p2 - step) % 4, 16), left if d == 0 else right]
        return ring(5, q, piece, piece, peer(1 - h, step))

    def ag_three(q, h, d):
        p1, _ = spot(h)
        piece = out_hbm.at[out_at(q, h, p1, 0, 64)]
        return ring(6, q, piece, piece, peer(h, 1 - 2 * d))

    def ag_four(q, h, d):
        p1, _ = spot(h)
        step = 1 - 2 * d
        piece = out_hbm.at[out_at(q, h, (p1 - step) % 4, 0, 64), left if d == 0 else right]
        return ring(7, q, piece, piece, peer(h, step))

    def last_copy(q, h, d):
        p1, _ = spot(h)
        piece = out_hbm.at[out_at(q, h, (p1 + d) % 4, 0, 64)]
        return remote(piece, piece, last_send, last_recv, sibling)

    def swapped(group):
        counts = ((3, 6), (3, 4))[group]
        pl.when(parity == 0)(lambda: arrived_rows(counts[0] * ROWS, swap_recv.at[group]))
        pl.when(parity == 1)(lambda: arrived_rows(counts[1] * ROWS, swap_recv.at[group]))

    def multiply(q):
        k = chunk(q)
        feed_down = (parity == 1) & (k < 4)
        from_context = (parity == 0) & (k == 7)
        a = jnp.where(feed_down, 2 + k, jnp.where(from_context, 1, 0))
        b = jnp.where(feed_down, 1, jnp.where(from_context, 2, 2 + k))
        pl.when(q == 0)(lambda: swapped(0))
        pl.when(q == 1 + 3 * parity)(lambda: swapped(1))
        right_own, right_other = ops[b].reshape(ROWS, WIDTH), other[b].reshape(ROWS, WIDTH)
        for cut in range(2):
            columns = pl.ds(pl.multiple_of(core * 512 + cut * 256, 256), 256)
            product = dot_tn(ops[a, :, :, columns].reshape(ROWS, 256), right_own)
            product = product + dot_tn(other[a, :, :, columns].reshape(ROWS, 256), right_other)
            buffer[pl.ds(pl.multiple_of(k * 1024 + core * 512 + cut * 256, 256), 256), :] = product.astype(BF16)

    def stage_0(q):
        pl.when(multiplies(q))(lambda: multiply(q))
        pl.when(exported(q))(lambda: export_copy().start())
        pl.when(imported(q))(lambda: export_copy().wait_recv())

        @pl.when(reduces(q))
        def _():
            pl.when(q == jnp.where(sends_out, 1, 0))(lambda: pl.semaphore_wait(ready, 4))
            for h, d in both:
                rs_one(q, h, d).start()

    def stage_2(q):
        arrived_rows(128, ring_recv.at[0, q])
        for h, d in both:
            p1, _ = spot(h)
            rows = at(q, h, (p1 + 1 - 2 * d) % 4, 0, 64)
            cut = left if d == 0 else right
            buffer[rows, cut] = buffer[rows, cut] + land_one(q, h, d)[...]
            rs_two(q, h, d).start()

    def stage_3(q):
        arrived_rows(256, ring_recv.at[1, q])
        for h in (0, 1):
            p1, _ = spot(h)
            rows = at(q, h, p1, 0, 64)
            total = buffer[rows, :].astype(F32) + land_two(q, h, 0)[...].astype(F32) + land_two(q, h, 1)[...].astype(F32)
            buffer[rows, :] = total.astype(BF16)
            for d in (0, 1):
                rs_three(q, h, d).start()

    def stage_4(q):
        arrived_rows(32, ring_recv.at[2, q])
        for h, d in both:
            p1, p2 = spot(h)
            rows = at(q, h, p1, (p2 + 1 - 2 * d) % 4, 16)
            cut = left if d == 0 else right
            buffer[rows, cut] = buffer[rows, cut] + land_three(q, h, d)[...]
            rs_four(q, h, d).start()

    def stage_5(q):
        @pl.when(reduces(q))
        def _():
            arrived_rows(64, ring_recv.at[3, q])
            for h in (0, 1):
                p1, p2 = spot(h)
                rows = at(q, h, p1, p2, 16)
                arrival = land_four(q, h, 0)[...].astype(F32) + land_four(q, h, 1)[...].astype(F32)
                buffer[rows, :] = (buffer[rows, :].astype(F32) + arrival).astype(BF16)

        @pl.when(hands_over(q))
        def _():
            for h in (0, 1):
                z_copy(q, h).start()

        @pl.when(takes_over(q))
        def _():
            for h in (0, 1):
                p1, p2 = spot(h)
                z_arrival(q, h).wait_recv()
                buffer[at(q, h, p1, p2, 16), :] = z[chunk(q), h]

        @pl.when(gathers(q))
        def _():
            for h in (0, 1):
                own_copy(q, h).start()
                for d in (0, 1):
                    ag_one(q, h, d).start()

    def stage_6(q):
        arrived_rows(64, ring_recv.at[4, q])
        for h, d in both:
            ag_two(q, h, d).start()
        arrived_rows(32, own_sem.at[q])

    def stage_7(q):
        arrived_rows(32, ring_recv.at[5, q])
        for h, d in both:
            ag_three(q, h, d).start()
        for h in (0, 1):
            last_copy(q, h, 0).start()

    def stage_8(q):
        arrived_rows(256, ring_recv.at[6, q])
        for h, d in both:
            ag_four(q, h, d).start()
        for h in (0, 1):
            last_copy(q, h, 1).start()
            last_copy(q, h, 3).start()

    def stage_9(q):
        arrived_rows(128, ring_recv.at[7, q])
        for h in (0, 1):
            last_copy(q, h, 2).start()

    stages = [stage_0, None, stage_2, stage_3, stage_4, stage_5, stage_6, stage_7, stage_8, stage_9]

    def tiny(phase, d):
        if phase == 0:
            return remote(small, sx.at[d - 1], tiny_send.at[d - 1], tiny_recv.at[d - 1], peer(0, d))
        if phase == 1:
            return remote(sums.at[0], sy.at[d - 1], tiny_send.at[d + 2], tiny_recv.at[d + 2], peer(1, d))
        if phase == 2:
            return remote(sums.at[1], ss, tiny_send.at[6], tiny_recv.at[6], sibling)
        return remote(
            sums.at[2], small_hbm.at[section], tiny_send.at[6 + d], tiny_recv.at[6 + d],
            device((section + d) % 4, x, y, core),
        )

    keep_own = [
        pltpu.make_async_copy(sums.at[2], small_hbm.at[section], tiny_send.at[10]),
        pltpu.make_async_copy(sums.at[2], small_hbm.at[SECTIONS], tiny_send.at[11]),
    ]

    def tiny_0():
        for d in (1, 2, 3):
            tiny(0, d).start()

    def tiny_1():
        for d in (1, 2, 3):
            tiny(0, d).wait()
        sums[0] = (small[...] + sx[0]) + (sx[1] + sx[2])
        for d in (1, 2, 3):
            tiny(1, d).start()

    def tiny_2():
        for d in (1, 2, 3):
            tiny(1, d).wait()
        sums[1] = (sums[0] + sy[0]) + (sy[1] + sy[2])
        tiny(2, 1).start()

    def tiny_3():
        tiny(2, 1).wait()
        sums[2] = sums[1] + ss[...]
        for copy in keep_own:
            copy.start()
        for d in (1, 2, 3):
            tiny(3, d).start()

    pl.when(parity == 1)(lambda: arrived_rows(1984, ag_send))
    for axis in (0, 1):
        for d in (1, 3):
            pl.semaphore_signal(ready, inc=1, device_id=peer(axis, d), device_id_type=MESH)

    def slot(t, carry):
        pl.when((t >= 3) & (t < 3 + SLOTS))(lambda: row_sums(t - 3))
        for number, turn in enumerate((tiny_0, tiny_1, tiny_2, tiny_3)):
            pl.when(t == 3 + SLOTS + number)(turn)
        for s in ORDER:
            k = t - jnp.where(parity == 1, OFFSET_FEED[s], OFFSET_ATTEND[s])
            live = (k >= 0) & (k < CHUNKS)
            if s == 0:
                live = live & (multiplies(k) | imported(k))
            elif s < 5:
                live = live & reduces(k)
            elif s == 5:
                live = live & (reduces(k) | gathers(k))
            else:
                live = live & gathers(k)
            pl.when(live)(lambda turn=stages[s], k=k: turn(k))
        return carry

    lax.fori_loop(0, CHUNKS + max(OFFSET_FEED + OFFSET_ATTEND), slot, 0)

    for d in (1, 2, 3):
        tiny(3, d).wait()
    for copy in keep_own:
        copy.wait()

    def sent(rows, sem):
        arrived_rows(rows, sem)

    pl.when(parity == 1)(lambda: sent(10 * ROWS, swap_send))
    pl.when(parity == 0)(lambda: sent(6 * ROWS, swap_send))
    pl.when(parity == 0)(lambda: sent(64, down_send))
    for number, (ring_count, z_count) in enumerate(((4, 0), (7, 1), (5, 1), (8, 2))):
        @pl.when(section == number)
        def _():
            sent(ring_count * 480, ring_send.at[0])
            if z_count:
                sent(z_count * 32, z_send)

    pl.when(sends_out)(lambda: export_copy().wait_send())
    sent(6 * 480, ring_send.at[1])
    sent(6 * 512, last_send)
    sent(6 * 512, last_recv)

    @pl.when(jnp.logical_not(first))
    def _():
        for micro in range(SLOTS):
            bwd_copy(micro).wait_send()
            ig_copy(micro, 1).wait_recv()

    @pl.when(first)
    def _():
        for micro in range(SLOTS):
            ig_own(micro).wait()
            for d in (1, 2, 3):
                ig_copy(micro, d).wait_send()


def mega(block, cot, group_ids, live_count, group_scale, gains, shifts, qv_bias, up_bias, out_bias, w1, down):
    any_space = pl.BlockSpec(memory_space=pl.ANY)
    dma = pltpu.SemaphoreType.DMA
    return pl.pallas_call(
        mega_kernel,
        name="mega",
        out_shape=[
            jax.ShapeDtypeStruct((6 * 1024, WIDTH), BF16),
            jax.ShapeDtypeStruct((SECTIONS + 1, 16, WIDTH), F32),
            jax.ShapeDtypeStruct((SLOTS, LEN, 256), BF16),
        ],
        in_specs=[any_space] * 12,
        out_specs=[any_space, any_space, any_space],
        scratch_shapes=[
            pltpu.SMEM((SLOTS,), jnp.int32),
            pltpu.SMEM((1,), jnp.int32),
            pltpu.SMEM((8,), F32),
            pltpu.VMEM((1, 2, WIDTH), F32),
            pltpu.VMEM((1, 2, WIDTH), F32),
            pltpu.VMEM((2, 2, WIDTH), F32),
            pltpu.VMEM((2, FF), F32),
            pltpu.VMEM((1, WIDTH), F32),
            pltpu.VMEM((WIDTH, FF), BF16),
            pltpu.VMEM((2 * FF, WIDTH), BF16),
            pltpu.VMEM((WIDTH, FF), BF16),
            pltpu.VMEM((10, SLOTS, LEN, WIDTH), BF16),
            pltpu.VMEM((10, SLOTS, LEN, WIDTH), BF16),
            pltpu.VMEM((SLOTS, LEN, WIDTH), BF16),
            pltpu.VMEM((SLOTS, LEN, 3), F32),
            pltpu.VMEM((SLOTS, LEN, WIDTH), BF16),
            pltpu.VMEM((SLOTS, LEN, WIDTH), BF16),
            pltpu.VMEM((SLOTS, LEN, WIDTH), BF16),
            pltpu.VMEM((SLOTS, LEN, WIDTH), BF16),
            pltpu.VMEM((LEN, WIDTH), F32),
            pltpu.VMEM((16, WIDTH), F32),
            pltpu.VMEM((16, WIDTH), F32),
            pltpu.VMEM((2, 2, 16, WIDTH), BF16),
            pltpu.VMEM((3, 16, WIDTH), F32),
            pltpu.VMEM((3, 16, WIDTH), F32),
            pltpu.VMEM((16, WIDTH), F32),
            pltpu.VMEM((3, 16, WIDTH), F32),
            dma((12,)), dma, dma((2,)), dma, dma((4, 2)),
            dma((SLOTS,)), dma((SLOTS,)), dma((SLOTS,)), dma((SLOTS,)),
            dma((SLOTS, 4)), dma((SLOTS,)), pltpu.SemaphoreType.REGULAR, pltpu.SemaphoreType.REGULAR,
            dma, dma((2,)), pltpu.SemaphoreType.REGULAR,
            dma((2,)), dma((8, CHUNKS)), dma, dma((2, 2)), dma, dma, dma((CHUNKS,)), dma, dma,
            dma((12,)), dma((12,)),
        ],
        compiler_params=pltpu.CompilerParams(
            collective_id=0, has_side_effects=True, vmem_limit_bytes=63 * 2**20
        ),
    )(block, cot, group_ids, live_count, group_scale, gains, shifts, qv_bias, up_bias, out_bias, w1, down)


def widen_kernel(
    reduced, sums_hbm, grad_in,
    first_out, down_out, qv_out, up_out, bias_out, gain_out, shift_out, grad_out,
    narrow, wide, sums, qv, up, bias, gain, shift, in_sem, out_sem, small_sem,
):
    rows, depth = wide.shape[1], wide.shape[0]
    count = 6 * 1024 // rows

    def load(i):
        return pltpu.make_async_copy(reduced.at[pl.ds(i * rows, rows)], narrow.at[i % depth], in_sem.at[i % depth])

    def store(i):
        chunk, cut = i * rows // 1024, pl.ds(i * rows % 1024, rows)
        if chunk < 2:
            target = down_out.at[pl.ds(i * rows, rows)]
        else:
            target = first_out.at[0, cut, pl.ds((chunk - 2) * 1024, 1024)]
        return pltpu.make_async_copy(wide.at[i % depth], target, out_sem.at[i % depth])

    for i in range(depth):
        load(i).start()
    load_sums = pltpu.make_async_copy(sums_hbm, sums, small_sem.at[0])
    load_sums.start()
    move_grad = pltpu.make_async_copy(grad_in, grad_out, small_sem.at[1])
    move_grad.start()
    small = [(qv, qv_out), (up, up_out), (bias, bias_out), (gain, gain_out), (shift, shift_out)]
    small = [pltpu.make_async_copy(*piece, small_sem.at[2 + j]) for j, piece in enumerate(small)]
    for i in range(count):
        load(i).wait()
        if i >= depth:
            store(i - depth).wait()
        wide[i % depth] = narrow[i % depth].astype(F32)
        store(i).start()
        if i + depth < count:
            load(i + depth).start()
        if i == 2:
            load_sums.wait()
            for layer in (0, 1):
                qv[layer, 0:1, :] = sums[2 * layer, 5:6, :]
                qv[layer, 1:2, :] = sums[2 * layer, 7:8, :]
                for j in range(4):
                    up[layer : layer + 1, j * WIDTH : (j + 1) * WIDTH] = sums[2 * layer + 1, 5 + j : 6 + j, :]
            bias[...] = sums[SECTIONS, 4:5, :]
            gain[0] = sums[SECTIONS, 0:2, :]
            shift[0] = sums[SECTIONS, 2:4, :]
            for copy in small:
                copy.start()
    for i in range(count - depth, count):
        store(i).wait()
    for copy in small:
        copy.wait()
    move_grad.wait()


def widen(reduced, sums, grad):
    any_space = pl.BlockSpec(memory_space=pl.ANY)
    rows, depth = 1024, 3
    dma = pltpu.SemaphoreType.DMA
    shapes = [(2, 2, WIDTH), (2, FF), (1, WIDTH), (1, 2, WIDTH), (1, 2, WIDTH)]
    return pl.pallas_call(
        widen_kernel,
        name="widen",
        out_shape=[
            jax.ShapeDtypeStruct((1, WIDTH, FF), F32),
            jax.ShapeDtypeStruct((2 * WIDTH, WIDTH), F32),
            *[jax.ShapeDtypeStruct(shape, F32) for shape in shapes],
            jax.ShapeDtypeStruct((SLOTS, LEN, 256), BF16),
        ],
        in_specs=[any_space] * 3,
        out_specs=[any_space] * 8,
        scratch_shapes=[
            pltpu.VMEM((depth, rows, WIDTH), BF16),
            pltpu.VMEM((depth, rows, WIDTH), F32),
            pltpu.VMEM((SECTIONS + 1, 16, WIDTH), F32),
            *[pltpu.VMEM(shape, F32) for shape in shapes],
            dma((depth,)), dma((depth,)), dma((7,)),
        ],
        compiler_params=pltpu.CompilerParams(vmem_limit_bytes=63 * 2**20),
    )(reduced, sums, grad)


def on_device(
    block_input, cotangent, group_ids, live_count, group_scale, norm_gain, norm_bias, first_weight,
    qv_bias, up_bias, down_weight, out_bias,
):
    reduced, sums, grad = mega(
        block_input, cotangent, group_ids, live_count, group_scale, norm_gain, norm_bias,
        qv_bias, up_bias, out_bias, first_weight, down_weight,
    )
    first_grad, down_grad, qv_grad, up_grad, bias_grad, gain_grad, shift_grad, input_grad = widen(reduced, sums, grad)
    return input_grad, first_grad, down_grad, qv_grad, up_grad, bias_grad, gain_grad, shift_grad


def solution(mesh):
    in_specs = (
        P("dp", None, None),
        P("dp", None, None),
        P("dp"),
        P("dp"),
        P(),
        P("section", None, None),
        P("section", None, None),
        P("section", None, None),
        P(),
        P(),
        P("section", None),
        P("section", None),
    )
    out_specs = (
        P("dp", None, "section"),
        P("section", None, None),
        P("section", None),
        P(),
        P(),
        P("section", None),
        P("section", None, None),
        P("section", None, None),
    )
    return jax.shard_map(on_device, mesh=mesh, in_specs=in_specs, out_specs=out_specs, check_vma=False)
```

```python
import math

import jax
import jax.numpy as jnp
from jax import lax
from jax.experimental import pallas as pl
from jax.experimental.pallas import tpu as pltpu
from jax.sharding import PartitionSpec as P

MESH = pl.DeviceIdType.MESH
BF16 = jnp.bfloat16
F32 = jnp.float32

WIDTH = 1024
FF = 4096
LEN = 128
SLOTS = 4
ROWS = SLOTS * LEN
PAIRS = 8
SECTIONS = 4
NORM_EPS = 1e-05
GELU_C = math.sqrt(2.0 / math.pi)
CHUNKS = 8
ORDER = (7, 0, 3, 8, 4, 5, 6, 2, 9)
OFFSET_FEED = (0, 0, 1, 3, 4, 5, 6, 8, 10, 12)
OFFSET_ATTEND = (0, 0, 1, 3, 4, 5, 6, 8, 11, 14)


def device(section, x, y, core):
    return (section, x * 8 + y * 2 + core)


def place():
    at = lax.axis_index("dp")
    return lax.axis_index("section"), at // 8, (at // 2) % 4, at % 2


def greet(section, x, y, core, here):
    barrier = pltpu.get_barrier_semaphore()
    others = [device(section, x, y, 1 - core), device(section + 1 - 2 * (section % 2), x, y, core)]
    for d in (1, 2, 3):
        others.append(device(section, (x + d) % 4, y, core))
        others.append(device(section, x, (y + d) % 4, core))
    for other in others:
        pl.semaphore_signal(barrier, inc=1, device_id=other, device_id_type=MESH)

    @pl.when(section < 2)
    def _():
        for high in (2, 3):
            pl.semaphore_signal(barrier, inc=1, device_id=device(high, x, y, core), device_id_type=MESH)

    def wait():
        pl.semaphore_wait(barrier, jnp.where(section < 2, 8, 10))

        @pl.when(section >= 2)
        def _():
            for low in (0, 1):
                pl.semaphore_signal(here, inc=1, device_id=device(low, x, y, core), device_id_type=MESH)

    return wait


def remote(source, target, send_sem, recv_sem, to):
    return pltpu.make_async_remote_copy(
        src_ref=source,
        dst_ref=target,
        send_sem=send_sem,
        recv_sem=recv_sem,
        device_id=to,
        device_id_type=MESH,
    )


def dot(a, b):
    return jnp.dot(a, b, preferred_element_type=F32)


def dot_nt(a, b):
    return lax.dot_general(a, b, (((1,), (1,)), ((), ())), preferred_element_type=F32)


def dot_tn(a, b):
    return lax.dot_general(a, b, (((0,), (0,)), ((), ())), preferred_element_type=F32)


def normalize(entries):
    average = jnp.mean(entries, axis=-1, keepdims=True)
    centered = entries - average
    inverse = lax.rsqrt(jnp.mean(centered * centered, axis=-1, keepdims=True) + NORM_EPS)
    return centered * inverse, inverse


def norm_backward(grad_out, unit, inverse, gain):
    scaled = grad_out * gain
    middle = jnp.mean(scaled, axis=-1, keepdims=True)
    along = jnp.mean(scaled * unit, axis=-1, keepdims=True)
    return inverse * (scaled - middle - unit * along)


def column_sum(entries):
    return jnp.sum(entries, axis=0, keepdims=True)


def mega_kernel(
    block_hbm, cot_hbm, group_hbm, live_hbm, scale_hbm, gains_hbm, shifts_hbm, qv_hbm, up_hbm, bias_hbm, w1_hbm, down_hbm,
    out_hbm, small_hbm, grad_hbm,
    group_ids, live_count, group_scale, gains, shifts, qv_bias, up_bias, out_bias,
    w1, buffer, w2t, ops, other, units, stats, r_in, r_out, g_in, g_out, wide, small, vectors,
    z, sx, sy, ss, sums,
    load_sem, down_send, down_recv, ag_send, ag_recv,
    fwd_send, fwd_recv, bwd_send, bwd_recv, ig_send, ig_recv, token, here,
    swap_send, swap_recv, ready, ring_send, ring_recv, z_send, z_recv, export_send, export_recv, own_sem, last_send, last_recv,
    tiny_send, tiny_recv,
):
    section, x, y, core = place()
    parity = section % 2
    layer = section // 2
    last = section == SECTIONS - 1
    first = section == 0
    sibling = device(section, x, y, 1 - core)
    w1t, w2 = buffer.at[pl.ds(0, FF)], buffer.at[pl.ds(FF, FF)]

    meet = greet(section, x, y, core, here)
    load_w1 = pltpu.make_async_copy(w1_hbm.at[0], w1, load_sem.at[0])
    load_own = pltpu.make_async_copy(down_hbm, w2.at[pl.ds(2048, 2048)], load_sem.at[1])
    load_block = pltpu.make_async_copy(block_hbm, r_in, load_sem.at[2])
    load_cot = pltpu.make_async_copy(cot_hbm, g_in, load_sem.at[3])

    pieces = [
        (gains_hbm, gains), (shifts_hbm, shifts), (bias_hbm, out_bias), (qv_hbm, qv_bias), (up_hbm, up_bias),
        (group_hbm, group_ids), (live_hbm, live_count), (scale_hbm, group_scale),
    ]
    load_pieces = [pltpu.make_async_copy(*piece, load_sem.at[4 + j]) for j, piece in enumerate(pieces)]

    @pl.when(first)
    def _():
        load_block.start()

    for copy in load_pieces:
        copy.start()
    load_w1.start()

    @pl.when(parity == 1)
    def _():
        load_own.start()

    @pl.when(last)
    def _():
        load_cot.start()

    meet()

    left, right = pl.ds(0, 512), pl.ds(512, 512)
    both = [(h, d) for h in (0, 1) for d in (0, 1)]

    def peer(axis, d):
        if axis == 0:
            return device(section, (x + d) % 4, y, core)
        return device(section, x, (y + d) % 4, core)

    def arrived_rows(rows, sem):
        piece = buffer.at[pl.ds(0, rows)]
        pltpu.make_async_copy(piece, piece, sem).wait()

    def down_rows(h, p, major, minor, n):
        row = h * 1024 + core * 512 + p * 256 + major * 64 + minor * 16
        return pl.ds(pl.multiple_of(row, 16), n)

    def down_spot(h):
        return (y, x) if h == 0 else (x, y)

    def down_copy(p, h):
        rows = down_rows(h, p, *down_spot(h), 16)
        return remote(
            down_hbm.at[rows], w2.at[rows], down_send, down_recv.at[p], device((section + 1) % 4, x, y, core)
        )

    def down_near(p, h, d):
        rows = down_rows(h, p, *down_spot(h), 16)
        return remote(w2.at[rows], w2.at[rows], ag_send, ag_recv.at[0, p], peer(h, d))

    def down_ring(p, h, d):
        rows = down_rows(h, p, down_spot(h)[0], 0, 64)
        return remote(w2.at[rows], w2.at[rows], ag_send, ag_recv.at[1, p], peer(1 - h, 1 - 2 * d))

    def down_pass(p, h, d):
        step = 1 - 2 * d
        rows = down_rows(h, p, (down_spot(h)[0] - step) % 4, 0, 64)
        piece = w2.at[rows, left if d == 0 else right]
        return remote(piece, piece, ag_send, ag_recv.at[2, p], peer(1 - h, step))

    def down_share(p, h, d):
        rows = down_rows(h, p, (down_spot(h)[0] + d) % 4, 0, 64)
        return remote(w2.at[rows], w2.at[rows], ag_send, ag_recv.at[3, 0], sibling)

    @pl.when(parity == 0)
    def _():
        for p in (0, 1):
            for h in (0, 1):
                down_copy(p, h).start()

    for copy in load_pieces:
        copy.wait()

    @pl.when(parity == 0)
    def _():
        vectors[5:6, :] = qv_bias[layer, 0:1, :]
        vectors[6:7, :] = jnp.zeros((1, WIDTH), F32)
        vectors[7:8, :] = qv_bias[layer, 1:2, :]

    @pl.when(parity == 1)
    def _():
        for j in range(4):
            vectors[5 + j : 6 + j, :] = up_bias[pl.ds(layer, 1), j * WIDTH : (j + 1) * WIDTH]

    def sequence_weight(micro):
        group = group_ids[micro]
        chosen = jnp.float32(0.0)
        for label in range(8):
            chosen = jnp.where(group == label, group_scale[label], chosen)
        weight = jnp.where(micro < live_count[0], chosen, 0.0)
        return jnp.where(last, weight, 1.0)

    small[...] = jnp.zeros_like(small)

    def gather_start():
        for p in (0, 1):
            arrived_rows(32, down_recv.at[p])
            for h in (0, 1):
                for d in (1, 3, 2):
                    down_near(p, h, d).start()
        for p in (0, 1):
            arrived_rows(96, ag_recv.at[0, p])
            for h, d in both:
                down_ring(p, h, d).start()
            for h in (0, 1):
                down_share(p, h, 0).start()
        gather_pass(0)
        gather_pass(1)
        load_own.wait()

    def gather_pass(p):
        arrived_rows(256, ag_recv.at[1, p])
        for h, d in both:
            down_pass(p, h, d).start()
        for h in (0, 1):
            down_share(p, h, 1).start()
            down_share(p, h, 3).start()

    def gather_end():
        for p in (0, 1):
            arrived_rows(128, ag_recv.at[2, p])
            for h in (0, 1):
                down_share(p, h, 2).start()
        arrived_rows(1024, ag_recv.at[3, 0])

    pl.when(parity == 1)(gather_start)
    pl.when(last)(gather_end)

    load_w1.wait()

    @pl.when(first)
    def _():
        load_block.wait()

    @pl.when(last)
    def _():
        load_cot.wait()

    def fwd_copy(micro):
        return remote(
            r_out.at[micro], r_in.at[micro], fwd_send.at[micro], fwd_recv.at[micro],
            device((section + 1) % 4, x, y, core),
        )

    def bwd_copy(micro):
        return remote(
            g_out.at[micro], g_in.at[micro], bwd_send.at[micro], bwd_recv.at[micro],
            device((section + 3) % 4, x, y, core),
        )

    def ig_copy(micro, d):
        to = (section + d) % 4
        return remote(
            g_out.at[micro, :, pl.ds(d * 256, 256)], grad_hbm.at[micro], ig_send.at[micro, d], ig_recv.at[micro],
            device(to, x, y, core),
        )

    def ig_own(micro):
        return pltpu.make_async_copy(g_out.at[micro, :, pl.ds(0, 256)], grad_hbm.at[micro], ig_send.at[micro, 0])

    lanes = lax.broadcasted_iota(jnp.int32, (LEN, 128), 1)
    low_lanes = lanes < 64

    def two_heads(entries):
        zero = jnp.zeros_like(entries)
        return jnp.concatenate([jnp.where(low_lanes, entries, zero), jnp.where(low_lanes, zero, entries)], axis=0)

    def transposes():
        def one(j, carry):
            cut = pl.ds(pl.multiple_of(j * 256, 256), 256)
            w1t[cut, :] = w1[:, cut].T
            return carry

        lax.fori_loop(0, 16, one, 0)

        @pl.when(parity == 1)
        def _():
            def two(j, carry):
                cut = pl.ds(pl.multiple_of(j * 256, 256), 256)
                w2t[:, cut] = w2[cut, :].T
                return carry

            lax.fori_loop(0, 16, two, 0)

    def attention_forward(micro):
        normed = ops[0, micro]
        for j in range(3):
            part = dot(normed, w1[:, j * WIDTH : (j + 1) * WIDTH]) + vectors[5 + j : 6 + j, :]
            ops[6 + j, micro] = part.astype(BF16)
        rows = lax.broadcasted_iota(jnp.int32, (LEN, LEN), 0)
        columns = lax.broadcasted_iota(jnp.int32, (LEN, LEN), 1)
        causal = rows <= columns
        for p in range(PAIRS):
            cut = slice(p * 128, (p + 1) * 128)
            query, key, value = (ops[6 + j, micro, :, cut] for j in range(3))
            scores = dot_nt(two_heads(key), query) * 0.125
            parts = []
            for head in (0, 1):
                part = jnp.where(causal, scores[head * LEN : (head + 1) * LEN], -1e9)
                powers = jnp.exp(part - jnp.max(part, axis=0, keepdims=True))
                part = (powers / jnp.sum(powers, axis=0, keepdims=True)).astype(BF16)
                ops[3 + p // 4, micro, :, (p % 4 * 2 + head) * 128 : (p % 4 * 2 + head + 1) * 128] = part
                parts.append(part)
            ops[2, micro, :, cut] = dot_tn(jnp.concatenate(parts, axis=0), two_heads(value)).astype(BF16)

        @pl.when(section == 2)
        def _():
            wide[...] = dot(ops[2, micro], w1t[3 * WIDTH :, :]) + out_bias[...]

        @pl.when(section != 2)
        def _():
            wide[...] = dot_nt(ops[2, micro], w1[:, 3 * WIDTH :]) + out_bias[...]

    def feed_forward(micro):
        normed = ops[0, micro]
        branch = out_bias[...]
        def product(j):
            b, cut = j * 256 // WIDTH, slice(j * 256 % WIDTH, j * 256 % WIDTH + 256)
            return dot(normed, w1[:, j * 256 : (j + 1) * 256]) + vectors[5 + b : 6 + b, cut]

        def gate(j, hidden):
            b, cut = j * 256 // WIDTH, slice(j * 256 % WIDTH, j * 256 % WIDTH + 256)
            square = hidden * hidden
            above = 0.5 + 0.5 * jnp.tanh(hidden * (GELU_C + (GELU_C * 0.044715) * square))
            active = hidden * above
            slope = above + (active - active * above) * (2.0 * GELU_C + (6.0 * GELU_C * 0.044715) * square)
            ops[6 + b, micro, :, cut] = slope.astype(BF16)
            ops[2 + b, micro, :, cut] = active.astype(BF16)

        order = (8, 9, 10, 11, 12, 13, 14, 15, 0, 1, 2, 3, 4, 5, 6, 7)
        hidden = product(order[0])
        for step, j in enumerate(order):
            ahead = product(order[step + 1]) if step + 1 < len(order) else None
            gate(j, hidden)
            hidden = ahead
        branch = out_bias[...]
        for j in (2, 3, 0, 1):
            if j == 0:
                pl.when((micro == 0) & (section == 1))(gather_end)
            branch = branch + dot(ops[2 + j, micro], w2[j * WIDTH : (j + 1) * WIDTH, :])
        wide[...] = branch

    def attention_backward(micro):
        ops[9, micro] = dot(ops[1, micro], w1[:, 3 * WIDTH :]).astype(BF16)
        for p in range(PAIRS):
            cut = slice(p * 128, (p + 1) * 128)
            query, key, value = (ops[6 + j, micro, :, cut] for j in range(3))
            grad = ops[9, micro, :, cut]
            parts = [ops[3 + p // 4, micro, :, (p % 4 * 2 + h) * 128 : (p % 4 * 2 + h + 1) * 128] for h in (0, 1)]
            grad_weights = dot_nt(two_heads(value), grad)
            grad_scores = []
            for head in (0, 1):
                part = parts[head].astype(F32)
                product = part * grad_weights[head * LEN : (head + 1) * LEN]
                grad_scores.append((product - part * jnp.sum(product, axis=0, keepdims=True)).astype(BF16))
            grad_scores = jnp.concatenate(grad_scores, axis=0)
            grad_query = dot_tn(grad_scores, two_heads(key)) * 0.125
            both_heads = dot(grad_scores, query) * 0.125
            grad_key = jnp.where(low_lanes, both_heads[:LEN], both_heads[LEN:])
            both_heads = dot(jnp.concatenate(parts, axis=0), grad)
            grad_value = jnp.where(low_lanes, both_heads[:LEN], both_heads[LEN:])
            for j, part in enumerate((grad_query, grad_key, grad_value)):
                ops[6 + j, micro, :, cut] = part.astype(BF16)
        total = jnp.zeros((LEN, WIDTH), F32)
        for j in range(3):
            part = ops[6 + j, micro]
            total = total + dot(part, w1t[j * WIDTH : (j + 1) * WIDTH, :])
        wide[...] = total

    def feed_backward(micro):
        grad_branch = ops[1, micro]
        total = jnp.zeros((LEN, WIDTH), F32)
        for j in range(4):
            grad = dot(grad_branch, w2t[:, j * WIDTH : (j + 1) * WIDTH])
            grad = (grad * ops[6 + j, micro].astype(F32)).astype(BF16)
            ops[6 + j, micro] = grad
            total = total + dot(grad, w1t[j * WIDTH : (j + 1) * WIDTH, :])
        wide[...] = total

    def swap(block, count, micro, group):
        piece = pl.ds(block, count)
        return remote(ops.at[piece, micro], other.at[piece, micro], swap_send, swap_recv.at[group], sibling)

    def forward(micro):
        @pl.when(jnp.logical_not(first))
        def _():
            fwd_copy(micro).wait_recv()

        residual = r_in[micro].astype(F32)
        mean = jnp.mean(residual, axis=-1, keepdims=True)
        centered = residual - mean
        inverse = lax.rsqrt(jnp.mean(centered * centered, axis=-1, keepdims=True) + NORM_EPS)
        stats[micro, :, 0:1] = mean
        stats[micro, :, 1:2] = inverse
        ops[0, micro] = (centered * inverse * gains[0, 0:1, :] + shifts[0, 0:1, :]).astype(BF16)
        pl.when(jnp.logical_not(last))(lambda: swap(0, 1, micro, 0).start())

        @pl.when(parity == 0)
        def _():
            attention_forward(micro)

        @pl.when(parity == 1)
        def _():
            feed_forward(micro)

        unit, inverse = normalize(wide[...])

        @pl.when(jnp.logical_not(last))
        def _():
            after = r_in[micro].astype(F32) + unit * gains[0, 1:2, :] + shifts[0, 1:2, :]
            r_out[micro] = after.astype(BF16)
            leads = (section == 1) & (core == 1)
            follows = (section == 1) & (core == 0)
            pl.when(micro > jnp.where(leads, 1, 0))(lambda: fwd_copy(micro - 1).wait_send())
            pl.when((section < 2) & (micro == 0))(lambda: pl.semaphore_wait(here, 2))
            pl.when(follows & (micro == 0))(lambda: pl.semaphore_wait(token, 1))
            fwd_copy(micro).start()

            @pl.when(leads & (micro == 0))
            def _():
                fwd_copy(micro).wait_send()
                pl.semaphore_signal(token, inc=1, device_id=sibling, device_id_type=MESH)

        units[micro] = unit.astype(BF16)
        stats[micro, :, 2:3] = inverse
        pl.when(parity == 0)(lambda: swap(2, 1, micro, 0).start())
        pl.when(section == 1)(lambda: swap(2, 4, micro, 0).start())

    def backward(micro):
        @pl.when(jnp.logical_not(last))
        def _():
            bwd_copy(micro).wait_recv()

        weight = sequence_weight(micro)
        incoming = g_in[micro].astype(F32) * weight
        unit = units[micro].astype(F32)
        ops[1, micro] = norm_backward(incoming, unit, stats[micro, :, 2:3], gains[0, 1:2, :]).astype(BF16)
        pl.when(jnp.logical_not(last))(lambda: swap(1, 1, micro, 0).start())

        @pl.when(parity == 0)
        def _():
            attention_backward(micro)

        @pl.when(parity == 1)
        def _():
            feed_backward(micro)

        inverse = stats[micro, :, 1:2]
        unit = (r_in[micro].astype(F32) - stats[micro, :, 0:1]) * inverse
        incoming = g_in[micro].astype(F32) * weight
        grad = incoming + norm_backward(wide[...], unit, inverse, gains[0, 0:1, :])
        g_out[micro] = grad.astype(BF16)

        @pl.when(jnp.logical_not(first))
        def _():
            bwd_copy(micro).start()

        @pl.when(first)
        def _():
            ig_own(micro).start()
            for d in (1, 2, 3):
                ig_copy(micro, d).start()

        r_out[micro] = wide[...].astype(BF16)
        pl.when(parity == 0)(lambda: swap(6, 3, micro, 1).start())
        pl.when(section == 1)(lambda: swap(6, 4, micro, 1).start())

    def row_sums(micro):
        weight = sequence_weight(micro)
        unit = (r_in[micro].astype(F32) - stats[micro, :, 0:1]) * stats[micro, :, 1:2]
        grad = r_out[micro].astype(F32)
        small[0:1, :] += column_sum(grad * unit)
        small[2:3, :] += column_sum(grad)
        incoming = g_in[micro].astype(F32) * weight
        small[1:2, :] += column_sum(incoming * units[micro].astype(F32))
        small[3:4, :] += column_sum(incoming)
        small[4:5, :] += column_sum(ops[1, micro].astype(F32))
        for j in range(4):
            small[5 + j : 6 + j, :] += column_sum(ops[6 + j, micro].astype(F32))

    turn_at = jnp.where(section >= 2, 0, SLOTS)

    def step(t, carry):
        is_forward = jnp.where(last, (t + 1) % 2, jnp.where(t < SLOTS, 1, 0))
        micro = jnp.where(last, t // 2, t % SLOTS)

        @pl.when((t == SLOTS) & jnp.logical_not(last))
        def _():
            fwd_copy(SLOTS - 1).wait_send()

        @pl.when(t == turn_at)
        def _():
            transposes()

        @pl.when(is_forward == 1)
        def _():
            forward(micro)

        @pl.when(is_forward == 0)
        def _():
            backward(micro)

        return carry

    lax.fori_loop(0, 2 * SLOTS, step, 0)

    @pl.when(last)
    def _():
        for block, count, group in ((0, 6, 0), (6, 4, 1)):
            piece = pl.ds(block, count)
            remote(ops.at[piece], other.at[piece], swap_send, swap_recv.at[group], sibling).start()

    def spot(h):
        return (x, y) if h == 0 else (y, x)

    sends_out = section == 1
    takes_in = section == 2

    def chunk(q):
        late = jnp.where(takes_in, jnp.where(q == 6, 2, q - 4), jnp.where(q == 4, 1, 0))
        return jnp.where(parity == 1, q, jnp.where(q < 4, 7 - q, late))

    def exported(q):
        return sends_out & (q == 0)

    def imported(q):
        return takes_in & (q == 6)

    def multiplies(q):
        return (parity == 1) | (q < 4)

    def reduces(q):
        return (multiplies(q) & jnp.logical_not(exported(q))) | imported(q)

    def hands_over(q):
        return ((section == 3) & (q < 2)) | (sends_out & (q == 1)) | imported(q)

    def takes_over(q):
        return ((section == 0) & ((q == 4) | (q == 6))) | (takes_in & ((q == 4) | (q == 5)))

    def gathers(q):
        return ((parity == 1) & (q >= 2)) | ((parity == 0) & (q < 4)) | takes_over(q)

    def at(q, h, b1, b2, n):
        row = chunk(q) * 1024 + core * 512 + h * 256 + b1 * 64 + b2 * 16
        return pl.ds(pl.multiple_of(row, 16), n)

    def export_copy():
        return remote(
            buffer.at[pl.ds(pl.multiple_of(core * 512, 512), 512)],
            buffer.at[pl.ds(pl.multiple_of(2048 + core * 512, 512), 512)],
            export_send, export_recv, device((section + 1) % 4, x, y, core),
        )

    def out_at(q, h, b1, b2, n):
        k = chunk(q)
        k = jnp.where((parity == 1) | (k >= 4), k - 2, k)
        row = k * 1024 + core * 512 + h * 256 + b1 * 64 + b2 * 16
        return pl.ds(pl.multiple_of(row, 16), n)

    def ring(stage, q, source, target, to):
        return remote(source, target, ring_send.at[stage // 4], ring_recv.at[stage, q], to)

    def land_one(q, h, d):
        return w1.at[pl.ds((q * 2 + h) * 64, 64), pl.ds(d * 512, 512)]

    def land_two(q, h, d):
        return w2t.at[pl.ds((q * 2 + h) * 64, 64), pl.ds(d * 1024, 1024)]

    def land_three(q, h, d):
        return w2t.at[pl.ds((q * 2 + h) * 64 + 16, 16), pl.ds(2048 + d * 1024, 512)]

    def land_four(q, h, d):
        return w2t.at[pl.ds((q * 2 + h) * 64, 16), pl.ds(2048 + d * 1024, 1024)]

    def rs_one(q, h, d):
        p1, _ = spot(h)
        rows = at(q, h, (p1 + 2) % 4, 0, 64)
        return ring(0, q, buffer.at[rows, left if d == 0 else right], land_one(q, h, d), peer(h, 1 - 2 * d))

    def rs_two(q, h, d):
        p1, _ = spot(h)
        step = 1 - 2 * d
        return ring(1, q, buffer.at[at(q, h, (p1 + step) % 4, 0, 64)], land_two(q, h, d), peer(h, step))

    def rs_three(q, h, d):
        p1, p2 = spot(h)
        rows = at(q, h, p1, (p2 + 2) % 4, 16)
        return ring(2, q, buffer.at[rows, left if d == 0 else right], land_three(q, h, d), peer(1 - h, 1 - 2 * d))

    def rs_four(q, h, d):
        p1, p2 = spot(h)
        step = 1 - 2 * d
        return ring(3, q, buffer.at[at(q, h, p1, (p2 + step) % 4, 16)], land_four(q, h, d), peer(1 - h, step))

    def z_copy(q, h):
        p1, p2 = spot(h)
        to = jnp.where(takes_in, 0, section - 1)
        slot = jnp.where(takes_in, 0, chunk(q))
        return remote(
            buffer.at[at(q, h, p1, p2, 16)], z.at[slot, h], z_send, z_recv.at[slot, h], device(to, x, y, core)
        )

    def z_arrival(q, h):
        return remote(z.at[chunk(q), h], z.at[chunk(q), h], z_send, z_recv.at[chunk(q), h], sibling)

    def own_copy(q, h):
        p1, p2 = spot(h)
        return pltpu.make_async_copy(
            buffer.at[at(q, h, p1, p2, 16)], out_hbm.at[out_at(q, h, p1, p2, 16)], own_sem.at[q]
        )

    def ag_one(q, h, d):
        p1, p2 = spot(h)
        target = out_hbm.at[out_at(q, h, p1, p2, 16)]
        return ring(4, q, buffer.at[at(q, h, p1, p2, 16)], target, peer(1 - h, 1 - 2 * d))

    def ag_two(q, h, d):
        p1, p2 = spot(h)
        step = 1 - 2 * d
        piece = out_hbm.at[out_at(q, h, p1, (p2 - step) % 4, 16), left if d == 0 else right]
        return ring(5, q, piece, piece, peer(1 - h, step))

    def ag_three(q, h, d):
        p1, _ = spot(h)
        piece = out_hbm.at[out_at(q, h, p1, 0, 64)]
        return ring(6, q, piece, piece, peer(h, 1 - 2 * d))

    def ag_four(q, h, d):
        p1, _ = spot(h)
        step = 1 - 2 * d
        piece = out_hbm.at[out_at(q, h, (p1 - step) % 4, 0, 64), left if d == 0 else right]
        return ring(7, q, piece, piece, peer(h, step))

    def last_copy(q, h, d):
        p1, _ = spot(h)
        piece = out_hbm.at[out_at(q, h, (p1 + d) % 4, 0, 64)]
        return remote(piece, piece, last_send, last_recv, sibling)

    def swapped(group):
        counts = ((3, 6), (3, 4))[group]
        pl.when(parity == 0)(lambda: arrived_rows(counts[0] * ROWS, swap_recv.at[group]))
        pl.when(parity == 1)(lambda: arrived_rows(counts[1] * ROWS, swap_recv.at[group]))

    def multiply(q):
        k = chunk(q)
        feed_down = (parity == 1) & (k < 4)
        from_context = (parity == 0) & (k == 7)
        a = jnp.where(feed_down, 2 + k, jnp.where(from_context, 1, 0))
        b = jnp.where(feed_down, 1, jnp.where(from_context, 2, 2 + k))
        pl.when(q == 0)(lambda: swapped(0))
        pl.when(q == 1 + 3 * parity)(lambda: swapped(1))
        right_own, right_other = ops[b].reshape(ROWS, WIDTH), other[b].reshape(ROWS, WIDTH)
        for cut in range(2):
            columns = pl.ds(pl.multiple_of(core * 512 + cut * 256, 256), 256)
            product = dot_tn(ops[a, :, :, columns].reshape(ROWS, 256), right_own)
            product = product + dot_tn(other[a, :, :, columns].reshape(ROWS, 256), right_other)
            buffer[pl.ds(pl.multiple_of(k * 1024 + core * 512 + cut * 256, 256), 256), :] = product.astype(BF16)

    def stage_0(q):
        pl.when(multiplies(q))(lambda: multiply(q))
        pl.when(exported(q))(lambda: export_copy().start())
        pl.when(imported(q))(lambda: export_copy().wait_recv())

        @pl.when(reduces(q))
        def _():
            pl.when(q == jnp.where(sends_out, 1, 0))(lambda: pl.semaphore_wait(ready, 4))
            for h, d in both:
                rs_one(q, h, d).start()

    def stage_2(q):
        arrived_rows(128, ring_recv.at[0, q])
        for h, d in both:
            p1, _ = spot(h)
            rows = at(q, h, (p1 + 1 - 2 * d) % 4, 0, 64)
            cut = left if d == 0 else right
            buffer[rows, cut] = buffer[rows, cut] + land_one(q, h, d)[...]
            rs_two(q, h, d).start()

    def stage_3(q):
        arrived_rows(256, ring_recv.at[1, q])
        for h in (0, 1):
            p1, _ = spot(h)
            rows = at(q, h, p1, 0, 64)
            total = buffer[rows, :].astype(F32) + land_two(q, h, 0)[...].astype(F32) + land_two(q, h, 1)[...].astype(F32)
            buffer[rows, :] = total.astype(BF16)
            for d in (0, 1):
                rs_three(q, h, d).start()

    def stage_4(q):
        arrived_rows(32, ring_recv.at[2, q])
        for h, d in both:
            p1, p2 = spot(h)
            rows = at(q, h, p1, (p2 + 1 - 2 * d) % 4, 16)
            cut = left if d == 0 else right
            buffer[rows, cut] = buffer[rows, cut] + land_three(q, h, d)[...]
            rs_four(q, h, d).start()

    def stage_5(q):
        @pl.when(reduces(q))
        def _():
            arrived_rows(64, ring_recv.at[3, q])
            for h in (0, 1):
                p1, p2 = spot(h)
                rows = at(q, h, p1, p2, 16)
                arrival = land_four(q, h, 0)[...].astype(F32) + land_four(q, h, 1)[...].astype(F32)
                buffer[rows, :] = (buffer[rows, :].astype(F32) + arrival).astype(BF16)

        @pl.when(hands_over(q))
        def _():
            for h in (0, 1):
                z_copy(q, h).start()

        @pl.when(takes_over(q))
        def _():
            for h in (0, 1):
                p1, p2 = spot(h)
                z_arrival(q, h).wait_recv()
                buffer[at(q, h, p1, p2, 16), :] = z[chunk(q), h]

        @pl.when(gathers(q))
        def _():
            for h in (0, 1):
                own_copy(q, h).start()
                for d in (0, 1):
                    ag_one(q, h, d).start()

    def stage_6(q):
        arrived_rows(64, ring_recv.at[4, q])
        for h, d in both:
            ag_two(q, h, d).start()
        arrived_rows(32, own_sem.at[q])

    def stage_7(q):
        arrived_rows(32, ring_recv.at[5, q])
        for h, d in both:
            ag_three(q, h, d).start()
        for h in (0, 1):
            last_copy(q, h, 0).start()

    def stage_8(q):
        arrived_rows(256, ring_recv.at[6, q])
        for h, d in both:
            ag_four(q, h, d).start()
        for h in (0, 1):
            last_copy(q, h, 1).start()
            last_copy(q, h, 3).start()

    def stage_9(q):
        arrived_rows(128, ring_recv.at[7, q])
        for h in (0, 1):
            last_copy(q, h, 2).start()

    stages = [stage_0, None, stage_2, stage_3, stage_4, stage_5, stage_6, stage_7, stage_8, stage_9]

    def tiny(phase, d):
        if phase == 0:
            return remote(small, sx.at[d - 1], tiny_send.at[d - 1], tiny_recv.at[d - 1], peer(0, d))
        if phase == 1:
            return remote(sums.at[0], sy.at[d - 1], tiny_send.at[d + 2], tiny_recv.at[d + 2], peer(1, d))
        if phase == 2:
            return remote(sums.at[1], ss, tiny_send.at[6], tiny_recv.at[6], sibling)
        return remote(
            sums.at[2], small_hbm.at[section], tiny_send.at[6 + d], tiny_recv.at[6 + d],
            device((section + d) % 4, x, y, core),
        )

    keep_own = [
        pltpu.make_async_copy(sums.at[2], small_hbm.at[section], tiny_send.at[10]),
        pltpu.make_async_copy(sums.at[2], small_hbm.at[SECTIONS], tiny_send.at[11]),
    ]

    def tiny_0():
        for d in (1, 2, 3):
            tiny(0, d).start()

    def tiny_1():
        for d in (1, 2, 3):
            tiny(0, d).wait()
        sums[0] = (small[...] + sx[0]) + (sx[1] + sx[2])
        for d in (1, 2, 3):
            tiny(1, d).start()

    def tiny_2():
        for d in (1, 2, 3):
            tiny(1, d).wait()
        sums[1] = (sums[0] + sy[0]) + (sy[1] + sy[2])
        tiny(2, 1).start()

    def tiny_3():
        tiny(2, 1).wait()
        sums[2] = sums[1] + ss[...]
        for copy in keep_own:
            copy.start()
        for d in (1, 2, 3):
            tiny(3, d).start()

    pl.when(parity == 1)(lambda: arrived_rows(1984, ag_send))
    for axis in (0, 1):
        for d in (1, 3):
            pl.semaphore_signal(ready, inc=1, device_id=peer(axis, d), device_id_type=MESH)

    def slot(t, carry):
        for number, turn in enumerate((tiny_0, tiny_1, tiny_2, tiny_3)):
            pl.when(t == 2 + SLOTS + number)(turn)
        for s in ORDER:
            k = t - jnp.where(parity == 1, OFFSET_FEED[s], OFFSET_ATTEND[s])
            live = (k >= 0) & (k < CHUNKS)
            if s == 0:
                live = live & (multiplies(k) | imported(k))
            elif s < 5:
                live = live & reduces(k)
            elif s == 5:
                live = live & (reduces(k) | gathers(k))
            else:
                live = live & gathers(k)
            pl.when(live)(lambda turn=stages[s], k=k: turn(k))
        pl.when((t >= 1) & (t < 1 + SLOTS))(lambda: row_sums(t - 1))
        return carry

    lax.fori_loop(0, CHUNKS + max(OFFSET_FEED + OFFSET_ATTEND), slot, 0)

    for d in (1, 2, 3):
        tiny(3, d).wait()
    for copy in keep_own:
        copy.wait()

    def sent(rows, sem):
        arrived_rows(rows, sem)

    pl.when(parity == 1)(lambda: sent(10 * ROWS, swap_send))
    pl.when(parity == 0)(lambda: sent(6 * ROWS, swap_send))
    pl.when(parity == 0)(lambda: sent(64, down_send))
    for number, (ring_count, z_count) in enumerate(((4, 0), (7, 1), (5, 1), (8, 2))):
        @pl.when(section == number)
        def _():
            sent(ring_count * 480, ring_send.at[0])
            if z_count:
                sent(z_count * 32, z_send)

    pl.when(sends_out)(lambda: export_copy().wait_send())
    sent(6 * 480, ring_send.at[1])
    sent(6 * 512, last_send)
    sent(6 * 512, last_recv)

    @pl.when(jnp.logical_not(first))
    def _():
        for micro in range(SLOTS):
            bwd_copy(micro).wait_send()
            ig_copy(micro, 1).wait_recv()

    @pl.when(first)
    def _():
        for micro in range(SLOTS):
            ig_own(micro).wait()
            for d in (1, 2, 3):
                ig_copy(micro, d).wait_send()


def mega(block, cot, group_ids, live_count, group_scale, gains, shifts, qv_bias, up_bias, out_bias, w1, down):
    any_space = pl.BlockSpec(memory_space=pl.ANY)
    dma = pltpu.SemaphoreType.DMA
    return pl.pallas_call(
        mega_kernel,
        name="mega",
        out_shape=[
            jax.ShapeDtypeStruct((6 * 1024, WIDTH), BF16),
            jax.ShapeDtypeStruct((SECTIONS + 1, 16, WIDTH), F32),
            jax.ShapeDtypeStruct((SLOTS, LEN, 256), BF16),
        ],
        in_specs=[any_space] * 12,
        out_specs=[any_space, any_space, any_space],
        scratch_shapes=[
            pltpu.SMEM((SLOTS,), jnp.int32),
            pltpu.SMEM((1,), jnp.int32),
            pltpu.SMEM((8,), F32),
            pltpu.VMEM((1, 2, WIDTH), F32),
            pltpu.VMEM((1, 2, WIDTH), F32),
            pltpu.VMEM((2, 2, WIDTH), F32),
            pltpu.VMEM((2, FF), F32),
            pltpu.VMEM((1, WIDTH), F32),
            pltpu.VMEM((WIDTH, FF), BF16),
            pltpu.VMEM((2 * FF, WIDTH), BF16),
            pltpu.VMEM((WIDTH, FF), BF16),
            pltpu.VMEM((10, SLOTS, LEN, WIDTH), BF16),
            pltpu.VMEM((10, SLOTS, LEN, WIDTH), BF16),
            pltpu.VMEM((SLOTS, LEN, WIDTH), BF16),
            pltpu.VMEM((SLOTS, LEN, 3), F32),
            pltpu.VMEM((SLOTS, LEN, WIDTH), BF16),
            pltpu.VMEM((SLOTS, LEN, WIDTH), BF16),
            pltpu.VMEM((SLOTS, LEN, WIDTH), BF16),
            pltpu.VMEM((SLOTS, LEN, WIDTH), BF16),
            pltpu.VMEM((LEN, WIDTH), F32),
            pltpu.VMEM((16, WIDTH), F32),
            pltpu.VMEM((16, WIDTH), F32),
            pltpu.VMEM((2, 2, 16, WIDTH), BF16),
            pltpu.VMEM((3, 16, WIDTH), F32),
            pltpu.VMEM((3, 16, WIDTH), F32),
            pltpu.VMEM((16, WIDTH), F32),
            pltpu.VMEM((3, 16, WIDTH), F32),
            dma((12,)), dma, dma((2,)), dma, dma((4, 2)),
            dma((SLOTS,)), dma((SLOTS,)), dma((SLOTS,)), dma((SLOTS,)),
            dma((SLOTS, 4)), dma((SLOTS,)), pltpu.SemaphoreType.REGULAR, pltpu.SemaphoreType.REGULAR,
            dma, dma((2,)), pltpu.SemaphoreType.REGULAR,
            dma((2,)), dma((8, CHUNKS)), dma, dma((2, 2)), dma, dma, dma((CHUNKS,)), dma, dma,
            dma((12,)), dma((12,)),
        ],
        compiler_params=pltpu.CompilerParams(
            collective_id=0, has_side_effects=True, vmem_limit_bytes=63 * 2**20
        ),
    )(block, cot, group_ids, live_count, group_scale, gains, shifts, qv_bias, up_bias, out_bias, w1, down)


def widen_kernel(
    reduced, sums_hbm, grad_in,
    first_out, down_out, qv_out, up_out, bias_out, gain_out, shift_out, grad_out,
    narrow, wide, sums, qv, up, bias, gain, shift, in_sem, out_sem, small_sem,
):
    rows, depth = wide.shape[1], wide.shape[0]
    count = 6 * 1024 // rows

    def load(i):
        return pltpu.make_async_copy(reduced.at[pl.ds(i * rows, rows)], narrow.at[i % depth], in_sem.at[i % depth])

    def store(i):
        chunk, cut = i * rows // 1024, pl.ds(i * rows % 1024, rows)
        if chunk < 2:
            target = down_out.at[pl.ds(i * rows, rows)]
        else:
            target = first_out.at[0, cut, pl.ds((chunk - 2) * 1024, 1024)]
        return pltpu.make_async_copy(wide.at[i % depth], target, out_sem.at[i % depth])

    for i in range(depth):
        load(i).start()
    load_sums = pltpu.make_async_copy(sums_hbm, sums, small_sem.at[0])
    load_sums.start()
    move_grad = pltpu.make_async_copy(grad_in, grad_out, small_sem.at[1])
    move_grad.start()
    small = [(qv, qv_out), (up, up_out), (bias, bias_out), (gain, gain_out), (shift, shift_out)]
    small = [pltpu.make_async_copy(*piece, small_sem.at[2 + j]) for j, piece in enumerate(small)]
    for i in range(count):
        load(i).wait()
        if i >= depth:
            store(i - depth).wait()
        wide[i % depth] = narrow[i % depth].astype(F32)
        store(i).start()
        if i + depth < count:
            load(i + depth).start()
        if i == 2:
            load_sums.wait()
            for layer in (0, 1):
                qv[layer, 0:1, :] = sums[2 * layer, 5:6, :]
                qv[layer, 1:2, :] = sums[2 * layer, 7:8, :]
                for j in range(4):
                    up[layer : layer + 1, j * WIDTH : (j + 1) * WIDTH] = sums[2 * layer + 1, 5 + j : 6 + j, :]
            bias[...] = sums[SECTIONS, 4:5, :]
            gain[0] = sums[SECTIONS, 0:2, :]
            shift[0] = sums[SECTIONS, 2:4, :]
            for copy in small:
                copy.start()
    for i in range(count - depth, count):
        store(i).wait()
    for copy in small:
        copy.wait()
    move_grad.wait()


def widen(reduced, sums, grad):
    any_space = pl.BlockSpec(memory_space=pl.ANY)
    rows, depth = 1024, 3
    dma = pltpu.SemaphoreType.DMA
    shapes = [(2, 2, WIDTH), (2, FF), (1, WIDTH), (1, 2, WIDTH), (1, 2, WIDTH)]
    return pl.pallas_call(
        widen_kernel,
        name="widen",
        out_shape=[
            jax.ShapeDtypeStruct((1, WIDTH, FF), F32),
            jax.ShapeDtypeStruct((2 * WIDTH, WIDTH), F32),
            *[jax.ShapeDtypeStruct(shape, F32) for shape in shapes],
            jax.ShapeDtypeStruct((SLOTS, LEN, 256), BF16),
        ],
        in_specs=[any_space] * 3,
        out_specs=[any_space] * 8,
        scratch_shapes=[
            pltpu.VMEM((depth, rows, WIDTH), BF16),
            pltpu.VMEM((depth, rows, WIDTH), F32),
            pltpu.VMEM((SECTIONS + 1, 16, WIDTH), F32),
            *[pltpu.VMEM(shape, F32) for shape in shapes],
            dma((depth,)), dma((depth,)), dma((7,)),
        ],
        compiler_params=pltpu.CompilerParams(vmem_limit_bytes=63 * 2**20),
    )(reduced, sums, grad)


def on_device(
    block_input, cotangent, group_ids, live_count, group_scale, norm_gain, norm_bias, first_weight,
    qv_bias, up_bias, down_weight, out_bias,
):
    reduced, sums, grad = mega(
        block_input, cotangent, group_ids, live_count, group_scale, norm_gain, norm_bias,
        qv_bias, up_bias, out_bias, first_weight, down_weight,
    )
    first_grad, down_grad, qv_grad, up_grad, bias_grad, gain_grad, shift_grad, input_grad = widen(reduced, sums, grad)
    return input_grad, first_grad, down_grad, qv_grad, up_grad, bias_grad, gain_grad, shift_grad


def solution(mesh):
    in_specs = (
        P("dp", None, None),
        P("dp", None, None),
        P("dp"),
        P("dp"),
        P(),
        P("section", None, None),
        P("section", None, None),
        P("section", None, None),
        P(),
        P(),
        P("section", None),
        P("section", None),
    )
    out_specs = (
        P("dp", None, "section"),
        P("section", None, None),
        P("section", None),
        P(),
        P(),
        P("section", None),
        P("section", None, None),
        P("section", None, None),
    )
    return jax.shard_map(on_device, mesh=mesh, in_specs=in_specs, out_specs=out_specs, check_vma=False)
```
